32 devices in a mesh: seq: 8 (over z, x), mp: 4 (over y, core).
Axes of the slice: x: 2, y: 2, z: 4, core: 2. Of those that a mesh axis runs over, the one named last changes fastest.
Arguments:
- block_input: bfloat16 [2, 1024, 2048], P(None, 'seq'), may hold values from -6 to 6
- segment_ids: int32 [2, 1024], replicated, may hold values from 0 to 2, as said below
- gain_mix: float32 [2048], replicated, may hold values from 0.5 to 1.5
- w_rec: bfloat16 [2048, 2560], P(None, 'mp'), may hold values from -0.125 to 0.125
- w_gel: bfloat16 [2048, 2560], P(None, 'mp'), may hold values from -0.125 to 0.125
- conv_weight: float32 [4, 2560], P(None, 'mp'), may hold values from -3 to 3
- conv_bias: float32 [2560], P('mp'), may hold values from -2 to 2
- gate_a: bfloat16 [256, 2560], P(None, 'mp'), may hold values from -0.375 to 0.375
- gate_x: bfloat16 [256, 2560], P(None, 'mp'), may hold values from -0.375 to 0.375
- bias_a: float32 [2560], P('mp'), may hold values from -3 to 3
- bias_x: float32 [2560], P('mp'), may hold values from -3 to 3
- log_rate: float32 [2560], P('mp'), may hold values from -16 to -4
- w_out: bfloat16 [2560, 2048], P('mp'), may hold values from -0.3125 to 0.3125
- gain_ffn: float32 [2048], replicated, may hold values from 0.5 to 1.5
- w_gate: bfloat16 [2048, 6144], P(None, 'mp'), may hold values from -0.125 to 0.125
- w_up: bfloat16 [2048, 6144], P(None, 'mp'), may hold values from -0.125 to 0.125
- w_down: bfloat16 [6144, 2048], P('mp'), may hold values from -0.15625 to 0.15625
- cotangent: bfloat16 [2, 1024, 2048], P(None, 'seq'), may hold values from -6 to 6
Outputs:
- block_output: float32 [2, 1024, 2048], P(None, 'seq')
- grad_input: float32 [2, 1024, 2048], P(None, 'seq')
- grad_gain_mix: float32 [2048], P('seq')
- grad_w_rec: float32 [2048, 2560], P('seq', 'mp')
- grad_w_gel: float32 [2048, 2560], P('seq', 'mp')
- grad_conv_weight: float32 [4, 2560], P(None, ('mp', 'seq'))
- grad_conv_bias: float32 [2560], P(('mp', 'seq'))
- grad_gate_a: float32 [256, 2560], P('seq', 'mp')
- grad_gate_x: float32 [256, 2560], P('seq', 'mp')
- grad_bias_a: float32 [2560], P(('mp', 'seq'))
- grad_bias_x: float32 [2560], P(('mp', 'seq'))
- grad_log_rate: float32 [2560], P(('mp', 'seq'))
- grad_w_out: float32 [2560, 2048], P('mp', 'seq')
- grad_gain_ffn: float32 [2048], P('seq')
- grad_w_gate: float32 [2048, 6144], P('seq', 'mp')
- grad_w_up: float32 [2048, 6144], P('seq', 'mp')
- grad_w_down: float32 [6144, 2048], P('mp', 'seq')
The draws below stay inside these ranges and needn't reach their ends.
Inputs may be any that keep to these rules, and one draw needn't show every extreme that they name: `segment_ids`: in each row the ids start at 0, never fall, and rise by one where a new document starts. One row, drawn from the seed, is a single document; every other row holds three documents, the first ending before position 512 and the third starting at or after it.
All inputs are finite; a program needn't handle non-finite values.
Results may differ from the reference program's by a relative error of at most 0.013.
Values may be sent and summed in bfloat16 or wider, within the bound.
A program may use at most 256 MiB of HBM per device.

```python
import jax
import jax.numpy as jnp
from jax import lax

D = 2048
HEADS = 10
HEAD = 256
LRU = 2560
FF = 6144
KERNEL = 4
SEQS = 2
GROUP = 128
LENGTH = 1024
TOKENS = 2048


def draw_segment_ids(key, part):
    key = jax.random.fold_in(key, 7)
    key_row, key_first, key_second = jax.random.split(key, 3)
    whole_row = jax.random.randint(key_row, (), 0, SEQS)
    first_cut = jax.random.randint(key_first, (SEQS, 1), 1, LENGTH // 2)
    second_cut = jax.random.randint(key_second, (SEQS, 1), LENGTH // 2, LENGTH)
    position = jnp.arange(LENGTH, dtype=jnp.int32)[None, :]
    documents = (position >= first_cut).astype(jnp.int32) + (position >= second_cut).astype(jnp.int32)
    row_index = jnp.arange(SEQS, dtype=jnp.int32)[:, None]
    return jnp.where(row_index == whole_row, jnp.zeros_like(documents), documents)


def levels(own_key, dims, shards, smallest, largest):
    level, own = 1.0, jax.random.fold_in(own_key, 6)
    for dim, blocks in shards:
        heights = jnp.exp(jax.random.uniform(jax.random.fold_in(own, dim), (blocks,), jnp.float32, smallest / len(shards), largest / len(shards)))
        level = level * jnp.repeat(heights, dims[dim] // blocks).reshape([-1 if axis == dim else 1 for axis in range(len(dims))])
    return level


def scatter_about(key, extent, width, limit, shards=(), held_as=jnp.bfloat16):
    values = jax.random.normal(key, extent, jnp.float32) * width
    if len(shards) > 0:
        values = levels(key, extent, shards, -0.22, 0.18) * values
    return jnp.clip(values, min=-limit, max=limit).astype(held_as)


def setup_inputs(seed: int = 0) -> dict:
    key_list = jax.random.split(jax.random.key(seed), 19)
    return {
        "block_input": scatter_about(key_list[0], (SEQS, LENGTH, D), 1.0, 6.0, ((1, 8),)),
        "segment_ids": draw_segment_ids(jax.random.fold_in(key_list[18], 71), 0),
        "gain_mix": jnp.clip(1.0 + 0.1 * jax.random.normal(key_list[2], (D,), jnp.float32), 0.5, 1.5),
        "w_rec": scatter_about(key_list[3], (D, LRU), D ** -0.5, 0.125, ((1, 4),)),
        "w_gel": scatter_about(key_list[4], (D, LRU), D ** -0.5, 0.125, ((1, 4),)),
        "conv_weight": scatter_about(key_list[5], (KERNEL, LRU), 0.5, 3.0, ((1, 4),), jnp.float32),
        "conv_bias": scatter_about(key_list[6], (LRU,), 0.3, 2.0, ((0, 4),), jnp.float32),
        "gate_a": scatter_about(key_list[7], (HEAD, LRU), HEAD ** -0.5, 0.375, ((1, 4),)),
        "gate_x": scatter_about(key_list[8], (HEAD, LRU), HEAD ** -0.5, 0.375, ((1, 4),)),
        "bias_a": scatter_about(key_list[9], (LRU,), 0.5, 3.0, ((0, 4),), jnp.float32),
        "bias_x": scatter_about(key_list[10], (LRU,), 0.5, 3.0, ((0, 4),), jnp.float32),
        "log_rate": jnp.clip(-16.0 + 12.0 * jax.random.uniform(key_list[11], (LRU,), jnp.float32) ** levels(key_list[11], (LRU,), ((0, 4),), -0.2, 0.2), -16.0, -4.0),
        "w_out": scatter_about(key_list[12], (LRU, D), (LRU // 8) ** -0.5, 0.3125, ((0, 4),)),
        "gain_ffn": jnp.clip(1.0 + 0.1 * jax.random.normal(key_list[13], (D,), jnp.float32), 0.5, 1.5),
        "w_gate": scatter_about(key_list[14], (D, FF), D ** -0.5, 0.125, ((1, 4),)),
        "w_up": scatter_about(key_list[15], (D, FF), D ** -0.5, 0.125, ((1, 4),)),
        "w_down": scatter_about(key_list[16], (FF, D), (FF // 4) ** -0.5, 0.15625, ((0, 4),)),
        "cotangent": scatter_about(key_list[17], (SEQS, LENGTH, D), 1.0, 6.0, ((1, 8),)),
    }


EPS = 1e-06
RATE_SCALE = 8.0

@jax.custom_vjp
def low(v):
    return lax.optimization_barrier(v.astype(jnp.bfloat16)).astype(jnp.float32)

@jax.custom_vjp
def low_back(v):
    return v

def low_keep(v):
    return (low(v), None)

def low_pass(kept, grad):
    return (grad,)

def back_keep(v):
    return (v, None)

def back_low(kept, grad):
    return (low(grad),)
low.defvjp(low_keep, low_pass)
low_back.defvjp(back_keep, back_low)

def matmul(left, right):
    return jnp.dot(left, right, precision=lax.Precision.HIGHEST)

def row_norm(values, gain):
    scale = lax.rsqrt(lax.optimization_barrier(jnp.mean(values * values, axis=-1, keepdims=True)) + EPS)
    return values * scale * gain

def gelu_tanh(values):
    return jax.nn.gelu(values, approximate=True)

def linear_scan(coeff, drive):
    blocks = LENGTH // GROUP

    def time_major(values):
        return values.reshape(SEQS, LENGTH, LRU).transpose(1, 0, 2).reshape(blocks, GROUP, SEQS, LRU)

    def one_block(state, pair):

        def one_step(inner, item):
            inner = item[0] * inner + item[1]
            return (inner, inner)
        return lax.scan(one_step, state, pair)
    final_state, states = lax.scan(jax.checkpoint(one_block), jnp.zeros((SEQS, LRU), jnp.float32), (time_major(coeff), time_major(drive)))
    return states.reshape(LENGTH, SEQS, LRU).transpose(1, 0, 2).reshape(TOKENS, LRU)

def head_product(conv_out, gate, offset):
    rolled = jnp.roll(conv_out, offset, axis=1).reshape(TOKENS, HEADS, HEAD)
    table = jnp.roll(gate, offset, axis=1).reshape(HEAD, HEADS, HEAD)
    result = jnp.einsum('thi,ihj->thj', rolled, table, precision=lax.Precision.HIGHEST).reshape(TOKENS, LRU)
    return jnp.roll(result, -offset, axis=1)

def forward(block_x, gain_mix, w_rec, w_gel, conv_weight, conv_bias, gate_a, gate_x, bias_a, bias_x, log_rate, w_out, gain_ffn, w_gate, w_up, w_down, segment_ids):
    flat_x = block_x.reshape(TOKENS, D)
    normed_mix = low(row_norm(flat_x, gain_mix))
    pre_rec = low(low_back(matmul(normed_mix, w_rec))).reshape(SEQS, LENGTH, LRU)
    pre_gel = low_back(matmul(normed_mix, w_gel))
    gelu_gate = gelu_tanh(pre_gel)
    padded_ids = jnp.concatenate([jnp.full((SEQS, KERNEL - 1), -1, jnp.int32), segment_ids], axis=1)
    conv_acc = conv_bias + jnp.zeros((SEQS, LENGTH, LRU), jnp.float32)
    for offset in range(KERNEL):
        same = (padded_ids[:, KERNEL - 1 - offset:KERNEL - 1 - offset + LENGTH] == segment_ids).astype(jnp.float32)
        shifted = jnp.concatenate([jnp.zeros((SEQS, offset, LRU), jnp.float32), pre_rec[:, :LENGTH - offset]], axis=1)
        conv_acc = conv_acc + conv_weight[offset] * (same[:, :, None] * shifted)
    conv_out = low(conv_acc).reshape(TOKENS, LRU)
    head_offset = HEAD // 4
    pre_a = low_back(head_product(conv_out, gate_a, head_offset) + bias_a)
    pre_x = low_back(head_product(conv_out, gate_x, head_offset) + bias_x)
    recur = jax.nn.sigmoid(pre_a)
    inject = jax.nn.sigmoid(pre_x)
    log_decay = -RATE_SCALE * jax.nn.softplus(log_rate) * recur
    decay = jnp.exp(log_decay)
    spread = jnp.sqrt(-jnp.expm1(2.0 * log_decay))
    keep_mask = jnp.concatenate([jnp.zeros((SEQS, 1), jnp.float32), (segment_ids[:, 1:] == segment_ids[:, :-1]).astype(jnp.float32)], axis=1).reshape(TOKENS)
    drive = spread * inject * conv_out
    coeff = decay * keep_mask[:, None]
    state = linear_scan(coeff, drive)
    mixed = low(state * gelu_gate)
    branch = low_back(matmul(mixed, w_out))
    resid = flat_x + branch
    normed_ffn = low(row_norm(resid, gain_ffn))
    pre_gate = low_back(matmul(normed_ffn, w_gate))
    pre_up = low_back(matmul(normed_ffn, w_up))
    hidden = low(gelu_tanh(pre_gate) * pre_up)
    ffn_out = low_back(matmul(hidden, w_down))
    return (resid + ffn_out).reshape(SEQS, LENGTH, D)

def reference(block_input, segment_ids, gain_mix, w_rec, w_gel, conv_weight, conv_bias, gate_a, gate_x, bias_a, bias_x, log_rate, w_out, gain_ffn, w_gate, w_up, w_down, cotangent):
    params = (block_input.astype(jnp.float32), gain_mix, w_rec.astype(jnp.float32), w_gel.astype(jnp.float32), conv_weight, conv_bias, gate_a.astype(jnp.float32), gate_x.astype(jnp.float32), bias_a, bias_x, log_rate, w_out.astype(jnp.float32), gain_ffn, w_gate.astype(jnp.float32), w_up.astype(jnp.float32), w_down.astype(jnp.float32))

    def closed(*values):
        return forward(*values, segment_ids)
    block_output, back_fn = jax.vjp(closed, *params)
    grads = back_fn(cotangent.astype(jnp.float32))
    return (block_output, grads[0], grads[1], grads[2], grads[3], grads[4], grads[5], grads[6], grads[7], grads[8], grads[9], grads[10], grads[11], grads[12], grads[13], grads[14], grads[15])
```

```python
import functools
import types

import jax
import jax.numpy as jnp
from jax import lax
from jax.experimental import pallas as pl
from jax.experimental.pallas import tpu as pltpu
from jax.sharding import PartitionSpec as P

EPS = 1e-06
RATE_SCALE = 8.0
Z_CHIPS = 4
CORES = 2
GELU_C = 0.7978845608028654
GELU_A = 0.044715
MESH = pl.DeviceIdType.MESH
F32 = jnp.float32
BF16 = jnp.bfloat16


def dot(left, right):
    return jnp.dot(left, right, preferred_element_type=F32)


def dot_nt(left, right):
    return lax.dot_general(left, right, (((1,), (1,)), ((), ())), preferred_element_type=F32)


def remote(src, dst, send_sem, recv_sem, device):
    return pltpu.make_async_remote_copy(
        src_ref=src,
        dst_ref=dst,
        send_sem=send_sem,
        recv_sem=recv_sem,
        device_id=device,
        device_id_type=MESH,
    )


def loop(count, body):
    def step(i, carry):
        body(i)
        return carry

    lax.fori_loop(0, count, step, 0)


def rows16(i, offset=0):
    return pl.ds(pl.multiple_of(i * 16 + offset, 16), 16)


def gelu_tanh(v):
    t = jnp.tanh(GELU_C * (v + GELU_A * (v * v * v)))
    return 0.5 * v * (1.0 + t)


def gelu_and_slope(v):
    square = v * v
    t = jnp.tanh(GELU_C * (v + GELU_A * (square * v)))
    half = 0.5 * (1.0 + t)
    slope = half + 0.5 * v * (1.0 - t * t) * (GELU_C * (1.0 + 3.0 * GELU_A * square))
    return v * half, slope


def minus_expm1(v):
    acc = 1.0 + v * (1.0 / 8.0)
    for n in (7.0, 6.0, 5.0, 4.0, 3.0, 2.0):
        acc = 1.0 + v * (1.0 / n) * acc
    return -v * acc


def softplus_small(v):
    u = jnp.exp(v)
    acc = 1.0 / 6.0 - u * (1.0 / 7.0)
    for n in (5.0, 4.0, 3.0, 2.0):
        acc = 1.0 / n - u * acc
    return u * (1.0 - u * acc)


def scan_tile(decay, value, reverse):
    row = lax.broadcasted_iota(jnp.int32, decay.shape, 0)
    for k in (1, 2, 4):
        shift = 8 - k if reverse else k
        valid = row < 8 - k if reverse else row >= k
        decay_k = pltpu.roll(decay, shift, 0)
        value_k = pltpu.roll(value, shift, 0)
        value = jnp.where(valid, decay * value_k + value, value)
        decay = jnp.where(valid, decay * decay_k, decay)
    return decay, value


def fold8(v):
    return v[0:8] + v[8:16]


def layout(dims):
    d = dims
    T, D, L, LP, F, FB, DC = d.T, d.D, d.L, d.LP, d.F, d.FB, d.DC
    B, G, HW = d.B, d.G, d.HW
    outs = dict(
        o_block=((T, D), F32),
        o_gin=((T, D), F32),
        o_wrec=((DC, L), F32),
        o_wgel=((DC, L), F32),
        o_wgate=((DC, F), F32),
        o_wup=((DC, F), F32),
        o_wdown=((F, DC), F32),
        o_wout=((L, DC), F32),
        o_small=((8, L), F32),
        o_gain=((8, DC), F32),
        o_gates=((2, d.GR, L), F32),
        hz_d=((3, d.nz, T, FB), BF16),
        hz_r=((2, d.nz, T, LP), BF16),
        land_f=((6, 2 * (d.nz - 1), DC, FB), BF16),
        land_o=((2 * (d.nz - 1), DC, LP), BF16),
    )
    scratch = dict(
        x_v=((T, D), BF16),
        cot_v=((T, D), BF16),
        xh=((B * 16, D), BF16),
        scm=((T, 128), F32),
        scf=((T, 128), F32),
        idp=((8, 2 * G), jnp.int32),
        mk=((B, G + 8, 128), F32),
        rv=((8, L), F32),
        wl=((2, HW, L), BF16),
        wo=((2, LP, L), BF16),
        wr=((2, HW, L), BF16),
        extp=((B, 16 + G, L), F32),
        cv=((T, LP), BF16),
        st_l=((T, HW), BF16),
        st_r=((T, HW), BF16),
        hl=((T, HW), BF16),
        hr=((T, HW), BF16),
        pre_gel=((T, L), F32),
        recur=((T, L), F32),
        inj=((T, L), F32),
        cfp=((B, G + 8, L), F32),
        aloc=((T, L), F32),
        stp=((B, 8 + G, L), F32),
        pk=((2, 8, L), F32),
        pf=((2, d.nseq, 8, L), F32),
        resid=((T, D), F32),
        csend=((d.nb, T, d.CB), F32),
        cland=((d.nb, T, d.CB), F32),
        tot=((2 * d.nb, T, d.CB), F32),
        yl=((2, d.ny, d.nb, T, d.CB), BF16),
        fo=((2 * d.nb, T, d.CB), BF16),
        hd=((3, T, FB), BF16),
        gp=((6, d.nx, T, FB), BF16),
        mx=((d.nx, T, LP), BF16),
        gpg=((T, LP), BF16),
        gpr=((T, LP), BF16),
        nmT=((d.nseq, DC, T), BF16),
        cotT=((d.nseq, DC, T), BF16),
        nfT=((d.nseq, DC, T), BF16),
        gbT=((d.nseq, DC, T), BF16),
        ez=((2, d.nz, d.nx, DC, T), BF16),
        ex=((2, d.nx, d.nz, DC, T), BF16),
        xr_d=((3, d.nx - 1, DC, FB), BF16),
        xr_r=((2, d.nx - 1, DC, LP), BF16),
        gacc=((16, D), F32),
        gsend=((d.nseq, 8, DC), F32),
        gland=((d.nseq, 8, DC), F32),
        sacc=((8, 8, L), F32),
        smv=((8, L), F32),
        smland=((d.nseq, 8, L), F32),
        gt=((2, HW, L), BF16),
        gtland=((d.nseq, 2, d.GR, L), BF16),
        gs_l=((T, HW), BF16),
        gs_r=((T, HW), BF16),
        gi_l=((T, HW), BF16),
        gi_r=((T, HW), BF16),
        sp_s=((B * 8, L), F32),
        sp_r=((B * 8, L), F32),
    )
    sems = dict(
        ld=(16,),
        halo_s=(B,),
        halo_r=(B,),
        ex_s=(2,),
        ex_r=(2,),
        gi_s=(2,),
        gi_rs=(2,),
        pf_s=(2, d.nseq),
        pf_r=(2, d.nseq),
        c_s=(4, d.nb),
        c_r=(4, d.nb),
        y_s=(4, d.ny, d.nb),
        y_r=(4, d.ny, d.nb),
        a_s=(4, d.nb),
        a_r=(4, d.nb),
        ez_s=(2, d.nz),
        ez_r=(2, d.nz),
        exz_s=(2, d.nx, d.nz),
        exz_r=(2, d.nx, d.nz),
        hz_s=(5, d.nz, 2),
        hz_rs=(5, d.nz),
        hx_s=(7, d.nx),
        hx_r=(7, d.nx),
        xr_s=(5, d.nx),
        xr_rs=(5, d.nx),
        p_s=(7, d.nz),
        p_r=(7, 2 * (d.nz - 1)),
        sm_s=(d.nseq,),
        sm_r=(d.nseq,),
        ga_s=(d.nseq,),
        ga_r=(d.nseq,),
        gt_s=(d.nseq,),
        gt_r=(d.nseq,),
        sp_ss=(1,),
        sp_rs=(1,),
        pl_s=(2,),
        ow=(16,),
    )
    return outs, scratch, sems


def body(d, r):
    T, D, L, LP, F, FB, DC = d.T, d.D, d.L, d.LP, d.F, d.FB, d.DC
    B, G, HW, CB, nb = d.B, d.G, d.HW, d.CB, d.nb
    nseq, nz, nx, ny, nm = d.nseq, d.nz, d.nx, d.ny, d.nm
    s, m = lax.axis_index("seq"), lax.axis_index("mp")
    z, x = lax.div(s, nx), lax.rem(s, nx)
    y, c = lax.div(m, CORES), lax.rem(m, CORES)
    partner = (s, y * CORES + 1 - c)
    left_m, right_m = lax.rem(m + nm - 1, nm), lax.rem(m + 1, nm)
    pending = []

    def later(make, when=None):
        pending.append((make, when))

    def start(make, when=None):
        if when is None:
            make().start()
        else:
            pl.when(when())(lambda: make().start())
        pending.append((make, when))

    barrier = pltpu.get_barrier_semaphore()
    for k in range(1, nseq):
        pl.semaphore_signal(
            barrier, inc=1, device_id=(lax.rem(s + k, nseq), m), device_id_type=MESH
        )
    for k in range(1, nm):
        pl.semaphore_signal(barrier, inc=1, device_id=(s, lax.rem(m + k, nm)), device_id_type=MESH)

    def local(src, dst, i):
        copy = pltpu.make_async_copy(src, dst, r.ld.at[i])
        copy.start()
        return copy

    ld_x = local(r.x_in, r.x_v, 0)

    half = nb * CB

    def psum_start(k, part):
        par = k % 2

        def send_half(j):
            r.csend[j] = part((1 - c) * half + j * CB)
            remote(r.csend.at[j], r.cland.at[j], r.c_s.at[k, j], r.c_r.at[k, j], partner).start()

        loop(nb, send_half)

        def own_half(j):
            v = part(c * half + j * CB)
            remote(
                r.csend.at[j], r.cland.at[j], r.c_s.at[k, j], r.c_r.at[k, j], partner
            ).wait_recv()
            r.yl[par, y, j] = (v + r.cland[j]).astype(BF16)
            for q in range(1, ny):
                to = lax.rem(y + q, ny)
                remote(
                    r.yl.at[par, y, j],
                    r.yl.at[par, y, j],
                    r.y_s.at[k, q, j],
                    r.y_r.at[k, q, j],
                    (s, to * CORES + c),
                ).start()

        loop(nb, own_half)

    def psum_finish(k):
        par = k % 2

        def total(j):
            for q in range(1, ny):
                src = lax.rem(y + ny - q, ny)
                remote(
                    r.yl.at[par, src, j],
                    r.yl.at[par, src, j],
                    r.y_s.at[k, q, j],
                    r.y_r.at[k, q, j],
                    partner,
                ).wait_recv()
            v = r.yl[par, 0, j].astype(F32)
            for q in range(1, ny):
                v = v + r.yl[par, q, j].astype(F32)
            at = c * nb + j
            r.tot[at] = v
            remote(r.tot.at[at], r.tot.at[at], r.a_s.at[k, j], r.a_r.at[k, j], partner).start()

        loop(nb, total)

        def close(j):
            at = (1 - c) * nb + j
            remote(
                r.tot.at[at], r.tot.at[at], r.a_s.at[k, j], r.a_r.at[k, j], partner
            ).wait()
            remote(
                r.csend.at[j], r.cland.at[j], r.c_s.at[k, j], r.c_r.at[k, j], partner
            ).wait_send()
            for q in range(1, ny):
                remote(
                    r.yl.at[par, y, j],
                    r.yl.at[par, y, j],
                    r.y_s.at[k, q, j],
                    r.y_r.at[k, q, j],
                    partner,
                ).wait_send()

        loop(nb, close)

    def pairs_send(k):
        for q in range(1, nseq):
            start(
                lambda q=q: remote(
                    r.pk.at[k],
                    r.pf.at[k, s],
                    r.pf_s.at[k, q],
                    r.pf_r.at[k, q],
                    (lax.rem(s + q, nseq), m),
                )
            )

    def pairs_enter(k, reverse):
        for q in range(1, nseq):
            src = lax.rem(s + nseq - q, nseq)
            remote(
                r.pk.at[k], r.pf.at[k, src], r.pf_s.at[k, q], r.pf_r.at[k, q], partner
            ).wait_recv()
        r.pf[k, s] = r.pk[k]
        value = jnp.zeros((B, L), F32)
        for q in range(nseq - 1):
            at = nseq - 1 - q if reverse else q
            pair = r.pf[k, at]
            new = pair[0:B] * value + pair[B : 2 * B]
            value = jnp.where(at > s if reverse else at < s, new, value)
        return value

    def transposed(src, dst):
        def one(j):
            dst[j] = src[:, pl.ds(pl.multiple_of(j * DC, DC), DC)].T

        loop(nseq, one)

    def ez_send(e, src):
        def copy(k):
            to = lax.rem(z + k, nz)
            return remote(
                src.at[pl.ds(to * nx, nx)],
                r.ez.at[e, z],
                r.ez_s.at[e, k],
                r.ez_r.at[e, k],
                (to * nx + x, m),
            )

        for k in range(1, nz):
            start(functools.partial(copy, k))

    def ez_wait(e):
        for k in range(1, nz):
            src = lax.rem(z + nz - k, nz)
            remote(
                r.ez.at[e, src], r.ez.at[e, src], r.ez_s.at[e, k], r.ez_r.at[e, k], partner
            ).wait_recv()

    def ex_send(e, src):
        def copy(k, zc):
            to = lax.rem(x + k, nx)
            return remote(
                src.at[zc * nx + to],
                r.ex.at[e, x, zc],
                r.exz_s.at[e, k, zc],
                r.exz_r.at[e, k, zc],
                (z * nx + to, m),
            )

        for k in range(1, nx):
            for zc in range(nz):
                start(functools.partial(copy, k, zc))

    def ex_wait(e):
        for k in range(1, nx):
            src = lax.rem(x + nx - k, nx)
            for zc in range(nz):
                remote(
                    r.ex.at[e, src, zc],
                    r.ex.at[e, src, zc],
                    r.exz_s.at[e, k, zc],
                    r.exz_r.at[e, k, zc],
                    partner,
                ).wait_recv()

    def q_own(qb):
        return r.hd.at[qb] if qb < 3 else (r.gpg if qb == 3 else r.gpr)

    def q_land(qb, zo):
        return r.hz_d.at[qb, zo] if qb < 3 else r.hz_r.at[qb - 3, zo]

    def q_copy(qb, src, zo, way):
        to = s + nx if way == 0 else s - nx
        return remote(src, q_land(qb, zo), r.hz_s.at[qb, zo, way], r.hz_rs.at[qb, zo], (to, m))

    def q_send(qb):
        start(lambda: q_copy(qb, q_own(qb), z, 0), lambda: z < nz - 1)
        start(lambda: q_copy(qb, q_own(qb), z, 1), lambda: z > 0)

    def q_forward(qb, dist):
        @pl.when(z - dist >= 0)
        def _():
            zo = z - dist
            q_copy(qb, q_land(qb, zo), zo, 0).wait_recv()

            @pl.when(z < nz - 1)
            def _():
                q_copy(qb, q_land(qb, zo), zo, 0).start()

        @pl.when(z + dist <= nz - 1)
        def _():
            zo = z + dist
            q_copy(qb, q_land(qb, zo), zo, 1).wait_recv()

            @pl.when(z > 0)
            def _():
                q_copy(qb, q_land(qb, zo), zo, 1).start()

        if dist < nz - 1:
            later(
                lambda: q_copy(qb, q_land(qb, z - dist), z - dist, 0),
                lambda: (z - dist >= 0) & (z < nz - 1),
            )
            later(
                lambda: q_copy(qb, q_land(qb, z + dist), z + dist, 1),
                lambda: (z + dist <= nz - 1) & (z > 0),
            )

    def hx_ref(pb):
        return r.gp.at[pb] if pb < 6 else r.mx

    def hx_send(pb):
        def copy(k):
            to = lax.rem(x + k, nx)
            return remote(
                hx_ref(pb).at[x],
                hx_ref(pb).at[x],
                r.hx_s.at[pb, k],
                r.hx_r.at[pb, k],
                (z * nx + to, m),
            )

        for k in range(1, nx):
            start(functools.partial(copy, k))

    def hx_wait(pb):
        for k in range(1, nx):
            src = lax.rem(x + nx - k, nx)
            remote(
                hx_ref(pb).at[src],
                hx_ref(pb).at[src],
                r.hx_s.at[pb, k],
                r.hx_r.at[pb, k],
                partner,
            ).wait_recv()

    own_ids = r.ids[:, pl.ds(pl.multiple_of(s * G, G), G)]
    before = r.ids[:, pl.ds(pl.multiple_of(jnp.maximum(s - 1, 0) * G, G), G)]
    r.idp[...] = jnp.zeros((8, 2 * G), jnp.int32)
    r.idp[0:B, 0:G] = jnp.where(s > 0, before, -1)
    r.idp[0:B, G : 2 * G] = own_ids
    both = r.idp[...]
    square_row = lax.broadcasted_iota(jnp.int32, (G, G), 0)
    same = [
        jnp.where(pltpu.roll(both, k, 1)[:, G:] == both[:, G:], 1.0, 0.0) for k in range(1, d.taps)
    ]
    for b in range(B):
        square = jnp.zeros((G, G), F32)
        for k in range(1, d.taps):
            square = jnp.where(
                square_row == k, jnp.broadcast_to(same[k - 1][b : b + 1], (G, G)), square
            )
        r.mk[b, 0:G, :] = square.T
        r.mk[b, G : G + 8, :] = jnp.zeros((8, 128), F32)
    rates = r.vecs[7:8]
    r.rv[0:1] = -RATE_SCALE * softplus_small(rates)
    r.rv[1:2] = -RATE_SCALE * jax.nn.sigmoid(rates)
    r.sacc[...] = jnp.zeros((8, 8, L), F32)

    pl.semaphore_wait(barrier, nseq - 1 + nm - 1)

    for b in range(B):
        start(
            lambda b=b: remote(
                r.x_in.at[pl.ds(b * G + G - 16, 16)],
                r.xh.at[pl.ds(b * 16, 16)],
                r.halo_s.at[b],
                r.halo_r.at[b],
                (s + 1, m),
            ),
            lambda: s < nseq - 1,
        )

    base = L * m + HW // 4
    shift = HW.bit_length() - 1
    turn = lax.rem(base, HW)
    turn_right = lax.rem(base + L, HW)

    def head_mask(first, count):
        row = lax.broadcasted_iota(jnp.int32, (count, L), 0) + first
        col = lax.broadcasted_iota(jnp.int32, (count, L), 1) + base
        return lax.shift_right_arithmetic(row, shift) == lax.shift_right_arithmetic(col, shift)

    pieces = [(p, min(HW, LP - p)) for p in range(0, LP, HW)]

    def recurrent_forward(wrec_v, wgel_v, wout_v, nm_v, nmh, pa, px, g2):
        ld_gel = local(r.w_gel, wgel_v, 1)
        ld_rec = local(r.w_rec, wrec_v, 2)
        ld_g = [
            local(gate, g2.at[i, pl.ds(at * HW, HW)], 3 + 2 * i + at)
            for i, gate in enumerate((r.gate_a, r.gate_x))
            for at in range(2)
        ]
        ld_out = local(r.w_out, wout_v, 7)
        ld_cot = local(r.cot, r.cot_v, 8)
        ld_x.wait()

        def norm(i):
            at = rows16(i)
            v = r.x_v[at, :].astype(F32)
            scale = lax.rsqrt(jnp.mean(v * v, axis=1, keepdims=True) + EPS)
            nm_v[at, :] = (v * scale * r.gains[0:1]).astype(BF16)
            r.scm[at, :] = jnp.broadcast_to(scale, (16, 128))

        loop(T // 16, norm)
        ld_gel.wait()
        r.pre_gel[...] = dot(nm_v[...], wgel_v[...])
        ld_rec.wait()
        main = dot(nm_v[...], wrec_v[...]).astype(BF16).astype(F32)
        for b in range(B):
            r.extp[b, 16 : 16 + G, :] = main[b * G : (b + 1) * G]

        @pl.when(s > 0)
        def _():
            for b in range(B):
                remote(
                    r.x_in.at[pl.ds(b * G + G - 16, 16)],
                    r.xh.at[pl.ds(b * 16, 16)],
                    r.halo_s.at[b],
                    r.halo_r.at[b],
                    partner,
                ).wait_recv()

        @pl.when(s == 0)
        def _():
            r.xh[...] = jnp.zeros((B * 16, D), BF16)

        for b in range(B):
            v = r.xh[b * 16 : (b + 1) * 16, :].astype(F32)
            scale = lax.rsqrt(jnp.mean(v * v, axis=1, keepdims=True) + EPS)
            nmh[b * 16 : (b + 1) * 16, :] = (v * scale * r.gains[0:1]).astype(BF16)
        rim = dot(nmh[...], wrec_v[...]).astype(BF16).astype(F32)
        for b in range(B):
            r.extp[b, 0:16, :] = rim[b * 16 : (b + 1) * 16]

        if LP > L:
            for wide in (r.cv, r.gpg, r.gpr, r.mx.at[x]):
                wide[:, L:] = jnp.zeros((T, LP - L), BF16)

        def conv(i):
            for b in range(B):
                window = r.extp[b, pl.ds(pl.multiple_of(i * 16 + 8, 8), 24), :]
                keep = r.mk[b, rows16(i), :]
                acc = r.vecs[4:5] + r.vecs[0:1] * window[8:24]
                for k in range(1, d.taps):
                    acc = acc + r.vecs[k : k + 1] * (keep[:, k : k + 1] * window[8 - k : 24 - k])
                at = rows16(i, b * G)
                r.cv[at, 0:L] = acc.astype(BF16)
                r.st_l[at, :] = acc[:, :HW].astype(BF16)
                r.st_r[at, :] = acc[:, L - HW :].astype(BF16)

        loop(G // 16, conv)
        def to_left():
            return remote(r.st_l, r.hr, r.ex_s.at[0], r.ex_r.at[0], (s, left_m))

        def to_right():
            return remote(r.st_r, r.hl, r.ex_s.at[1], r.ex_r.at[1], (s, right_m))

        start(to_left)
        start(to_right)

        for copy in ld_g:
            copy.wait()
        for i in range(2):
            table = g2[i, pl.ds(pl.multiple_of(turn, HW // 4), HW), :].astype(F32)
            table_right = g2[i, pl.ds(pl.multiple_of(turn_right, HW // 4), HW), :].astype(F32)
            r.wl[i] = jnp.where(head_mask(base - HW, HW), table, 0.0).astype(BF16)
            r.wr[i] = jnp.where(head_mask(base + L, HW), table_right, 0.0).astype(BF16)
            for p, n in pieces:
                r.wo[i, p : p + n, :] = jnp.where(head_mask(base + p, n), table[:n], 0.0).astype(
                    BF16
                )
        pa[...] = dot(r.cv[...], r.wo[0]) + r.vecs[5:6]
        px[...] = dot(r.cv[...], r.wo[1]) + r.vecs[6:7]
        to_left().wait_recv()
        to_right().wait_recv()
        pa[...] += dot(r.hl[...], r.wl[0]) + dot(r.hr[...], r.wr[0])
        px[...] += dot(r.hl[...], r.wl[1]) + dot(r.hr[...], r.wr[1])

        def scan(i, carry):
            out = []
            for b in range(B):
                decay_in, state_in = carry[2 * b], carry[2 * b + 1]
                at = rows16(i, b * G)
                recur = jax.nn.sigmoid(pa[at, :])
                inject = jax.nn.sigmoid(px[at, :])
                log_decay = r.rv[0:1] * recur
                decay = jnp.exp(log_decay)
                spread = jnp.sqrt(minus_expm1(2.0 * log_decay))
                drive = spread * inject * r.cv[at, 0:L].astype(F32)
                coeff = decay * r.mk[b, rows16(i), :][:, 1:2]
                r.recur[at, :] = recur
                r.inj[at, :] = inject
                r.cfp[b, rows16(i), :] = coeff
                for h in range(2):
                    a, v = scan_tile(
                        coeff[8 * h : 8 * h + 8], drive[8 * h : 8 * h + 8], reverse=False
                    )
                    v = v + a * state_in
                    a = a * decay_in
                    decay_in, state_in = a[7:8], v[7:8]
                    r.aloc[pl.ds(pl.multiple_of(b * G + i * 16 + 8 * h, 8), 8), :] = a
                    r.stp[b, pl.ds(pl.multiple_of(8 + i * 16 + 8 * h, 8), 8), :] = v
                out += [decay_in, state_in]
            return tuple(out)

        one, zero = jnp.ones((1, L), F32), jnp.zeros((1, L), F32)
        ends = lax.fori_loop(0, G // 16, scan, (one, zero) * B)
        r.pk[0] = jnp.zeros((8, L), F32)
        for b in range(B):
            r.pk[0, b : b + 1, :] = ends[2 * b]
            r.pk[0, B + b : B + b + 1, :] = ends[2 * b + 1]
            r.cfp[b, G : G + 8, :] = jnp.ones((8, L), F32)
        pairs_send(0)
        transposed(nm_v, r.nmT)
        ld_cot.wait()
        transposed(r.cot_v, r.cotT)
        entered = pairs_enter(0, False)
        for b in range(B):
            r.stp[b, 0:8, :] = jnp.broadcast_to(entered[b : b + 1], (8, L))

        def states(i):
            for b in range(B):
                at = rows16(i, b * G)
                here = pl.ds(pl.multiple_of(8 + i * 16, 8), 16)
                state = r.stp[b, here, :] + r.aloc[at, :] * r.stp[b, 7:8, :]
                r.stp[b, here, :] = state
                r.mx[x, at, 0:L] = (state * gelu_tanh(r.pre_gel[at, :])).astype(BF16)

        loop(G // 16, states)
        ld_out.wait()
        psum_start(
            0,
            lambda col: dot(r.mx[x, :, 0:L], wout_v[:, pl.ds(pl.multiple_of(col, CB), CB)]),
        )
        hx_send(6)
        ez_send(0, r.cotT)
        ez_send(1, r.nmT)

    pl.run_scoped(
        recurrent_forward,
        pltpu.VMEM((D, L), BF16),
        pltpu.VMEM((D, L), BF16),
        pltpu.VMEM((L, D), BF16),
        pltpu.VMEM((T, D), BF16),
        pltpu.VMEM((B * 16, D), BF16),
        pltpu.VMEM((T, L), F32),
        pltpu.VMEM((T, L), F32),
        pltpu.VMEM((2, 2 * HW, L), BF16),
    )

    def feed_forward(wd_v, wg_v, wu_v, nf, gh, pg, pu):
        ld_d = [local(r.w_down.at[pl.ds(i * FB, FB)], wd_v.at[i], i) for i in range(3)]
        ld_g = [local(r.w_gate.at[:, pl.ds(i * FB, FB)], wg_v.at[i], 3 + i) for i in range(3)]
        ld_u = [local(r.w_up.at[:, pl.ds(i * FB, FB)], wu_v.at[i], 6 + i) for i in range(3)]
        for i in range(3):
            ld_d[i].wait()

        def hidden_grad(i):
            gh[i] = dot_nt(r.cot_v[...], wd_v[i])

        loop(3, hidden_grad)
        psum_finish(0)

        def residual(i):
            at = rows16(i)
            parts = [
                r.tot[j, at, :] + r.x_v[at, j * CB : (j + 1) * CB].astype(F32)
                for j in range(2 * nb)
            ]
            square = parts[0] * parts[0]
            for v in parts[1:]:
                square = square + v * v
            scale = lax.rsqrt(jnp.sum(square, axis=1, keepdims=True) / D + EPS)
            for j, v in enumerate(parts):
                cols = slice(j * CB, (j + 1) * CB)
                r.resid[at, cols] = v
                nf[at, cols] = (v * scale * r.gains[1:2, cols]).astype(BF16)
            r.scf[at, :] = jnp.broadcast_to(scale, (16, 128))

        loop(T // 16, residual)
        for i in range(3):
            ld_g[i].wait()
            ld_u[i].wait()

        for i in range(3):
            pg[...] = dot(nf[...], wg_v[i])
            pu[...] = dot(nf[...], wu_v[i])

            def units(t, i=i):
                at = rows16(t)
                up, back = pu[at, :], gh[i, at, :]
                active, slope = gelu_and_slope(pg[at, :])
                r.hd[i, at, :] = (active * up).astype(BF16)
                r.gp[2 * i, x, at, :] = (back * up * slope).astype(BF16)
                r.gp[2 * i + 1, x, at, :] = (back * active).astype(BF16)

            loop(T // 16, units)
            q_send(i)
            if i == 0:
                transposed(nf, r.nfT)
                ex_send(0, r.nfT)
            hx_send(2 * i)
            hx_send(2 * i + 1)

        def back_input(col):
            at = pl.ds(pl.multiple_of(col, CB), CB)
            v = dot_nt(r.gp[0, x], wg_v[0, at, :]) + dot_nt(r.gp[1, x], wu_v[0, at, :])
            for i in range(1, 3):
                v = v + dot_nt(r.gp[2 * i, x], wg_v[i, at, :])
                v = v + dot_nt(r.gp[2 * i + 1, x], wu_v[i, at, :])
            return v

        psum_start(1, back_input)

        def ffn_term(j):
            at = pl.ds(pl.multiple_of(j * CB, CB), CB)
            v = dot(r.hd[0], wd_v[0, :, at])
            for i in range(1, 3):
                v = v + dot(r.hd[i], wd_v[i, :, at])
            r.fo[j] = v.astype(BF16)

        loop(2 * nb, ffn_term)

    pl.run_scoped(
        feed_forward,
        pltpu.VMEM((3, FB, D), BF16),
        pltpu.VMEM((3, D, FB), BF16),
        pltpu.VMEM((3, D, FB), BF16),
        pltpu.VMEM((T, D), BF16),
        pltpu.VMEM((3, T, FB), F32),
        pltpu.VMEM((T, FB), F32),
        pltpu.VMEM((T, FB), F32),
    )

    def gain_rows(which):
        total = jnp.sum(r.gacc[...], axis=0, keepdims=True)
        for q in range(nseq):
            r.gsend[q, which : which + 1, :] = total[:, q * DC : (q + 1) * DC]

    def after_feed_forward(stage_f, load_f, pacc, ost_f, hload, qstage, q_own_sum):
        out_copies = {}

        def emit(ref, value, buf, sem):
            if sem in out_copies:
                out_copies[sem]().wait()

            def copy():
                return pltpu.make_async_copy(buf(), ref(), r.ow.at[sem])

            buf()[...] = value
            copy().start()
            out_copies[sem] = copy

        ffn = types.SimpleNamespace(
            n=FB,
            e=0,
            own=r.nfT,
            hx=lambda b: r.gp.at[b],
            land=lambda b, slot: r.land_f.at[b, slot],
            stage=lambda b, zc: stage_f.at[lax.rem(b, 2), zc],
            load=lambda slot: load_f.at[slot],
        )
        def sized(ref, n):
            return ref if n == d.W else ref.at[:, pl.ds(0, n)]

        def q_width(qb):
            return FB if qb < 3 else LP

        def q_exchange(qb, k):
            to = lax.rem(x + k, nx)
            land = r.xr_d.at[qb, nx - k - 1] if qb < 3 else r.xr_r.at[qb - 3, nx - k - 1]
            piece = sized(qstage.at[qb % 2, k - 1], q_width(qb))
            return remote(
                piece, land, r.xr_s.at[qb, k], r.xr_rs.at[qb, k], (z * nx + to, m)
            )

        def q_product(qb, e, e_own):
            n, own = q_width(qb), q_own(qb)

            def load(k):
                zo = lax.rem(z + k, nz)
                return pltpu.make_async_copy(
                    q_land(qb, zo), sized(hload.at[k - 1], n), r.ow.at[8 + k]
                )

            for k in range(1, nz):
                load(k).start()
            for k in range(1, nz):
                load(k).wait()
            for k in list(range(1, nx)) + [0]:
                xk = lax.rem(x + k, nx)
                v = dot(e_own[z * nx + xk], own[...])
                for k2 in range(1, nz):
                    zo = lax.rem(z + k2, nz)
                    v = v + dot(r.ez[e, zo, xk], sized(hload.at[k2 - 1], n)[...])
                if k == 0:
                    return v
                sized(qstage.at[qb % 2, k - 1], n)[...] = v.astype(BF16)
                q_exchange(qb, k).start()

        def q_close(qb, value):
            for k in range(1, nx):
                q_exchange(qb, k).wait()
            for k in range(1, nx):
                land = r.xr_d.at[qb, nx - k - 1] if qb < 3 else r.xr_r.at[qb - 3, nx - k - 1]
                value = value + land[...].astype(F32)
            return value

        def q_keep(qb):
            return q_own_sum.at[qb % 2, :, pl.ds(0, q_width(qb))]

        def q_first(qb):
            e, e_own = (0, r.cotT) if qb < 3 else (1, r.nmT)
            q_keep(qb)[...] = q_product(qb, e, e_own)

        def p_part(f, b, zc):
            hx = f.hx(b)
            v = dot(f.own[zc * nx + x], hx[x])
            for k in range(1, nx):
                xk = lax.rem(x + k, nx)
                v = v + dot(r.ex[f.e, xk, zc], hx[xk])
            return v

        def p_copy(f, b, zc, slot, to):
            return remote(
                f.stage(b, zc), f.land(b, slot), r.p_s.at[b, zc], r.p_r.at[b, slot], (to, m)
            )

        def p_load(f, b, slot, at):
            return pltpu.make_async_copy(f.land(b, slot), f.load(at), r.pl_s.at[at])

        def p_arrived(f, b, slot, at):
            p_copy(f, b, 0, slot, s).wait_recv()
            p_load(f, b, slot, at).start()

        def p_add(f, b, slot, at):
            p_load(f, b, slot, at).wait()
            pacc[:, 0 : f.n] += f.load(at)[...].astype(F32)

        def p_pass(f, b, right):
            has_input = z > 0 if right else z < nz - 1
            bias = 0 if right else nz - 1
            for dist in range(nz - 1, 0, -1):
                zc = z + dist if right else z - dist

                @pl.when(zc <= nz - 1 if right else zc >= 0)
                def _(dist=dist, zc=zc):
                    @pl.when(has_input)
                    def _():
                        p_arrived(f, b, bias + dist, 0)

                    pacc[:, 0 : f.n] = p_part(f, b, zc)

                    @pl.when(has_input)
                    def _():
                        p_add(f, b, bias + dist, 0)

                    if f is ffn:

                        @pl.when(b >= 2)
                        def _():
                            p_copy(f, b - 2, zc, 0, s).wait_send()

                    f.stage(b, zc)[...] = pacc[:, 0 : f.n].astype(BF16)
                    p_copy(f, b, zc, bias + dist - 1, s + nx if right else s - nx).start()

        def p_final(f, b):
            @pl.when(z > 0)
            def _():
                p_arrived(f, b, 0, 0)

            @pl.when(z < nz - 1)
            def _():
                p_arrived(f, b, nz - 1, 1)

            pacc[:, 0 : f.n] = p_part(f, b, z)

            @pl.when(z > 0)
            def _():
                p_add(f, b, 0, 0)

            @pl.when(z < nz - 1)
            def _():
                p_add(f, b, nz - 1, 1)

        def slot(k, out=None):
            if k == 0:
                ex_wait(0)
            if k < 6:
                hx_wait(k)
            if k == 6:
                hx_wait(6)
                ex_wait(1)
            for right in (True, False):
                b = k - z if right else k - (nz - 1) + z
                if k < 6 + nz - 1:

                    @pl.when((b >= 0) & (b < 6))
                    def _(b=b, right=right):
                        p_pass(ffn, b, right)

                if k >= 6:

                    @pl.when(b == 6)
                    def _(right=right):
                        p_pass(out, 6, right)

            b = k - (nz - 1)
            if 0 <= b < 6:
                p_final(ffn, b)
                ref = r.o_wup if b % 2 else r.o_wgate
                at = b // 2 * FB
                emit(
                    lambda: ref.at[:, at : at + FB], pacc[:, 0:FB], lambda: ost_f.at[b % 2], 4 + b % 2
                )

        def recurrent_backward(
            w_v, wout_v, gr, gb, gm, gcd, gcp, gmel, gpa, gpx, adj, t2
        ):
            ld_gel = local(r.w_gel, w_v, 2)
            ld_out = local(r.w_out, wout_v, 3)
            r.gsend[...] = jnp.zeros((nseq, 8, DC), F32)
            slot(0)
            for qb in range(2):
                q_forward(qb, 1)
            psum_finish(1)
            r.gacc[...] = jnp.zeros((16, D), F32)

            def norm_back(i):
                at = rows16(i)
                scale = r.scf[at, :][:, 0:1]
                inner = jnp.zeros((16, CB), F32)
                for j in range(2 * nb):
                    cols = slice(j * CB, (j + 1) * CB)
                    inner = inner + r.tot[j, at, :] * r.gains[1:2, cols] * r.resid[at, cols]
                factor = (scale * scale * scale) * (jnp.sum(inner, axis=1, keepdims=True) / D)
                for j in range(2 * nb):
                    cols = slice(j * CB, (j + 1) * CB)
                    n, v = r.tot[j, at, :], r.resid[at, cols]
                    r.gacc[:, cols] += n * v * scale
                    grad = r.cot_v[at, cols].astype(F32) + (
                        scale * (n * r.gains[1:2, cols]) - v * factor
                    )
                    gr[at, cols] = grad
                    gb[at, cols] = grad.astype(BF16)

            loop(T // 16, norm_back)
            gain_rows(1)
            ld_out.wait()
            gm[...] = dot_nt(gb[...], wout_v[...])

            def scan(t, carry):
                i = G // 16 - 1 - t
                out = []
                for b in range(B):
                    decay_in, value_in = carry[2 * b], carry[2 * b + 1]
                    at = rows16(i, b * G)
                    gate, slope = gelu_and_slope(r.pre_gel[at, :])
                    g = gm[at, :]
                    state = r.stp[b, pl.ds(pl.multiple_of(8 + i * 16, 8), 16), :]
                    r.gpg[at, 0:L] = (g * state * slope).astype(BF16)
                    value16 = g * gate
                    following = r.cfp[b, pl.ds(pl.multiple_of(i * 16, 16), 24), :][1:17]
                    for h in (1, 0):
                        a, v = scan_tile(
                            following[8 * h : 8 * h + 8], value16[8 * h : 8 * h + 8], reverse=True
                        )
                        v = v + a * value_in
                        a = a * decay_in
                        decay_in, value_in = a[0:1], v[0:1]
                        here = pl.ds(pl.multiple_of(b * G + i * 16 + 8 * h, 8), 8)
                        r.aloc[here, :] = a
                        adj[here, :] = v
                    out += [decay_in, value_in]
                return tuple(out)

            one, zero = jnp.ones((1, L), F32), jnp.zeros((1, L), F32)
            ends = lax.fori_loop(0, G // 16, scan, (one, zero) * B)
            r.pk[1] = jnp.zeros((8, L), F32)
            for b in range(B):
                first = r.cfp[b, 0:1, :]
                r.pk[1, b : b + 1, :] = first * ends[2 * b]
                r.pk[1, B + b : B + b + 1, :] = first * ends[2 * b + 1]
            pairs_send(1)
            q_send(3)
            ld_gel.wait()

            def gel_term(j):
                at = pl.ds(pl.multiple_of(j * CB, CB), CB)
                gmel[j] = dot_nt(r.gpg[:, 0:L], w_v[at, :])

            loop(2 * nb, gel_term)
            ld_rec = local(r.w_rec, w_v, 1)
            transposed(gb, r.gbT)
            ex_send(1, r.gbT)
            q_forward(2, 1)
            slot(1)
            q_forward(0, 2)
            outer = pairs_enter(1, True)

            def gate_back(i):
                for b in range(B):
                    at = rows16(i, b * G)
                    adjoint = adj[at, :] + r.aloc[at, :] * outer[b : b + 1]
                    recur, inject = r.recur[at, :], r.inj[at, :]
                    log_decay = r.rv[0:1] * recur
                    decay = jnp.exp(log_decay)
                    value = r.cv[at, 0:L].astype(F32)
                    spread = jnp.sqrt(minus_expm1(2.0 * log_decay))
                    prior = r.stp[b, pl.ds(pl.multiple_of(i * 16, 16), 24), :][7:23]
                    keep = r.mk[b, rows16(i), :][:, 1:2]
                    grad_log = (
                        adjoint * inject * value * (-(decay * decay) / spread)
                        + adjoint * prior * keep * decay
                    )
                    ga = (grad_log * r.rv[0:1] * recur * (1.0 - recur)).astype(BF16)
                    direct = adjoint * spread * inject
                    gx = (adjoint * spread * value * inject * (1.0 - inject)).astype(BF16)
                    gpa[at, :] = ga
                    gpx[at, :] = gx
                    gcd[at, :] = direct
                    r.sacc[5] += fold8(ga.astype(F32))
                    r.sacc[6] += fold8(gx.astype(F32))
                    r.sacc[7] += fold8(grad_log * recur)

            loop(G // 16, gate_back)
            r.gs_l[...] = (dot_nt(gpa[...], r.wl[0]) + dot_nt(gpx[...], r.wl[1])).astype(BF16)

            def to_left():
                return remote(r.gs_l, r.gi_r, r.gi_s.at[0], r.gi_rs.at[0], (s, left_m))

            start(to_left)
            r.gs_r[...] = (dot_nt(gpa[...], r.wr[0]) + dot_nt(gpx[...], r.wr[1])).astype(BF16)

            def to_right():
                return remote(r.gs_r, r.gi_l, r.gi_s.at[1], r.gi_rs.at[1], (s, right_m))

            start(to_right)
            own = dot_nt(gpa[...], r.wo[0]) + dot_nt(gpx[...], r.wo[1])
            gcd[...] += own[:, 0:L]

            slot(2)
            q_forward(1, 2)

            for i, grad in enumerate((gpa, gpx)):
                turned = jnp.where(head_mask(base - HW, HW), dot(r.hl[...].T, grad[...]), 0.0)
                t2[0:HW, :] = turned
                for p, n in pieces:
                    part = dot(r.cv[:, p : p + n].T, grad[...])
                    t2[0:n, :] += jnp.where(head_mask(base + p, n), part, 0.0)
                t2[HW : 2 * HW, :] = t2[0:HW, :]
                back = pl.multiple_of(lax.rem(HW - turn, HW), HW // 4)
                table = t2[pl.ds(back, HW), :]
                right = jnp.where(head_mask(base + L, HW), dot(r.hr[...].T, grad[...]), 0.0)
                t2[0:HW, :] = right
                t2[HW : 2 * HW, :] = right
                back = pl.multiple_of(lax.rem(HW - turn_right, HW), HW // 4)
                r.gt[i] = (table + t2[pl.ds(back, HW), :]).astype(BF16)

            to_left().wait_recv()
            to_right().wait_recv()
            gcd[:, 0:HW] += r.gi_l[...].astype(F32)
            gcd[:, L - HW : L] += r.gi_r[...].astype(F32)
            for b in range(B):
                gcp[b, 0:G, :] = gcd[b * G : (b + 1) * G, :]
                gcp[b, G : G + 8, :] = jnp.zeros((8, L), F32)

            for b in range(B):
                top, keep = gcp[b, 0:8, :], r.mk[b, 0:8, :]
                spill = jnp.zeros((8, L), F32)
                row = lax.broadcasted_iota(jnp.int32, (8, L), 0)
                for k in range(1, d.taps):
                    moved = pltpu.roll(r.vecs[k : k + 1] * (keep[:, k : k + 1] * top), 8 - k, 0)
                    spill = spill + jnp.where(row >= 8 - k, moved, 0.0)
                r.sp_s[b * 8 : (b + 1) * 8, :] = spill

            def spilled():
                return remote(r.sp_s, r.sp_r, r.sp_ss.at[0], r.sp_rs.at[0], (s - 1, m))

            start(spilled, lambda: s > 0)

            @pl.when(s == nseq - 1)
            def _():
                r.sp_r[...] = jnp.zeros((B * 8, L), F32)

            def conv_back(i, spill):
                for b in range(B):
                    grads = gcp[b, pl.ds(pl.multiple_of(i * 16, 16), 24), :]
                    keep = r.mk[b, pl.ds(pl.multiple_of(i * 16, 16), 24), :]
                    window = r.extp[b, pl.ds(pl.multiple_of(i * 16 + 8, 8), 24), :]
                    here = grads[0:16]
                    out = r.vecs[0:1] * here
                    if not spill:
                        r.sacc[4] += fold8(here)
                        r.sacc[0] += fold8(here * window[8:24])
                    for k in range(1, d.taps):
                        masked = keep[:, k : k + 1] * grads
                        out = out + r.vecs[k : k + 1] * masked[k : k + 16]
                        if not spill:
                            r.sacc[k] += fold8(masked[0:16] * window[8 - k : 24 - k])
                    if spill:
                        extra = r.sp_r[b * 8 : (b + 1) * 8, :]
                        out = out + jnp.concatenate([jnp.zeros((8, L), F32), extra], axis=0)
                    r.gpr[rows16(i, b * G), 0:L] = out.astype(BF16)

            loop(G // 16, lambda i: conv_back(i, False))
            for k in range(8):
                r.smv[k : k + 1, :] = jnp.sum(r.sacc[k], axis=0, keepdims=True)

            slot(3)
            q_forward(2, 2)

            @pl.when(s < nseq - 1)
            def _():
                spilled().wait_recv()

            conv_back(G // 16 - 1, True)
            q_send(4)
            ld_rec.wait()

            def mix_term(col):
                at = pl.ds(pl.multiple_of(col, CB), CB)
                return dot_nt(r.gpr[:, 0:L], w_v[at, :]) + gmel[lax.div(col, CB)]

            psum_start(2, mix_term)
            q_forward(3, 1)

            def small_copy(q):
                to = lax.rem(s + q, nseq)
                return remote(r.smv, r.smland.at[s], r.sm_s.at[q], r.sm_r.at[q], (to, m))

            def gates_copy(q):
                to = lax.rem(s + q, nseq)
                rows = pl.ds(pl.multiple_of(to * d.GR, 16), d.GR)
                return remote(
                    r.gt.at[:, rows, :], r.gtland.at[s], r.gt_s.at[q], r.gt_r.at[q], (to, m)
                )

            def gain_copy(q):
                to = lax.rem(s + q, nseq)
                return remote(r.gsend.at[to], r.gland.at[s], r.ga_s.at[q], r.ga_r.at[q], (to, m))

            for q in range(1, nseq):
                start(functools.partial(small_copy, q))
                start(functools.partial(gates_copy, q))
            slot(4)
            ez_wait(0)
            q_forward(0, 3)
            q_first(0)
            psum_finish(2)

            r.gacc[...] = jnp.zeros((16, D), F32)

            def norm_back_mix(i):
                at = rows16(i)
                scale = r.scm[at, :][:, 0:1]
                inner = jnp.zeros((16, CB), F32)
                for j in range(2 * nb):
                    cols = slice(j * CB, (j + 1) * CB)
                    v = r.x_v[at, cols].astype(F32)
                    inner = inner + r.tot[j, at, :] * r.gains[0:1, cols] * v
                factor = (scale * scale * scale) * (jnp.sum(inner, axis=1, keepdims=True) / D)
                for j in range(2 * nb):
                    cols = slice(j * CB, (j + 1) * CB)
                    n, v = r.tot[j, at, :], r.x_v[at, cols].astype(F32)
                    r.gacc[:, cols] += n * v * scale
                    gr[at, cols] = gr[at, cols] + (scale * (n * r.gains[0:1, cols]) - v * factor)

            loop(T // 16, norm_back_mix)
            out_gin = pltpu.make_async_copy(gr, r.o_gin, r.ow.at[0])
            out_gin.start()
            gain_rows(0)
            for q in range(1, nseq):
                start(functools.partial(gain_copy, q))

            psum_start(3, lambda col: r.fo[lax.div(col, CB)].astype(F32))
            slot(5)
            q_forward(3, 2)
            q_forward(4, 1)
            q_forward(1, 3)
            q_first(1)
            psum_finish(3)

            def block_out(i):
                at = rows16(i)
                for j in range(2 * nb):
                    cols = slice(j * CB, (j + 1) * CB)
                    r.resid[at, cols] += r.tot[j, at, :]

            loop(T // 16, block_out)
            out_block = pltpu.make_async_copy(r.resid, r.o_block, r.ow.at[1])
            out_block.start()

            out_gin.wait()
            out_block.wait()

        pl.run_scoped(
            recurrent_backward,
            pltpu.VMEM((D, L), BF16),
            pltpu.VMEM((L, D), BF16),
            pltpu.VMEM((T, D), F32),
            pltpu.VMEM((T, D), BF16),
            pltpu.VMEM((T, L), F32),
            pltpu.VMEM((T, L), F32),
            pltpu.VMEM((B, G + 8, L), F32),
            pltpu.VMEM((2 * nb, T, CB), F32),
            pltpu.VMEM((T, L), BF16),
            pltpu.VMEM((T, L), BF16),
            pltpu.VMEM((T, L), F32),
            pltpu.VMEM((2 * HW, L), F32),
        )


        def rest(stage_o, load_o, ost_d, ost_r, ost_o):
            out = types.SimpleNamespace(
                n=LP,
                e=1,
                own=r.gbT,
                hx=lambda b: r.mx,
                land=lambda b, slot: r.land_o.at[slot],
                stage=lambda b, zc: stage_o.at[zc],
                load=lambda slot: load_o.at[slot],
            )

            def q_last(qb):
                value = q_close(qb, q_keep(qb)[...])
                if qb < 3:
                    emit(
                        lambda: r.o_wdown.at[qb * FB : (qb + 1) * FB],
                        value.T,
                        lambda: ost_d.at[qb % 2],
                        7 + qb % 2,
                    )
                else:
                    ref = r.o_wgel if qb == 3 else r.o_wrec
                    emit(lambda: ref, value[:, 0:L], lambda: ost_r.at[qb % 2], 12 + qb % 2)

            slot(6, out)
            q_forward(4, 2)
            q_last(0)
            q_forward(2, 3)
            q_first(2)
            slot(7, out)
            q_last(1)
            q_forward(3, 3)
            ez_wait(1)
            q_first(3)
            slot(8, out)
            q_last(2)
            q_forward(4, 3)
            q_first(4)
            slot(9, out)
            p_final(out, 6)
            emit(lambda: r.o_wout, pacc[:, 0:LP].T[0:L], lambda: ost_o, 6)
            q_last(3)
            q_last(4)
            for b in (4, 5, 6):
                for dist in range(1, nz):
                    f = out if b == 6 else ffn

                    @pl.when(z + dist <= nz - 1)
                    def _(f=f, b=b, dist=dist):
                        p_copy(f, b, z + dist, 0, s).wait_send()

                    @pl.when(z - dist >= 0)
                    def _(f=f, b=b, dist=dist):
                        p_copy(f, b, z - dist, 0, s).wait_send()

            for q in range(1, nseq):
                src = lax.rem(s + nseq - q, nseq)
                remote(r.smv, r.smland.at[src], r.sm_s.at[q], r.sm_r.at[q], partner).wait_recv()
                remote(
                    r.gsend.at[src], r.gland.at[src], r.ga_s.at[q], r.ga_r.at[q], partner
                ).wait_recv()
                remote(
                    r.gtland.at[src], r.gtland.at[src], r.gt_s.at[q], r.gt_r.at[q], partner
                ).wait_recv()
            r.smland[s] = r.smv[...]
            r.gland[s] = r.gsend[s]
            r.gtland[s] = r.gt[:, pl.ds(pl.multiple_of(s * d.GR, 16), d.GR), :]
            small, gain, gates = r.smland[0], r.gland[0], r.gtland[0].astype(F32)
            for q in range(1, nseq):
                small = small + r.smland[q]
                gain = gain + r.gland[q]
                gates = gates + r.gtland[q].astype(F32)
            r.o_small[...] = small
            r.o_small[7:8, :] = small[7:8, :] * r.rv[1:2, :]
            r.o_gain[...] = gain
            r.o_gates[...] = gates

            for copy in out_copies.values():
                copy().wait()
            for make, when in pending:
                if when is None:
                    make().wait_send()
                else:
                    pl.when(when())(lambda make=make: make().wait_send())


        pl.run_scoped(
            rest,
            pltpu.VMEM((nz, DC, LP), BF16),
            pltpu.VMEM((2, DC, LP), BF16),
            pltpu.VMEM((2, FB, DC), F32),
            pltpu.VMEM((2, DC, L), F32),
            pltpu.VMEM((L, DC), F32),
        )

    pl.run_scoped(
        after_feed_forward,
        pltpu.VMEM((2, nz, DC, FB), BF16),
        pltpu.VMEM((2, DC, FB), BF16),
        pltpu.VMEM((DC, d.W), F32),
        pltpu.VMEM((2, DC, FB), F32),
        pltpu.VMEM((nz - 1, T, d.W), BF16),
        pltpu.VMEM((2, nx - 1, DC, d.W), BF16),
        pltpu.VMEM((2, DC, d.W), F32),
    )


IN_ANY = ("x_in", "w_rec", "w_gel", "w_out", "gate_a", "gate_x", "w_gate", "w_up", "w_down", "cot")
IN_VMEM = ("ids", "gains", "vecs")
OUT_VMEM = ("o_small", "o_gain", "o_gates")


def on_device(nseq, nm, *args):
    (
        block_input,
        segment_ids,
        gain_mix,
        w_rec,
        w_gel,
        conv_weight,
        conv_bias,
        gate_a,
        gate_x,
        bias_a,
        bias_x,
        log_rate,
        w_out,
        gain_ffn,
        w_gate,
        w_up,
        w_down,
        cotangent,
    ) = args
    B, G, D = block_input.shape
    T, L, F = B * G, w_rec.shape[1], w_gate.shape[1]
    nz = Z_CHIPS
    d = types.SimpleNamespace(
        B=B, G=G, T=T, D=D, L=L, F=F, LP=-(-L // 128) * 128, FB=F // 3, HW=gate_a.shape[0],
        DC=D // nseq, nseq=nseq, nm=nm, nz=nz, nx=nseq // nz, ny=nm // CORES, CB=256,
        nb=D // CORES // 256, taps=conv_weight.shape[0], GR=gate_a.shape[0] // nseq,
    )
    d.W = max(d.FB, d.LP)
    outs, scratch, sems = layout(d)
    vecs = jnp.concatenate([conv_weight, jnp.stack([conv_bias, bias_a, bias_x, log_rate])])
    gains = jnp.stack([gain_mix, gain_ffn])
    feed = dict(
        x_in=block_input.reshape(T, D), w_rec=w_rec, w_gel=w_gel, w_out=w_out, gate_a=gate_a,
        gate_x=gate_x, w_gate=w_gate, w_up=w_up, w_down=w_down, cot=cotangent.reshape(T, D),
        ids=segment_ids, gains=gains, vecs=vecs,
    )
    names_in = IN_ANY + IN_VMEM
    names = names_in + tuple(outs) + tuple(scratch) + tuple(sems)

    def kernel(*refs):
        body(d, types.SimpleNamespace(**dict(zip(names, refs))))

    results = pl.pallas_call(
        kernel,
        out_shape=[jax.ShapeDtypeStruct(*v) for v in outs.values()],
        in_specs=[pl.BlockSpec(memory_space=pl.ANY)] * len(IN_ANY)
        + [pl.BlockSpec(memory_space=pltpu.VMEM)] * len(IN_VMEM),
        out_specs=[
            pl.BlockSpec(memory_space=pltpu.VMEM if n in OUT_VMEM else pl.ANY) for n in outs
        ],
        scratch_shapes=[pltpu.VMEM(*v) for v in scratch.values()]
        + [pltpu.SemaphoreType.DMA(v) for v in sems.values()],
        compiler_params=pltpu.CompilerParams(
            collective_id=0, has_side_effects=True, vmem_limit_bytes=62 * 2**20
        ),
        name="block",
    )(*[feed[n] for n in names_in])
    o = types.SimpleNamespace(**dict(zip(outs, results)))
    place = lax.axis_index("seq")
    n = L // nseq
    small = lax.dynamic_slice_in_dim(o.o_small, place * n, n, 1)
    return (
        o.o_block.reshape(B, G, D),
        o.o_gin.reshape(B, G, D),
        o.o_gain[0],
        o.o_wrec,
        o.o_wgel,
        small[0:4],
        small[4],
        o.o_gates[0],
        o.o_gates[1],
        small[5],
        small[6],
        small[7],
        o.o_wout,
        o.o_gain[1],
        o.o_wgate,
        o.o_wup,
        o.o_wdown,
    )


def solution(mesh):
    nseq, nm = mesh.shape["seq"], mesh.shape["mp"]
    rows, cols, both = P(None, "seq", None), P(None, "mp"), P(("mp", "seq"))
    part = P("seq", "mp")
    in_specs = (
        rows, P(), P(), cols, cols, cols, P("mp"), cols, cols, P("mp"), P("mp"), P("mp"),
        P("mp", None), P(), cols, cols, P("mp", None), rows,
    )
    out_specs = (
        rows, rows, P("seq"), part, part, P(None, ("mp", "seq")), both, part, part, both, both,
        both, P("mp", "seq"), P("seq"), part, part, P("mp", "seq"),
    )

    def step(*args):
        return on_device(nseq, nm, *args)

    return jax.shard_map(step, mesh=mesh, in_specs=in_specs, out_specs=out_specs, check_vma=False)
```

```python
import functools
import types

import jax
import jax.numpy as jnp
from jax import lax
from jax.experimental import pallas as pl
from jax.experimental.pallas import tpu as pltpu
from jax.sharding import PartitionSpec as P

EPS = 1e-06
RATE_SCALE = 8.0
Z_CHIPS = 4
CORES = 2
GELU_C = 0.7978845608028654
GELU_A = 0.044715
MESH = pl.DeviceIdType.MESH
F32 = jnp.float32
BF16 = jnp.bfloat16

SCHEDULE = (
    (
        (),
        (),
        (),
        (),
    ),
    (
        (("P", 0, 1, 3), ("P", 0, 1, 2), ("P", 0, 1, 1), ("O", 0),),
        (("F", 0, 0), ("F", 0, 2), ("F", 1, 0), ("F", 1, 2), ("O", 0), ("F", 2, 0), ("F", 2, 2),),
        (("F", 0, 1), ("F", 0, 3), ("F", 1, 1), ("F", 1, 3), ("O", 0), ("F", 2, 1), ("F", 2, 3),),
        (("P", 0, -1, 0), ("P", 0, -1, 1), ("P", 0, -1, 2), ("O", 0),),
    ),
    (
        (("P", 1, 1, 3), ("P", 1, 1, 2), ("O", 1), ("O", 2), ("O", 3), ("P", 1, 1, 1), ("O", 4),),
        (("F", 0, 3), ("F", 1, 3), ("P", 0, 1, 3), ("F", 2, 3), ("P", 0, 1, 2),),
        (("F", 0, 0), ("F", 1, 0), ("P", 0, -1, 0), ("F", 2, 0), ("P", 0, -1, 1),),
        (),
    ),
    (
        (("P", 2, 1, 3), ("O", 5),),
        (("F", 3, 0), ("F", 3, 2), ("Q", 0), ("P", 1, 1, 3),),
        (("F", 3, 1), ("F", 3, 3), ("Q", 0),),
        (("P", 1, -1, 0), ("P", 1, -1, 1),),
    ),
    (
        (("P", 2, 1, 2), ("Q", 0), ("P", 2, 1, 1), ("Q", 1), ("P", 3, 1, 3), ("P", 3, 1, 2), ("Q", 2),),
        (("P", 1, 1, 2), ("P", 0, -1, 0), ("F", 3, 3), ("P", 2, 1, 3), ("P", 2, 1, 2),),
        (("P", 0, 1, 3), ("P", 1, -1, 0), ("F", 3, 0), ("P", 1, -1, 1), ("F", 4, 3),),
        (),
    ),
    (
        (("P", 3, 1, 1), ("Q", 3), ("P", 4, 1, 3), ("P", 4, 1, 2),),
        (("P", 1, -1, 0), ("P", 3, 1, 3), ("F", 4, 3), ("Q", 1), ("F", 4, 2), ("P", 3, 1, 2), ("F", 4, 0),),
        (("P", 1, 1, 3), ("P", 2, -1, 0), ("P", 2, 1, 3), ("Q", 1),),
        (("P", 1, -1, 2), ("Q", 0), ("P", 2, -1, 0), ("Q", 1),),
    ),
    (
        (("P", 4, 1, 1), ("P", 5, 1, 3), ("P", 5, 1, 2),),
        (("P", 4, 1, 3), ("P", 2, -1, 0), ("P", 4, 1, 2), ("P", 3, -1, 0),),
        (("F", 4, 1), ("P", 2, -1, 1), ("P", 3, -1, 0), ("P", 3, 1, 3), ("P", 3, -1, 1), ("F", 4, 0),),
        (("P", 2, -1, 1), ("P", 2, -1, 2), ("Q", 2), ("P", 3, -1, 0), ("Q", 3),),
    ),
    (
        (("O", 6), ("P", 5, 1, 1), ("Q", 4), ("P", 6, 1, 3), ("P", 6, 1, 2), ("P", 6, 1, 1),),
        (("Q", 2), ("P", 5, 1, 3), ("P", 5, 1, 2), ("P", 4, -1, 0), ("Q", 3), ("P", 6, 1, 3), ("P", 5, -1, 0), ("P", 6, 1, 2), ("Q", 4), ("P", 6, -1, 0), ("O", 1), ("O", 2), ("O", 3), ("O", 4), ("O", 5), ("O", 6),),
        (("P", 4, -1, 0), ("P", 4, -1, 1), ("Q", 2), ("P", 4, 1, 3), ("P", 5, -1, 0), ("P", 5, -1, 1), ("P", 5, 1, 3), ("Q", 3), ("P", 6, -1, 0), ("Q", 4), ("P", 6, 1, 3), ("P", 6, -1, 1), ("O", 1), ("O", 2), ("O", 3), ("O", 4), ("O", 5), ("O", 6),),
        (("P", 3, -1, 1), ("P", 3, -1, 2), ("O", 1), ("P", 4, -1, 0), ("O", 2), ("O", 3), ("O", 4), ("O", 5), ("P", 4, -1, 1), ("O", 6), ("P", 4, -1, 2), ("P", 5, -1, 0), ("P", 5, -1, 1), ("P", 5, -1, 2), ("P", 6, -1, 0), ("P", 6, -1, 1), ("Q", 4), ("P", 6, -1, 2),),
    ),
)


def dot(left, right):
    return jnp.dot(left, right, preferred_element_type=F32)


def dot_nt(left, right):
    return lax.dot_general(left, right, (((1,), (1,)), ((), ())), preferred_element_type=F32)


def remote(src, dst, send_sem, recv_sem, device):
    return pltpu.make_async_remote_copy(
        src_ref=src,
        dst_ref=dst,
        send_sem=send_sem,
        recv_sem=recv_sem,
        device_id=device,
        device_id_type=MESH,
    )


def loop(count, body):
    def step(i, carry):
        body(i)
        return carry

    lax.fori_loop(0, count, step, 0)


def rows16(i, offset=0):
    return pl.ds(pl.multiple_of(i * 16 + offset, 16), 16)


def gelu_tanh(v):
    t = jnp.tanh(GELU_C * (v + GELU_A * (v * v * v)))
    return 0.5 * v * (1.0 + t)


def gelu_and_slope(v):
    square = v * v
    t = jnp.tanh(GELU_C * (v + GELU_A * (square * v)))
    half = 0.5 * (1.0 + t)
    slope = half + 0.5 * v * (1.0 - t * t) * (GELU_C * (1.0 + 3.0 * GELU_A * square))
    return v * half, slope


def minus_expm1(v):
    acc = 1.0 + v * (1.0 / 8.0)
    for n in (7.0, 6.0, 5.0, 4.0, 3.0, 2.0):
        acc = 1.0 + v * (1.0 / n) * acc
    return -v * acc


def softplus_small(v):
    u = jnp.exp(v)
    acc = 1.0 / 6.0 - u * (1.0 / 7.0)
    for n in (5.0, 4.0, 3.0, 2.0):
        acc = 1.0 / n - u * acc
    return u * (1.0 - u * acc)


def scan_tile(decay, value, reverse):
    row = lax.broadcasted_iota(jnp.int32, decay.shape, 0)
    for k in (1, 2, 4):
        shift = 8 - k if reverse else k
        valid = row < 8 - k if reverse else row >= k
        decay_k = pltpu.roll(decay, shift, 0)
        value_k = pltpu.roll(value, shift, 0)
        value = jnp.where(valid, decay * value_k + value, value)
        decay = jnp.where(valid, decay * decay_k, decay)
    return decay, value


def fold8(v):
    return v[0:8] + v[8:16]


def layout(dims):
    d = dims
    T, D, L, LP, F, FB, DC = d.T, d.D, d.L, d.LP, d.F, d.FB, d.DC
    B, G, HW = d.B, d.G, d.HW
    outs = dict(
        k_block=((T, D), F32),
        k_gin=((T, D), F32),
        k_small=((8, LP), F32),
        k_gain=((8, DC), F32),
        k_gates=((2, d.GR, L), F32),
        own_f=((6, DC, FB), BF16),
        own_o=((DC, LP), BF16),
        own_d=((3, DC, FB), BF16),
        own_r=((2, DC, LP), BF16),
        land_f=((6, 2 * (d.nz - 1), DC, FB), BF16),
        land_o=((2 * (d.nz - 1), DC, LP), BF16),
        xr_d=((3, d.nx - 1, DC, FB), BF16),
        xr_r=((2, d.nx - 1, DC, LP), BF16),
        hz_d=((3, d.nz, T, FB), BF16),
        hz_r=((2, d.nz, T, LP), BF16),
    )
    scratch = dict(
        x_v=((T, D), BF16),
        cot_v=((T, D), BF16),
        xh=((B * 16, D), BF16),
        scm=((T, 128), F32),
        scf=((T, 128), F32),
        idp=((8, 2 * G), jnp.int32),
        mk=((B, G + 8, 128), F32),
        rv=((8, L), F32),
        wl=((2, HW, L), BF16),
        wo=((2, LP, L), BF16),
        wr=((2, HW, L), BF16),
        extp=((B, 16 + G, L), F32),
        cv=((T, LP), BF16),
        st_l=((T, HW), BF16),
        st_r=((T, HW), BF16),
        hl=((T, HW), BF16),
        hr=((T, HW), BF16),
        pre_gel=((T, L), F32),
        recur=((T, L), F32),
        inj=((T, L), F32),
        cfp=((B, G + 8, L), F32),
        aloc=((T, L), F32),
        stp=((B, 8 + G, L), F32),
        pk=((2, 8, L), F32),
        pf=((2, d.nseq, 8, L), F32),
        resid=((T, D), F32),
        csend=((d.nb, T, d.CB), F32),
        cland=((d.nb, T, d.CB), F32),
        tot=((2 * d.nb, T, d.CB), F32),
        yl=((2, d.ny, d.nb, T, d.CB), BF16),
        fo=((2 * d.nb, T, d.CB), BF16),
        hd=((3, T, FB), BF16),
        gp=((6, d.nx, T, FB), BF16),
        mx=((d.nx, T, LP), BF16),
        gpg=((T, LP), BF16),
        gpr=((T, LP), BF16),
        nmT=((d.nz, d.nx, DC, T), BF16),
        cotT=((d.nz, d.nx, DC, T), BF16),
        nfT=((d.nz, d.nx, DC, T), BF16),
        gbT=((d.nz, d.nx, DC, T), BF16),
        ez=((2, d.nx, DC, d.nz * T), BF16),
        ex=((2, d.nz, DC, d.nx * T), BF16),
        vecs=((8, L), F32),
        gains=((8, D), F32),
        gacc=((16, D), F32),
        gsend=((d.nseq, 8, DC), F32),
        gland=((d.nseq, 8, DC), F32),
        sacc=((8, 8, L), F32),
        smv=((8, L), F32),
        smx=((d.nx, 8, L), F32),
        smz=((d.nz, 8, L), F32),
        gt=((d.nz, d.nx, 2, d.GR, L), BF16),
        gtx=((d.nx, d.nz, 2, d.GR, L), BF16),
        gtz=((d.nz, 2, d.GR, L), BF16),
        gts=((d.nz, 2, d.GR, L), BF16),
        gs_l=((T, HW), BF16),
        gs_r=((T, HW), BF16),
        gi_l=((T, HW), BF16),
        gi_r=((T, HW), BF16),
        sp_s=((B * 8, L), F32),
        sp_r=((B * 8, L), F32),
    )
    sems = dict(
        ld=(16,),
        halo_s=(B,),
        halo_r=(B,),
        ex_s=(2,),
        ex_r=(2,),
        gi_s=(2,),
        gi_rs=(2,),
        pf_s=(2, d.nseq),
        pf_r=(2, d.nseq),
        c_s=(4, d.nb),
        c_r=(4, d.nb),
        y_s=(4, d.ny, d.nb),
        y_r=(4, d.ny, d.nb),
        a_s=(4, d.nb),
        a_r=(4, d.nb),
        ez_s=(2, d.nz),
        ez_r=(2, d.nz),
        ezc_s=(2, d.nz),
        ezc_r=(2, d.nz),
        ex_xs=(2, d.nx),
        ex_xr=(2, d.nx),
        exc_s=(2, d.nx),
        exc_r=(2, d.nx),
        own_l=(4,),
        hz_s=(5, d.nz, 2),
        hz_rs=(5, d.nz),
        hx_s=(7, d.nx),
        hx_r=(7, d.nx),
        xr_s=(5, d.nx),
        xr_rs=(5, d.nx),
        p_s=(7, d.nz),
        p_r=(7, 2 * (d.nz - 1)),
        smx_s=(d.nx,),
        smx_r=(d.nx,),
        smz_s=(d.nz,),
        smz_r=(d.nz,),
        ga_s=(d.nseq,),
        ga_r=(d.nseq,),
        gtx_s=(d.nx,),
        gtx_r=(d.nx,),
        gtz_s=(d.nz,),
        gtz_r=(d.nz,),
        sp_ss=(1,),
        sp_rs=(1,),
        pl_s=(2,),
        ow=(16,),
    )
    return outs, scratch, sems


def body(d, r):
    T, D, L, LP, F, FB, DC = d.T, d.D, d.L, d.LP, d.F, d.FB, d.DC
    B, G, HW, CB, nb = d.B, d.G, d.HW, d.CB, d.nb
    nseq, nz, nx, ny, nm = d.nseq, d.nz, d.nx, d.ny, d.nm
    s, m = lax.axis_index("seq"), lax.axis_index("mp")
    z, x = lax.div(s, nx), lax.rem(s, nx)
    y, c = lax.div(m, CORES), lax.rem(m, CORES)
    partner = (s, y * CORES + 1 - c)
    left_m, right_m = lax.rem(m + nm - 1, nm), lax.rem(m + 1, nm)
    pending = []

    def later(make, when=None):
        pending.append((make, when))

    def start(make, when=None):
        if when is None:
            make().start()
        else:
            pl.when(when())(lambda: make().start())
        pending.append((make, when))

    barrier = pltpu.get_barrier_semaphore()
    for k in range(1, nseq):
        pl.semaphore_signal(
            barrier, inc=1, device_id=(lax.rem(s + k, nseq), m), device_id_type=MESH
        )
    for k in range(1, nm):
        pl.semaphore_signal(barrier, inc=1, device_id=(s, lax.rem(m + k, nm)), device_id_type=MESH)

    def local(src, dst, i):
        copy = pltpu.make_async_copy(src, dst, r.ld.at[i])
        copy.start()
        return copy

    ld_x = local(r.x_in, r.x_v, 0)
    ld_cot = local(r.cot, r.cot_v, 8)

    half = nb * CB

    def psum_start(k, part):
        par = k % 2

        def send_half(j):
            r.csend[j] = part((1 - c) * half + j * CB)
            remote(r.csend.at[j], r.cland.at[j], r.c_s.at[k, j], r.c_r.at[k, j], partner).start()

        loop(nb, send_half)

        def own_half(j):
            v = part(c * half + j * CB)
            remote(
                r.csend.at[j], r.cland.at[j], r.c_s.at[k, j], r.c_r.at[k, j], partner
            ).wait_recv()
            r.yl[par, y, j] = (v + r.cland[j]).astype(BF16)
            for q in range(1, ny):
                to = lax.rem(y + q, ny)
                remote(
                    r.yl.at[par, y, j],
                    r.yl.at[par, y, j],
                    r.y_s.at[k, q, j],
                    r.y_r.at[k, q, j],
                    (s, to * CORES + c),
                ).start()

        loop(nb, own_half)

    def psum_finish(k):
        par = k % 2

        def total(j):
            for q in range(1, ny):
                src = lax.rem(y + ny - q, ny)
                remote(
                    r.yl.at[par, src, j],
                    r.yl.at[par, src, j],
                    r.y_s.at[k, q, j],
                    r.y_r.at[k, q, j],
                    partner,
                ).wait_recv()
            v = r.yl[par, 0, j].astype(F32)
            for q in range(1, ny):
                v = v + r.yl[par, q, j].astype(F32)
            at = c * nb + j
            r.tot[at] = v
            remote(r.tot.at[at], r.tot.at[at], r.a_s.at[k, j], r.a_r.at[k, j], partner).start()

        loop(nb, total)

        def close(j):
            at = (1 - c) * nb + j
            remote(
                r.tot.at[at], r.tot.at[at], r.a_s.at[k, j], r.a_r.at[k, j], partner
            ).wait()
            remote(
                r.csend.at[j], r.cland.at[j], r.c_s.at[k, j], r.c_r.at[k, j], partner
            ).wait_send()
            for q in range(1, ny):
                remote(
                    r.yl.at[par, y, j],
                    r.yl.at[par, y, j],
                    r.y_s.at[k, q, j],
                    r.y_r.at[k, q, j],
                    partner,
                ).wait_send()

        loop(nb, close)

    def pairs_send(k):
        for q in range(1, nseq):
            start(
                lambda q=q: remote(
                    r.pk.at[k],
                    r.pf.at[k, s],
                    r.pf_s.at[k, q],
                    r.pf_r.at[k, q],
                    (s + q if k == 0 else s - q, m),
                ),
                lambda q=q: s + q < nseq if k == 0 else s - q >= 0,
            )

    def pairs_enter(k, reverse):
        for q in range(1, nseq):
            src = s + q if reverse else s - q

            @pl.when(src < nseq if reverse else src >= 0)
            def _(q=q, src=src):
                remote(
                    r.pk.at[k], r.pf.at[k, src], r.pf_s.at[k, q], r.pf_r.at[k, q], partner
                ).wait_recv()

        value = jnp.zeros((B, L), F32)
        for q in range(nseq - 1):
            at = nseq - 1 - q if reverse else q
            pair = r.pf[k, at]
            new = pair[0:B] * value + pair[B : 2 * B]
            value = jnp.where(at > s if reverse else at < s, new, value)
        return value

    def transposed(src, dst):
        def one(j):
            dst[lax.div(j, nx), lax.rem(j, nx)] = src[:, pl.ds(pl.multiple_of(j * DC, DC), DC)].T

        loop(nseq, one)

    def lanes(i):
        return pl.ds(pl.multiple_of(i * T, T), T)

    ez_half, ex_half = DC // CORES, nz // CORES

    def ez_part(e, src_z, core):
        rows = pl.ds(pl.multiple_of(core * ez_half, ez_half), ez_half)
        return r.ez.at[e, :, rows, lanes(src_z)]

    def ez_own(e):
        src = r.nmT if e else r.cotT
        return pltpu.make_async_copy(src.at[z], r.ez.at[e, :, :, lanes(z)], r.own_l.at[e])

    def ez_copy(e, k):
        to = lax.rem(z + k, nz)
        rows = pl.ds(pl.multiple_of(c * ez_half, ez_half), ez_half)
        return remote(
            (r.nmT if e else r.cotT).at[to, :, rows],
            ez_part(e, z, c),
            r.ez_s.at[e, k],
            r.ez_r.at[e, k],
            (to * nx + x, m),
        )

    def ez_relay_copy(e, k):
        part = ez_part(e, lax.rem(z + nz - k, nz), c)
        return remote(part, part, r.ezc_s.at[e, k], r.ezc_r.at[e, k], partner)

    def ez_send(e):
        ez_own(e).start()
        for k in range(1, nz):
            start(functools.partial(ez_copy, e, k))

    def ez_relay(e):
        for k in range(1, nz):
            part = ez_part(e, lax.rem(z + nz - k, nz), c)
            remote(part, part, r.ez_s.at[e, k], r.ez_r.at[e, k], partner).wait_recv()
            start(functools.partial(ez_relay_copy, e, k))

    def ez_wait(e):
        ez_own(e).wait()
        for k in range(1, nz):
            part = ez_part(e, lax.rem(z + nz - k, nz), 1 - c)
            remote(part, part, r.ezc_s.at[e, k], r.ezc_r.at[e, k], partner).wait_recv()

    def ex_part(e, src_x, core):
        return r.ex.at[e, pl.ds(core * ex_half, ex_half), :, lanes(src_x)]

    def ex_own(e):
        src = r.gbT if e else r.nfT
        return pltpu.make_async_copy(src.at[:, x], r.ex.at[e, :, :, lanes(x)], r.own_l.at[2 + e])

    def ex_copy(e, k):
        to = lax.rem(x + k, nx)
        return remote(
            (r.gbT if e else r.nfT).at[pl.ds(c * ex_half, ex_half), to],
            ex_part(e, x, c),
            r.ex_xs.at[e, k],
            r.ex_xr.at[e, k],
            (z * nx + to, m),
        )

    def ex_relay_copy(e, k):
        part = ex_part(e, lax.rem(x + nx - k, nx), c)
        return remote(part, part, r.exc_s.at[e, k], r.exc_r.at[e, k], partner)

    def ex_send(e):
        ex_own(e).start()
        for k in range(1, nx):
            start(functools.partial(ex_copy, e, k))

    def ex_relay(e):
        for k in range(1, nx):
            part = ex_part(e, lax.rem(x + nx - k, nx), c)
            remote(part, part, r.ex_xs.at[e, k], r.ex_xr.at[e, k], partner).wait_recv()
            start(functools.partial(ex_relay_copy, e, k))

    def ex_wait(e):
        ex_own(e).wait()
        for k in range(1, nx):
            part = ex_part(e, lax.rem(x + nx - k, nx), 1 - c)
            remote(part, part, r.exc_s.at[e, k], r.exc_r.at[e, k], partner).wait_recv()

    def q_own(qb):
        return r.hd.at[qb] if qb < 3 else (r.gpg if qb == 3 else r.gpr)

    def q_land(qb, zo):
        return r.hz_d.at[qb, zo] if qb < 3 else r.hz_r.at[qb - 3, zo]

    def q_copy(qb, src, zo, way):
        to = s + nx if way == 0 else s - nx
        return remote(src, q_land(qb, zo), r.hz_s.at[qb, zo, way], r.hz_rs.at[qb, zo], (to, m))

    def q_send(qb):
        start(lambda: q_copy(qb, q_own(qb), z, 0), lambda: z < nz - 1)
        start(lambda: q_copy(qb, q_own(qb), z, 1), lambda: z > 0)

    def hx_ref(pb):
        return r.gp.at[pb] if pb < 6 else r.mx

    def hx_send(pb):
        def copy(k):
            to = lax.rem(x + k, nx)
            return remote(
                hx_ref(pb).at[x],
                hx_ref(pb).at[x],
                r.hx_s.at[pb, k],
                r.hx_r.at[pb, k],
                (z * nx + to, m),
            )

        for k in range(1, nx):
            start(functools.partial(copy, k))

    def hx_wait(pb):
        for k in range(1, nx):
            src = lax.rem(x + nx - k, nx)
            remote(
                hx_ref(pb).at[src],
                hx_ref(pb).at[src],
                r.hx_s.at[pb, k],
                r.hx_r.at[pb, k],
                partner,
            ).wait_recv()

    r.vecs[0 : d.taps] = r.conv_weight[...]
    for row, vector in enumerate((r.conv_bias, r.bias_a, r.bias_x, r.log_rate)):
        r.vecs[d.taps + row : d.taps + row + 1] = vector[...].reshape(1, L)
    r.gains[0:1] = r.gain_mix[...].reshape(1, D)
    r.gains[1:2] = r.gain_ffn[...].reshape(1, D)
    own_ids = r.ids[:, pl.ds(pl.multiple_of(s * G, G), G)]
    before = r.ids[:, pl.ds(pl.multiple_of(jnp.maximum(s - 1, 0) * G, G), G)]
    r.idp[...] = jnp.zeros((8, 2 * G), jnp.int32)
    r.idp[0:B, 0:G] = jnp.where(s > 0, before, -1)
    r.idp[0:B, G : 2 * G] = own_ids
    both = r.idp[...]
    square_row = lax.broadcasted_iota(jnp.int32, (G, G), 0)
    same = [
        jnp.where(pltpu.roll(both, k, 1)[:, G:] == both[:, G:], 1.0, 0.0) for k in range(1, d.taps)
    ]
    for b in range(B):
        square = jnp.zeros((G, G), F32)
        for k in range(1, d.taps):
            square = jnp.where(
                square_row == k, jnp.broadcast_to(same[k - 1][b : b + 1], (G, G)), square
            )
        r.mk[b, 0:G, :] = square.T
        r.mk[b, G : G + 8, :] = jnp.zeros((8, 128), F32)
    rates = r.vecs[7:8]
    r.rv[0:1] = -RATE_SCALE * softplus_small(rates)
    r.rv[1:2] = -RATE_SCALE * jax.nn.sigmoid(rates)
    r.sacc[...] = jnp.zeros((8, 8, L), F32)

    base = L * m + HW // 4
    shift = HW.bit_length() - 1
    turn = lax.rem(base, HW)
    turn_right = lax.rem(base + L, HW)

    def head_mask(first, count):
        row = lax.broadcasted_iota(jnp.int32, (count, L), 0) + first
        col = lax.broadcasted_iota(jnp.int32, (count, L), 1) + base
        return lax.shift_right_arithmetic(row, shift) == lax.shift_right_arithmetic(col, shift)

    pieces = [(p, min(HW, LP - p)) for p in range(0, LP, HW)]

    def recurrent_forward(wrec_v, wgel_v, wout_v, nm_v, nmh, pa, px, g2):
        ld_gel = local(r.w_gel, wgel_v, 1)
        ld_rec = local(r.w_rec, wrec_v, 2)
        ld_g = [
            local(gate, g2.at[i, pl.ds(at * HW, HW)], 3 + 2 * i + at)
            for i, gate in enumerate((r.gate_a, r.gate_x))
            for at in range(2)
        ]
        ld_out = local(r.w_out, wout_v, 7)
        ld_x.wait()

        def norm(i):
            at = rows16(i)
            v = r.x_v[at, :].astype(F32)
            scale = lax.rsqrt(jnp.mean(v * v, axis=1, keepdims=True) + EPS)
            nm_v[at, :] = (v * scale * r.gains[0:1]).astype(BF16)
            r.scm[at, :] = jnp.broadcast_to(scale, (16, 128))

        loop(T // 16, norm)
        ld_gel.wait()
        r.pre_gel[...] = dot(nm_v[...], wgel_v[...])
        ld_rec.wait()
        main = dot(nm_v[...], wrec_v[...]).astype(BF16).astype(F32)
        for b in range(B):
            r.extp[b, 16 : 16 + G, :] = main[b * G : (b + 1) * G]

        ld_cot.wait()
        transposed(r.cot_v, r.cotT)
        pl.semaphore_wait(barrier, nseq - 1 + nm - 1)

        for b in range(B):
            start(
                lambda b=b: remote(
                    r.x_in.at[pl.ds(b * G + G - 16, 16)],
                    r.xh.at[pl.ds(b * 16, 16)],
                    r.halo_s.at[b],
                    r.halo_r.at[b],
                    (s + 1, m),
                ),
                lambda: s < nseq - 1,
            )

        ez_send(0)

        @pl.when(s > 0)
        def _():
            for b in range(B):
                remote(
                    r.x_in.at[pl.ds(b * G + G - 16, 16)],
                    r.xh.at[pl.ds(b * 16, 16)],
                    r.halo_s.at[b],
                    r.halo_r.at[b],
                    partner,
                ).wait_recv()

        @pl.when(s == 0)
        def _():
            r.xh[...] = jnp.zeros((B * 16, D), BF16)

        for b in range(B):
            v = r.xh[b * 16 : (b + 1) * 16, :].astype(F32)
            scale = lax.rsqrt(jnp.mean(v * v, axis=1, keepdims=True) + EPS)
            nmh[b * 16 : (b + 1) * 16, :] = (v * scale * r.gains[0:1]).astype(BF16)
        rim = dot(nmh[...], wrec_v[...]).astype(BF16).astype(F32)
        for b in range(B):
            r.extp[b, 0:16, :] = rim[b * 16 : (b + 1) * 16]

        if LP > L:
            for wide in (r.cv, r.gpg, r.gpr, r.mx.at[x]):
                wide[:, L:] = jnp.zeros((T, LP - L), BF16)

        def conv(i):
            for b in range(B):
                window = r.extp[b, pl.ds(pl.multiple_of(i * 16 + 8, 8), 24), :]
                keep = r.mk[b, rows16(i), :]
                acc = r.vecs[4:5] + r.vecs[0:1] * window[8:24]
                for k in range(1, d.taps):
                    acc = acc + r.vecs[k : k + 1] * (keep[:, k : k + 1] * window[8 - k : 24 - k])
                at = rows16(i, b * G)
                r.cv[at, 0:L] = acc.astype(BF16)
                r.st_l[at, :] = acc[:, :HW].astype(BF16)
                r.st_r[at, :] = acc[:, L - HW :].astype(BF16)

        loop(G // 16, conv)
        def to_left():
            return remote(r.st_l, r.hr, r.ex_s.at[0], r.ex_r.at[0], (s, left_m))

        def to_right():
            return remote(r.st_r, r.hl, r.ex_s.at[1], r.ex_r.at[1], (s, right_m))

        start(to_left)
        start(to_right)

        for copy in ld_g:
            copy.wait()
        for i in range(2):
            table = g2[i, pl.ds(pl.multiple_of(turn, HW // 4), HW), :].astype(F32)
            table_right = g2[i, pl.ds(pl.multiple_of(turn_right, HW // 4), HW), :].astype(F32)
            r.wl[i] = jnp.where(head_mask(base - HW, HW), table, 0.0).astype(BF16)
            r.wr[i] = jnp.where(head_mask(base + L, HW), table_right, 0.0).astype(BF16)
            for p, n in pieces:
                r.wo[i, p : p + n, :] = jnp.where(head_mask(base + p, n), table[:n], 0.0).astype(
                    BF16
                )
        pa[...] = dot(r.cv[...], r.wo[0]) + r.vecs[5:6]
        px[...] = dot(r.cv[...], r.wo[1]) + r.vecs[6:7]
        to_left().wait_recv()
        to_right().wait_recv()
        pa[...] += dot(r.hl[...], r.wl[0]) + dot(r.hr[...], r.wr[0])
        px[...] += dot(r.hl[...], r.wl[1]) + dot(r.hr[...], r.wr[1])

        def scan(i, carry):
            out = []
            for b in range(B):
                decay_in, state_in = carry[2 * b], carry[2 * b + 1]
                at = rows16(i, b * G)
                recur = jax.nn.sigmoid(pa[at, :])
                inject = jax.nn.sigmoid(px[at, :])
                log_decay = r.rv[0:1] * recur
                decay = jnp.exp(log_decay)
                spread = jnp.sqrt(minus_expm1(2.0 * log_decay))
                drive = spread * inject * r.cv[at, 0:L].astype(F32)
                coeff = decay * r.mk[b, rows16(i), :][:, 1:2]
                r.recur[at, :] = recur
                r.inj[at, :] = inject
                r.cfp[b, rows16(i), :] = coeff
                for h in range(2):
                    a, v = scan_tile(
                        coeff[8 * h : 8 * h + 8], drive[8 * h : 8 * h + 8], reverse=False
                    )
                    v = v + a * state_in
                    a = a * decay_in
                    decay_in, state_in = a[7:8], v[7:8]
                    r.aloc[pl.ds(pl.multiple_of(b * G + i * 16 + 8 * h, 8), 8), :] = a
                    r.stp[b, pl.ds(pl.multiple_of(8 + i * 16 + 8 * h, 8), 8), :] = v
                out += [decay_in, state_in]
            return tuple(out)

        one, zero = jnp.ones((1, L), F32), jnp.zeros((1, L), F32)
        ends = lax.fori_loop(0, G // 16, scan, (one, zero) * B)
        r.pk[0] = jnp.zeros((8, L), F32)
        for b in range(B):
            r.pk[0, b : b + 1, :] = ends[2 * b]
            r.pk[0, B + b : B + b + 1, :] = ends[2 * b + 1]
            r.cfp[b, G : G + 8, :] = jnp.ones((8, L), F32)
        pairs_send(0)
        transposed(nm_v, r.nmT)
        ez_send(1)
        entered = pairs_enter(0, False)
        for b in range(B):
            r.stp[b, 0:8, :] = jnp.broadcast_to(entered[b : b + 1], (8, L))

        def states(i):
            for b in range(B):
                at = rows16(i, b * G)
                here = pl.ds(pl.multiple_of(8 + i * 16, 8), 16)
                state = r.stp[b, here, :] + r.aloc[at, :] * r.stp[b, 7:8, :]
                r.stp[b, here, :] = state
                r.mx[x, at, 0:L] = (state * gelu_tanh(r.pre_gel[at, :])).astype(BF16)

        loop(G // 16, states)
        ld_out.wait()
        psum_start(
            0,
            lambda col: dot(r.mx[x, :, 0:L], wout_v[:, pl.ds(pl.multiple_of(col, CB), CB)]),
        )
        hx_send(6)

    pl.run_scoped(
        recurrent_forward,
        pltpu.VMEM((D, L), BF16),
        pltpu.VMEM((D, L), BF16),
        pltpu.VMEM((L, D), BF16),
        pltpu.VMEM((T, D), BF16),
        pltpu.VMEM((B * 16, D), BF16),
        pltpu.VMEM((T, L), F32),
        pltpu.VMEM((T, L), F32),
        pltpu.VMEM((2, 2 * HW, L), BF16),
    )

    def feed_forward(wd_v, wg_v, wu_v, nf, gh, pg, pu):
        ld_d = [local(r.w_down.at[pl.ds(i * FB, FB)], wd_v.at[i], i) for i in range(3)]
        ld_g = [local(r.w_gate.at[:, pl.ds(i * FB, FB)], wg_v.at[i], 3 + i) for i in range(3)]
        ld_u = [local(r.w_up.at[:, pl.ds(i * FB, FB)], wu_v.at[i], 6 + i) for i in range(3)]
        for i in range(3):
            ld_d[i].wait()

        def hidden_grad(i):
            gh[i] = dot_nt(r.cot_v[...], wd_v[i])

        loop(3, hidden_grad)
        ez_relay(0)
        ez_relay(1)
        psum_finish(0)

        def residual(i):
            at = rows16(i)
            parts = [
                r.tot[j, at, :] + r.x_v[at, j * CB : (j + 1) * CB].astype(F32)
                for j in range(2 * nb)
            ]
            square = parts[0] * parts[0]
            for v in parts[1:]:
                square = square + v * v
            scale = lax.rsqrt(jnp.sum(square, axis=1, keepdims=True) / D + EPS)
            for j, v in enumerate(parts):
                cols = slice(j * CB, (j + 1) * CB)
                r.resid[at, cols] = v
                nf[at, cols] = (v * scale * r.gains[1:2, cols]).astype(BF16)
            r.scf[at, :] = jnp.broadcast_to(scale, (16, 128))

        loop(T // 16, residual)
        for i in range(3):
            ld_g[i].wait()
            ld_u[i].wait()

        for i in range(3):
            pg[...] = dot(nf[...], wg_v[i])
            pu[...] = dot(nf[...], wu_v[i])

            def units(t, i=i):
                at = rows16(t)
                up, back = pu[at, :], gh[i, at, :]
                active, slope = gelu_and_slope(pg[at, :])
                r.hd[i, at, :] = (active * up).astype(BF16)
                r.gp[2 * i, x, at, :] = (back * up * slope).astype(BF16)
                r.gp[2 * i + 1, x, at, :] = (back * active).astype(BF16)

            loop(T // 16, units)
            q_send(i)
            if i == 0:
                transposed(nf, r.nfT)
                ex_send(0)
            hx_send(2 * i)
            hx_send(2 * i + 1)

        def back_input(col):
            at = pl.ds(pl.multiple_of(col, CB), CB)
            v = dot_nt(r.gp[0, x], wg_v[0, at, :]) + dot_nt(r.gp[1, x], wu_v[0, at, :])
            for i in range(1, 3):
                v = v + dot_nt(r.gp[2 * i, x], wg_v[i, at, :])
                v = v + dot_nt(r.gp[2 * i + 1, x], wu_v[i, at, :])
            return v

        psum_start(1, back_input)

        def ffn_term(j):
            at = pl.ds(pl.multiple_of(j * CB, CB), CB)
            v = dot(r.hd[0], wd_v[0, :, at])
            for i in range(1, 3):
                v = v + dot(r.hd[i], wd_v[i, :, at])
            r.fo[j] = v.astype(BF16)

        loop(2 * nb, ffn_term)
        ex_relay(0)

    pl.run_scoped(
        feed_forward,
        pltpu.VMEM((3, FB, D), BF16),
        pltpu.VMEM((3, D, FB), BF16),
        pltpu.VMEM((3, D, FB), BF16),
        pltpu.VMEM((T, D), BF16),
        pltpu.VMEM((3, T, FB), F32),
        pltpu.VMEM((T, FB), F32),
        pltpu.VMEM((T, FB), F32),
    )

    def gain_rows(which):
        total = jnp.sum(r.gacc[...], axis=0, keepdims=True)
        for q in range(nseq):
            r.gsend[q, which : which + 1, :] = total[:, q * DC : (q + 1) * DC]

    def after_feed_forward(stage_f, load_f, own_st, hload, qstage):
        tail = []
        seen = [dict() for _ in range(nz)]

        def once(zz, *what):
            first = what not in seen[zz]
            seen[zz][what] = True
            return first

        def at_end(zz, make):
            seen[zz].setdefault("sent", []).append(make)

        def sized(ref, n):
            return ref if n == ref.shape[-1] else ref.at[:, pl.ds(0, n)]

        def own_write(zz, src, ref):
            turn_ = seen[zz].get("turn", 0)
            seen[zz]["turn"] = turn_ + 1
            at, n = turn_ % 2, src.shape[-1]

            def copy():
                return pltpu.make_async_copy(sized(own_st.at[at], n), ref(), r.ow.at[4 + at])

            held = seen[zz].setdefault("held", {})
            if at in held:
                held[at]().wait()
            sized(own_st.at[at], n)[...] = src.astype(BF16)
            copy().start()
            held[at] = copy

        def p_width(b):
            return FB if b < 6 else LP

        def p_stage(b, zc):
            return stage_f.at[b % 2, zc] if b < 6 else tail[0].at[zc]

        def p_land(b, place):
            return r.land_f.at[b, place] if b < 6 else r.land_o.at[place]

        def p_part(zz, b, zc):
            if once(zz, "hx", b):
                hx_wait(b)
            e = 0 if b < 6 else 1
            if once(zz, "ex", e):
                ex_wait(e)
            return dot(r.ex[e, zc], hx_ref(b)[...].reshape(nx * T, p_width(b)))

        def p_copy(b, zc, place, to):
            return remote(
                p_stage(b, zc), p_land(b, place), r.p_s.at[b, zc], r.p_r.at[b, place], (to, m)
            )

        def do_p(zz, b, way, zc):
            right = way > 0
            has_input = zz > 0 if right else zz < nz - 1
            place = abs(zc - zz) + (0 if right else nz - 1)
            load = load_f if b < 6 else tail[1]
            if has_input:
                fetch = pltpu.make_async_copy(p_land(b, place), load, r.pl_s.at[0])
                p_copy(b, zc, place, s).wait_recv()
                fetch.start()
            v = p_part(zz, b, zc)
            if has_input:
                fetch.wait()
                v = v + load[...].astype(F32)
            if 2 <= b < 6:
                p_copy(b - 2, zc, 0, s).wait_send()
            p_stage(b, zc)[...] = v.astype(BF16)
            p_copy(b, zc, place - 1, s + nx if right else s - nx).start()
            if b >= 4:
                at_end(zz, lambda: p_copy(b, zc, 0, s).wait_send())

        def do_own(zz, b):
            own_write(zz, p_part(zz, b, zz), lambda: r.own_f.at[b] if b < 6 else r.own_o)

        def q_arrived(zz, qb, zo):
            if once(zz, "hz", qb, zo):
                q_copy(qb, q_land(qb, zo), zo, 0 if zo < zz else 1).wait_recv()

        def do_forward(zz, qb, zo):
            q_arrived(zz, qb, zo)
            way, to = (0, zz + 1) if zo < zz else (1, zz - 1)
            if 0 <= to < nz:
                q_copy(qb, q_land(qb, zo), zo, way).start()
                at_end(zz, lambda: q_copy(qb, q_land(qb, zo), zo, way).wait_send())

        def q_exchange(qb, k, n):
            to = lax.rem(x + k, nx)
            land = r.xr_d.at[qb, nx - k - 1] if qb < 3 else r.xr_r.at[qb - 3, nx - k - 1]
            return remote(
                sized(qstage.at[qb % 2, k - 1], n),
                land,
                r.xr_s.at[qb, k],
                r.xr_rs.at[qb, k],
                (z * nx + to, m),
            )

        def do_q(zz, qb):
            e, n, own = (0, FB, q_own(qb)) if qb < 3 else (1, LP, q_own(qb))

            def piece(zo):
                return hload.at[zo] if n == d.W else hload.at[zo, :, pl.ds(0, n)]

            def fetch(zo):
                src = own if zo == zz else q_land(qb, zo)
                return pltpu.make_async_copy(src, piece(zo), r.ow.at[8 + zo])

            for zo in range(nz):
                if zo != zz:
                    q_arrived(zz, qb, zo)
                fetch(zo).start()
            if once(zz, "ez", e):
                ez_wait(e)
            if qb >= 2:
                for k in range(1, nx):
                    q_exchange(qb - 2, k, FB).wait_send()
            for zo in range(nz):
                fetch(zo).wait()
            gathered = hload[:, :, 0:n].reshape(nz * T, n)
            for k in range(1, nx):
                v = dot(r.ez[e, lax.rem(x + k, nx)], gathered)
                sized(qstage.at[qb % 2, k - 1], n)[...] = v.astype(BF16)
                q_exchange(qb, k, n).start()
            if qb >= 3:
                at_end(zz, lambda: [q_exchange(qb, k, n).wait_send() for k in range(1, nx)])
            own_write(
                zz,
                dot(r.ez[e, x], gathered),
                lambda: r.own_d.at[qb] if qb < 3 else r.own_r.at[qb - 3],
            )

        def work(point):
            for zz in range(nz):

                @pl.when(z == zz)
                def _(zz=zz):
                    for op in SCHEDULE[point][zz]:
                        kind, rest = op[0], op[1:]
                        {"F": do_forward, "P": do_p, "O": do_own, "Q": do_q}[kind](zz, *rest)

        def close():
            for zz in range(nz):

                @pl.when(z == zz)
                def _(zz=zz):
                    for copy in seen[zz].get("held", {}).values():
                        copy().wait()
                    for make in seen[zz].get("sent", []):
                        make()
                    for b in range(7):
                        for place, there in ((0, zz > 0), (nz - 1, zz < nz - 1)):
                            if there:
                                p_copy(b, 0, place, s).wait_recv()
                    for qb in range(5):
                        for k in range(1, nx):
                            q_exchange(qb, k, FB if qb < 3 else LP).wait_recv()

        def recurrent_backward(
            w_v, wout_v, gr, gb, gm, gcd, gcp, gmel, gpa, gpx, adj, t2
        ):
            ld_gel = local(r.w_gel, w_v, 2)
            ld_out = local(r.w_out, wout_v, 3)
            r.gsend[...] = jnp.zeros((nseq, 8, DC), F32)
            work(1)
            psum_finish(1)
            r.gacc[...] = jnp.zeros((16, D), F32)

            def norm_back(i):
                at = rows16(i)
                scale = r.scf[at, :][:, 0:1]
                inner = jnp.zeros((16, CB), F32)
                for j in range(2 * nb):
                    cols = slice(j * CB, (j + 1) * CB)
                    inner = inner + r.tot[j, at, :] * r.gains[1:2, cols] * r.resid[at, cols]
                factor = (scale * scale * scale) * (jnp.sum(inner, axis=1, keepdims=True) / D)
                for j in range(2 * nb):
                    cols = slice(j * CB, (j + 1) * CB)
                    n, v = r.tot[j, at, :], r.resid[at, cols]
                    r.gacc[:, cols] += n * v * scale
                    grad = r.cot_v[at, cols].astype(F32) + (
                        scale * (n * r.gains[1:2, cols]) - v * factor
                    )
                    gr[at, cols] = grad
                    gb[at, cols] = grad.astype(BF16)

            loop(T // 16, norm_back)
            gain_rows(1)
            ld_out.wait()
            gm[...] = dot_nt(gb[...], wout_v[...])

            def scan(t, carry):
                i = G // 16 - 1 - t
                out = []
                for b in range(B):
                    decay_in, value_in = carry[2 * b], carry[2 * b + 1]
                    at = rows16(i, b * G)
                    gate, slope = gelu_and_slope(r.pre_gel[at, :])
                    g = gm[at, :]
                    state = r.stp[b, pl.ds(pl.multiple_of(8 + i * 16, 8), 16), :]
                    r.gpg[at, 0:L] = (g * state * slope).astype(BF16)
                    value16 = g * gate
                    following = r.cfp[b, pl.ds(pl.multiple_of(i * 16, 16), 24), :][1:17]
                    for h in (1, 0):
                        a, v = scan_tile(
                            following[8 * h : 8 * h + 8], value16[8 * h : 8 * h + 8], reverse=True
                        )
                        v = v + a * value_in
                        a = a * decay_in
                        decay_in, value_in = a[0:1], v[0:1]
                        here = pl.ds(pl.multiple_of(b * G + i * 16 + 8 * h, 8), 8)
                        r.aloc[here, :] = a
                        adj[here, :] = v
                    out += [decay_in, value_in]
                return tuple(out)

            one, zero = jnp.ones((1, L), F32), jnp.zeros((1, L), F32)
            ends = lax.fori_loop(0, G // 16, scan, (one, zero) * B)
            r.pk[1] = jnp.zeros((8, L), F32)
            for b in range(B):
                first = r.cfp[b, 0:1, :]
                r.pk[1, b : b + 1, :] = first * ends[2 * b]
                r.pk[1, B + b : B + b + 1, :] = first * ends[2 * b + 1]
            pairs_send(1)
            q_send(3)
            ld_gel.wait()

            def gel_term(j):
                at = pl.ds(pl.multiple_of(j * CB, CB), CB)
                gmel[j] = dot_nt(r.gpg[:, 0:L], w_v[at, :])

            loop(2 * nb, gel_term)
            ld_rec = local(r.w_rec, w_v, 1)
            transposed(gb, r.gbT)
            ex_send(1)
            work(2)
            outer = pairs_enter(1, True)

            def gate_back(i):
                for b in range(B):
                    at = rows16(i, b * G)
                    adjoint = adj[at, :] + r.aloc[at, :] * outer[b : b + 1]
                    recur, inject = r.recur[at, :], r.inj[at, :]
                    log_decay = r.rv[0:1] * recur
                    decay = jnp.exp(log_decay)
                    value = r.cv[at, 0:L].astype(F32)
                    spread = jnp.sqrt(minus_expm1(2.0 * log_decay))
                    prior = r.stp[b, pl.ds(pl.multiple_of(i * 16, 16), 24), :][7:23]
                    keep = r.mk[b, rows16(i), :][:, 1:2]
                    grad_log = (
                        adjoint * inject * value * (-(decay * decay) / spread)
                        + adjoint * prior * keep * decay
                    )
                    ga = (grad_log * r.rv[0:1] * recur * (1.0 - recur)).astype(BF16)
                    direct = adjoint * spread * inject
                    gx = (adjoint * spread * value * inject * (1.0 - inject)).astype(BF16)
                    gpa[at, :] = ga
                    gpx[at, :] = gx
                    gcd[at, :] = direct
                    r.sacc[5] += fold8(ga.astype(F32))
                    r.sacc[6] += fold8(gx.astype(F32))
                    r.sacc[7] += fold8(grad_log * recur)

            loop(G // 16, gate_back)
            r.gs_l[...] = (dot_nt(gpa[...], r.wl[0]) + dot_nt(gpx[...], r.wl[1])).astype(BF16)

            def to_left():
                return remote(r.gs_l, r.gi_r, r.gi_s.at[0], r.gi_rs.at[0], (s, left_m))

            start(to_left)
            r.gs_r[...] = (dot_nt(gpa[...], r.wr[0]) + dot_nt(gpx[...], r.wr[1])).astype(BF16)

            def to_right():
                return remote(r.gs_r, r.gi_l, r.gi_s.at[1], r.gi_rs.at[1], (s, right_m))

            start(to_right)
            own = dot_nt(gpa[...], r.wo[0]) + dot_nt(gpx[...], r.wo[1])
            gcd[...] += own[:, 0:L]

            for i, grad in enumerate((gpa, gpx)):
                turned = jnp.where(head_mask(base - HW, HW), dot(r.hl[...].T, grad[...]), 0.0)
                t2[0:HW, :] = turned
                for p, n in pieces:
                    part = dot(r.cv[:, p : p + n].T, grad[...])
                    t2[0:n, :] += jnp.where(head_mask(base + p, n), part, 0.0)
                t2[HW : 2 * HW, :] = t2[0:HW, :]
                back = pl.multiple_of(lax.rem(HW - turn, HW), HW // 4)
                table = t2[pl.ds(back, HW), :]
                right = jnp.where(head_mask(base + L, HW), dot(r.hr[...].T, grad[...]), 0.0)
                t2[0:HW, :] = right
                t2[HW : 2 * HW, :] = right
                back = pl.multiple_of(lax.rem(HW - turn_right, HW), HW // 4)
                table = (table + t2[pl.ds(back, HW), :]).astype(BF16)
                for q in range(nseq):
                    r.gt[q // nx, q % nx, i] = table[q * d.GR : (q + 1) * d.GR]

            ex_relay(1)
            work(3)
            to_left().wait_recv()
            to_right().wait_recv()
            gcd[:, 0:HW] += r.gi_l[...].astype(F32)
            gcd[:, L - HW : L] += r.gi_r[...].astype(F32)
            for b in range(B):
                gcp[b, 0:G, :] = gcd[b * G : (b + 1) * G, :]
                gcp[b, G : G + 8, :] = jnp.zeros((8, L), F32)

            for b in range(B):
                top, keep = gcp[b, 0:8, :], r.mk[b, 0:8, :]
                spill = jnp.zeros((8, L), F32)
                row = lax.broadcasted_iota(jnp.int32, (8, L), 0)
                for k in range(1, d.taps):
                    moved = pltpu.roll(r.vecs[k : k + 1] * (keep[:, k : k + 1] * top), 8 - k, 0)
                    spill = spill + jnp.where(row >= 8 - k, moved, 0.0)
                r.sp_s[b * 8 : (b + 1) * 8, :] = spill

            def spilled():
                return remote(r.sp_s, r.sp_r, r.sp_ss.at[0], r.sp_rs.at[0], (s - 1, m))

            start(spilled, lambda: s > 0)

            @pl.when(s == nseq - 1)
            def _():
                r.sp_r[...] = jnp.zeros((B * 8, L), F32)

            def conv_back(i, spill):
                for b in range(B):
                    grads = gcp[b, pl.ds(pl.multiple_of(i * 16, 16), 24), :]
                    keep = r.mk[b, pl.ds(pl.multiple_of(i * 16, 16), 24), :]
                    window = r.extp[b, pl.ds(pl.multiple_of(i * 16 + 8, 8), 24), :]
                    here = grads[0:16]
                    out = r.vecs[0:1] * here
                    if not spill:
                        r.sacc[4] += fold8(here)
                        r.sacc[0] += fold8(here * window[8:24])
                    for k in range(1, d.taps):
                        masked = keep[:, k : k + 1] * grads
                        out = out + r.vecs[k : k + 1] * masked[k : k + 16]
                        if not spill:
                            r.sacc[k] += fold8(masked[0:16] * window[8 - k : 24 - k])
                    if spill:
                        extra = r.sp_r[b * 8 : (b + 1) * 8, :]
                        out = out + jnp.concatenate([jnp.zeros((8, L), F32), extra], axis=0)
                    r.gpr[rows16(i, b * G), 0:L] = out.astype(BF16)

            loop(G // 16, lambda i: conv_back(i, False))
            for k in range(8):
                r.smv[k : k + 1, :] = jnp.sum(r.sacc[k], axis=0, keepdims=True)

            work(4)

            @pl.when(s < nseq - 1)
            def _():
                spilled().wait_recv()

            conv_back(G // 16 - 1, True)
            q_send(4)
            ld_rec.wait()

            def mix_term(col):
                at = pl.ds(pl.multiple_of(col, CB), CB)
                return dot_nt(r.gpr[:, 0:L], w_v[at, :]) + gmel[lax.div(col, CB)]

            psum_start(2, mix_term)

            def small_x(k):
                to = lax.rem(x + k, nx)
                return remote(
                    r.smv, r.smx.at[x], r.smx_s.at[k], r.smx_r.at[k], (z * nx + to, m)
                )

            def gates_x(k):
                to = lax.rem(x + k, nx)
                return remote(
                    r.gt.at[:, to], r.gtx.at[x], r.gtx_s.at[k], r.gtx_r.at[k], (z * nx + to, m)
                )

            def small_z(k):
                to = lax.rem(z + k, nz)
                return remote(
                    r.smv, r.smz.at[z], r.smz_s.at[k], r.smz_r.at[k], (to * nx + x, m)
                )

            def gates_z(k):
                to = lax.rem(z + k, nz)
                return remote(
                    r.gts.at[to], r.gtz.at[z], r.gtz_s.at[k], r.gtz_r.at[k], (to * nx + x, m)
                )

            def gain_copy(q):
                to = lax.rem(s + q, nseq)
                return remote(r.gsend.at[to], r.gland.at[s], r.ga_s.at[q], r.ga_r.at[q], (to, m))

            for k in range(1, nx):
                small_x(k).start()
                gates_x(k).start()
            work(5)
            psum_finish(2)

            r.gacc[...] = jnp.zeros((16, D), F32)

            def norm_back_mix(i):
                at = rows16(i)
                scale = r.scm[at, :][:, 0:1]
                inner = jnp.zeros((16, CB), F32)
                for j in range(2 * nb):
                    cols = slice(j * CB, (j + 1) * CB)
                    v = r.x_v[at, cols].astype(F32)
                    inner = inner + r.tot[j, at, :] * r.gains[0:1, cols] * v
                factor = (scale * scale * scale) * (jnp.sum(inner, axis=1, keepdims=True) / D)
                for j in range(2 * nb):
                    cols = slice(j * CB, (j + 1) * CB)
                    n, v = r.tot[j, at, :], r.x_v[at, cols].astype(F32)
                    r.gacc[:, cols] += n * v * scale
                    gr[at, cols] = gr[at, cols] + (scale * (n * r.gains[0:1, cols]) - v * factor)

            loop(T // 16, norm_back_mix)
            out_gin = pltpu.make_async_copy(gr, r.k_gin, r.ow.at[0])
            out_gin.start()
            gain_rows(0)
            for q in range(1, nseq):
                start(functools.partial(gain_copy, q))

            psum_start(3, lambda col: r.fo[lax.div(col, CB)].astype(F32))
            small, gates = r.smv[...], r.gt[:, x].astype(F32)
            for k in range(1, nx):
                src = lax.rem(x + nx - k, nx)
                remote(r.smv, r.smx.at[src], r.smx_s.at[k], r.smx_r.at[k], partner).wait_recv()
                remote(r.gt.at[:, x], r.gtx.at[src], r.gtx_s.at[k], r.gtx_r.at[k], partner).wait()
                small_x(k).wait_send()
            for k in range(1, nx):
                src = lax.rem(x + nx - k, nx)
                small = small + r.smx[src]
                gates = gates + r.gtx[src].astype(F32)
            r.smv[...] = small
            r.gts[...] = gates.astype(BF16)
            for k in range(1, nz):
                start(functools.partial(small_z, k))
                start(functools.partial(gates_z, k))
            work(6)
            psum_finish(3)

            def block_out(i):
                at = rows16(i)
                for j in range(2 * nb):
                    cols = slice(j * CB, (j + 1) * CB)
                    r.resid[at, cols] += r.tot[j, at, :]

            loop(T // 16, block_out)
            out_block = pltpu.make_async_copy(r.resid, r.k_block, r.ow.at[1])
            out_block.start()

            out_gin.wait()
            out_block.wait()

        pl.run_scoped(
            recurrent_backward,
            pltpu.VMEM((D, L), BF16),
            pltpu.VMEM((L, D), BF16),
            pltpu.VMEM((T, D), F32),
            pltpu.VMEM((T, D), BF16),
            pltpu.VMEM((T, L), F32),
            pltpu.VMEM((T, L), F32),
            pltpu.VMEM((B, G + 8, L), F32),
            pltpu.VMEM((2 * nb, T, CB), F32),
            pltpu.VMEM((T, L), BF16),
            pltpu.VMEM((T, L), BF16),
            pltpu.VMEM((T, L), F32),
            pltpu.VMEM((2 * HW, L), F32),
        )


        def rest(stage_o, load_o):
            tail.extend((stage_o, load_o))
            work(7)
            close()

        pl.run_scoped(rest, pltpu.VMEM((nz, DC, LP), BF16), pltpu.VMEM((DC, LP), BF16))

        for q in range(1, nseq):
            src = lax.rem(s + nseq - q, nseq)
            remote(
                r.gsend.at[src], r.gland.at[src], r.ga_s.at[q], r.ga_r.at[q], partner
            ).wait_recv()
        for k in range(1, nz):
            src = lax.rem(z + nz - k, nz)
            remote(r.smv, r.smz.at[src], r.smz_s.at[k], r.smz_r.at[k], partner).wait_recv()
            remote(
                r.gts.at[src], r.gtz.at[src], r.gtz_s.at[k], r.gtz_r.at[k], partner
            ).wait_recv()
        r.gland[s] = r.gsend[s]
        r.smz[z] = r.smv[...]
        r.gtz[z] = r.gts[z]
        small, gates, gain = r.smz[0], r.gtz[0].astype(F32), r.gland[0]
        for q in range(1, nz):
            small = small + r.smz[q]
            gates = gates + r.gtz[q].astype(F32)
        for q in range(1, nseq):
            gain = gain + r.gland[q]
        r.k_small[...] = jnp.zeros((8, LP), F32)
        r.k_small[:, 0:L] = small
        r.k_small[7:8, 0:L] = small[7:8, :] * r.rv[1:2, :]
        r.k_gain[...] = gain
        r.k_gates[...] = gates

        for make, when in pending:
            if when is None:
                make().wait_send()
            else:
                pl.when(when())(lambda make=make: make().wait_send())

    pl.run_scoped(
        after_feed_forward,
        pltpu.VMEM((2, nz, DC, FB), BF16),
        pltpu.VMEM((DC, FB), BF16),
        pltpu.VMEM((2, DC, d.W), BF16),
        pltpu.VMEM((nz, T, d.W), BF16),
        pltpu.VMEM((2, nx - 1, DC, d.W), BF16),
    )


def finish(d, r):
    L, LP, FB, DC, nseq, nz, nx = d.L, d.LP, d.FB, d.DC, d.nseq, d.nz, d.nx
    s = lax.axis_index("seq")
    z = lax.div(s, nx)
    copies, loads, used = [], [], [0]

    def copy(src, dst):
        used[0] += 1
        return pltpu.make_async_copy(src, dst, r.sem.at[used[0] - 1])

    def load(*pairs):
        group = [copy(*pair) for pair in pairs]
        for one in group:
            one.start()
        loads.append(group)

    far = nz - 1
    for b in range(6):
        load((r.own_f.at[b], r.a_f.at[b]), (r.land_f.at[b, 0], r.b_f.at[b]), (r.land_f.at[b, far], r.c_f.at[b]))
    load((r.own_o, r.a_o), (r.land_o.at[0], r.b_o), (r.land_o.at[far], r.c_o))
    for qb in range(3):
        load((r.own_d.at[qb], r.a_d.at[qb]), (r.xr_d.at[qb], r.b_d.at[qb]))
    for qb in range(2):
        load((r.own_r.at[qb], r.a_r.at[qb]), (r.xr_r.at[qb], r.b_r.at[qb]))
    load((r.k_block, r.w_block))
    load((r.k_gin, r.w_gin))

    def write(buf, ref):
        one = copy(buf, ref)
        one.start()
        copies.append(one)

    def emit(value, buf, ref):
        buf[...] = value
        write(buf, ref)

    def chained(a, left, right):
        v = a.astype(F32) + jnp.where(z > 0, left.astype(F32), 0.0)
        return v + jnp.where(z < nz - 1, right.astype(F32), 0.0)

    def arrived(i):
        for one in loads[i]:
            one.wait()

    for b in range(6):
        arrived(b)
        ref = r.o_wup if b % 2 else r.o_wgate
        v = chained(r.a_f[b], r.b_f[b], r.c_f[b])
        emit(v, r.v_f.at[b], ref.at[:, b // 2 * FB : (b // 2 + 1) * FB])
    arrived(6)
    emit(chained(r.a_o[...], r.b_o[...], r.c_o[...]).T[0:L], r.v_o, r.o_wout)
    for qb in range(5):
        arrived(7 + qb)
        a, b = (r.a_d[qb], r.b_d[qb]) if qb < 3 else (r.a_r[qb - 3], r.b_r[qb - 3])
        v = a.astype(F32)
        for k in range(nx - 1):
            v = v + b[k].astype(F32)
        if qb < 3:
            emit(v.T, r.v_d.at[qb], r.o_wdown.at[qb * FB : (qb + 1) * FB])
        else:
            emit(v[:, 0:L], r.v_r.at[qb - 3], r.o_wgel if qb == 3 else r.o_wrec)

    arrived(12)
    write(r.w_block, r.o_block)
    arrived(13)
    write(r.w_gin, r.o_gin)
    part = L // nseq
    small = pltpu.roll(r.k_small[...], lax.rem(LP - s * part, LP), 1)
    r.o_cw[...] = small[0:4, 0:part]
    r.o_cb[...] = small[4, 0:part]
    r.o_ba[...] = small[5, 0:part]
    r.o_bx[...] = small[6, 0:part]
    r.o_lr[...] = small[7, 0:part]
    r.o_gm[...] = r.k_gain[0, :]
    r.o_gf[...] = r.k_gain[1, :]
    r.o_ga[...] = r.k_gates[0]
    r.o_gx[...] = r.k_gates[1]
    for one in copies:
        one.wait()


IN_ANY = ("x_in", "w_rec", "w_gel", "w_out", "gate_a", "gate_x", "w_gate", "w_up", "w_down", "cot")
IN_VMEM = (
    "ids", "gain_mix", "gain_ffn", "conv_weight", "conv_bias", "bias_a", "bias_x", "log_rate"
)
MID_VMEM = ("k_small", "k_gain", "k_gates")
LIMIT = 62 * 2**20


def space(in_vmem):
    return pl.BlockSpec(memory_space=pltpu.VMEM if in_vmem else pl.ANY)


def on_device(nseq, nm, *args):
    (
        block_input,
        segment_ids,
        gain_mix,
        w_rec,
        w_gel,
        conv_weight,
        conv_bias,
        gate_a,
        gate_x,
        bias_a,
        bias_x,
        log_rate,
        w_out,
        gain_ffn,
        w_gate,
        w_up,
        w_down,
        cotangent,
    ) = args
    B, G, D = block_input.shape
    T, L, F = B * G, w_rec.shape[1], w_gate.shape[1]
    nz = Z_CHIPS
    d = types.SimpleNamespace(
        B=B, G=G, T=T, D=D, L=L, F=F, LP=-(-L // 128) * 128, FB=F // 3, HW=gate_a.shape[0],
        DC=D // nseq, nseq=nseq, nm=nm, nz=nz, nx=nseq // nz, ny=nm // CORES, CB=256,
        nb=D // CORES // 256, taps=conv_weight.shape[0], GR=gate_a.shape[0] // nseq,
    )
    d.W = max(d.FB, d.LP)
    outs, scratch, sems = layout(d)
    feed = dict(
        x_in=block_input.reshape(T, D), w_rec=w_rec, w_gel=w_gel, w_out=w_out, gate_a=gate_a,
        gate_x=gate_x, w_gate=w_gate, w_up=w_up, w_down=w_down, cot=cotangent.reshape(T, D),
        ids=segment_ids, gain_mix=gain_mix, gain_ffn=gain_ffn, conv_weight=conv_weight,
        conv_bias=conv_bias, bias_a=bias_a, bias_x=bias_x, log_rate=log_rate,
    )
    names_in = IN_ANY + IN_VMEM
    names = names_in + tuple(outs) + tuple(scratch) + tuple(sems)

    def kernel(*refs):
        body(d, types.SimpleNamespace(**dict(zip(names, refs))))

    mid = pl.pallas_call(
        kernel,
        out_shape=[jax.ShapeDtypeStruct(*v) for v in outs.values()],
        in_specs=[space(n in IN_VMEM) for n in names_in],
        out_specs=[space(n in MID_VMEM) for n in outs],
        scratch_shapes=[pltpu.VMEM(*v) for v in scratch.values()]
        + [pltpu.SemaphoreType.DMA(v) for v in sems.values()],
        compiler_params=pltpu.CompilerParams(
            collective_id=0, has_side_effects=True, vmem_limit_bytes=LIMIT
        ),
        name="block",
    )(*[feed[n] for n in names_in])
    mid = dict(zip(outs, mid))
    for n in ("hz_d", "hz_r"):
        mid.pop(n)
    DC, FB, LP, GR, part = d.DC, d.FB, d.LP, d.GR, L // nseq
    last = dict(
        o_block=(T, D), o_gin=(T, D), o_gm=(DC,), o_wrec=(DC, L), o_wgel=(DC, L),
        o_cw=(d.taps, part), o_cb=(part,), o_ga=(GR, L), o_gx=(GR, L), o_ba=(part,), o_bx=(part,),
        o_lr=(part,), o_wout=(L, DC), o_gf=(DC,), o_wgate=(DC, F), o_wup=(DC, F), o_wdown=(F, DC),
    )
    large = ("o_block", "o_gin", "o_wrec", "o_wgel", "o_wout", "o_wgate", "o_wup", "o_wdown")
    buffers = dict(
        a_f=((6, DC, FB), BF16), b_f=((6, DC, FB), BF16), c_f=((6, DC, FB), BF16),
        a_o=((DC, LP), BF16), b_o=((DC, LP), BF16), c_o=((DC, LP), BF16),
        a_d=((3, DC, FB), BF16), b_d=((3, d.nx - 1, DC, FB), BF16),
        a_r=((2, DC, LP), BF16), b_r=((2, d.nx - 1, DC, LP), BF16),
        w_block=((T, D), F32), w_gin=((T, D), F32),
        v_f=((6, DC, FB), F32), v_o=((L, DC), F32), v_d=((3, FB, DC), F32), v_r=((2, DC, L), F32),
    )
    names_last = tuple(mid) + tuple(last) + tuple(buffers) + ("sem",)

    def last_kernel(*refs):
        finish(d, types.SimpleNamespace(**dict(zip(names_last, refs))))

    results = pl.pallas_call(
        last_kernel,
        out_shape=[jax.ShapeDtypeStruct(v, F32) for v in last.values()],
        in_specs=[space(n in MID_VMEM) for n in mid],
        out_specs=[space(n not in large) for n in last],
        scratch_shapes=[pltpu.VMEM(*v) for v in buffers.values()] + [pltpu.SemaphoreType.DMA((64,))],
        compiler_params=pltpu.CompilerParams(vmem_limit_bytes=LIMIT),
        name="finish",
    )(*mid.values())
    results = list(results)
    results[0] = results[0].reshape(B, G, D)
    results[1] = results[1].reshape(B, G, D)
    return tuple(results)


def solution(mesh):
    nseq, nm = mesh.shape["seq"], mesh.shape["mp"]
    rows, cols, both = P(None, "seq", None), P(None, "mp"), P(("mp", "seq"))
    part = P("seq", "mp")
    in_specs = (
        rows, P(), P(), cols, cols, cols, P("mp"), cols, cols, P("mp"), P("mp"), P("mp"),
        P("mp", None), P(), cols, cols, P("mp", None), rows,
    )
    out_specs = (
        rows, rows, P("seq"), part, part, P(None, ("mp", "seq")), both, part, part, both, both,
        both, P("mp", "seq"), P("seq"), part, part, P("mp", "seq"),
    )

    def step(*args):
        return on_device(nseq, nm, *args)

    return jax.shard_map(step, mesh=mesh, in_specs=in_specs, out_specs=out_specs, check_vma=False)
```

```python
import functools
import types

import jax
import jax.numpy as jnp
from jax import lax
from jax.experimental import pallas as pl
from jax.experimental.pallas import tpu as pltpu
from jax.sharding import PartitionSpec as P

EPS = 1e-06
RATE_SCALE = 8.0
Z_CHIPS = 4
CORES = 2
RING = 3
GELU_C = 0.7978845608028654
GELU_A = 0.044715
MESH = pl.DeviceIdType.MESH
F32 = jnp.float32
BF16 = jnp.bfloat16

SCHEDULE = (
    (
        (),
        (),
        (),
        (),
    ),
    (
        (("P", 0, 1, 3), ("P", 0, 1, 2), ("P", 0, 1, 1),),
        (("F", 0, 0), ("F", 0, 2), ("F", 1, 0), ("F", 1, 2), ("F", 2, 0),),
        (("F", 0, 1), ("F", 0, 3), ("F", 1, 1), ("F", 1, 3), ("F", 2, 1),),
        (("P", 0, -1, 0), ("P", 0, -1, 1), ("P", 0, -1, 2),),
    ),
    (
        (("P", 1, 1, 3), ("P", 1, 1, 2), ("P", 1, 1, 1), ("P", 2, 1, 3), ("P", 2, 1, 2), ("P", 2, 1, 1),),
        (("F", 0, 3), ("F", 2, 2), ("P", 0, 1, 3), ("P", 0, 1, 2), ("F", 1, 3), ("F", 3, 0), ("F", 3, 2),),
        (("F", 0, 0), ("F", 1, 0), ("F", 2, 3), ("P", 0, -1, 0), ("P", 0, -1, 1), ("F", 2, 0),),
        (),
    ),
    (
        (("P", 3, 1, 3), ("P", 3, 1, 2), ("P", 3, 1, 1),),
        (("P", 1, 1, 3), ("F", 2, 3),),
        (("F", 3, 1), ("P", 0, 1, 3), ("F", 3, 3),),
        (("P", 1, -1, 0), ("P", 1, -1, 1), ("P", 1, -1, 2), ("P", 2, -1, 0),),
    ),
    (
        (("P", 4, 1, 3), ("P", 4, 1, 2),),
        (("P", 1, 1, 2), ("P", 0, -1, 0), ("P", 2, 1, 3), ("F", 3, 3),),
        (("P", 1, -1, 0), ("P", 1, -1, 1), ("F", 3, 0), ("P", 1, 1, 3), ("P", 2, -1, 0),),
        (("P", 2, -1, 1), ("P", 2, -1, 2), ("P", 3, -1, 0),),
    ),
    (
        (("Q", 0), ("Q", 1), ("Q", 2), ("P", 4, 1, 1), ("O", 0), ("O", 1), ("O", 2), ("Q", 3), ("P", 5, 1, 3),),
        (("P", 2, 1, 2), ("Q", 0), ("P", 1, -1, 0), ("Q", 1), ("Q", 2), ("Q", 3), ("P", 3, 1, 3), ("O", 0),),
        (("Q", 0), ("P", 2, 1, 3), ("P", 2, -1, 1), ("Q", 1), ("Q", 2), ("Q", 3), ("F", 4, 1), ("O", 0), ("O", 1),),
        (("Q", 0), ("Q", 1), ("Q", 2), ("O", 0), ("P", 3, -1, 1), ("O", 1), ("O", 2), ("O", 3), ("O", 4), ("O", 5),),
    ),
    (
        (("O", 3), ("O", 4), ("O", 5), ("P", 5, 1, 2), ("P", 5, 1, 1),),
        (("F", 4, 2), ("P", 3, 1, 2), ("P", 2, -1, 0), ("O", 1), ("O", 2), ("O", 3), ("O", 4), ("P", 4, 1, 3), ("O", 5), ("P", 4, 1, 2),),
        (("F", 4, 3), ("P", 3, 1, 3), ("P", 3, -1, 0), ("O", 2), ("O", 3), ("O", 4), ("O", 5), ("P", 3, -1, 1),),
        (("P", 3, -1, 2), ("Q", 3), ("P", 4, -1, 0), ("P", 4, -1, 1),),
    ),
    (
        (("P", 6, 1, 3), ("P", 6, 1, 2), ("P", 6, 1, 1), ("O", 6), ("Q", 4),),
        (("O", 6), ("F", 4, 0), ("P", 5, 1, 3), ("F", 4, 3), ("Q", 4), ("P", 3, -1, 0), ("P", 5, 1, 2), ("P", 4, -1, 0), ("P", 6, 1, 3), ("P", 5, -1, 0), ("P", 6, 1, 2), ("P", 6, -1, 0),),
        (("O", 6), ("P", 4, -1, 0), ("P", 4, -1, 1), ("P", 4, 1, 3), ("P", 5, -1, 0), ("P", 5, -1, 1), ("F", 4, 0), ("Q", 4), ("P", 5, 1, 3), ("P", 6, -1, 0), ("P", 6, -1, 1), ("P", 6, 1, 3),),
        (("P", 4, -1, 2), ("P", 5, -1, 0), ("P", 5, -1, 1), ("P", 5, -1, 2), ("O", 6), ("P", 6, -1, 0), ("P", 6, -1, 1), ("P", 6, -1, 2), ("Q", 4),),
    ),
)


def dot(left, right):
    return jnp.dot(left, right, preferred_element_type=F32)


def dot_nt(left, right):
    return lax.dot_general(left, right, (((1,), (1,)), ((), ())), preferred_element_type=F32)


def remote(src, dst, send_sem, recv_sem, device):
    return pltpu.make_async_remote_copy(
        src_ref=src,
        dst_ref=dst,
        send_sem=send_sem,
        recv_sem=recv_sem,
        device_id=device,
        device_id_type=MESH,
    )


def loop(count, body):
    def step(i, carry):
        body(i)
        return carry

    lax.fori_loop(0, count, step, 0)


def rows16(i, offset=0):
    return pl.ds(pl.multiple_of(i * 16 + offset, 16), 16)


def gelu_tanh(v):
    t = jnp.tanh(GELU_C * (v + GELU_A * (v * v * v)))
    return 0.5 * v * (1.0 + t)


def gelu_and_slope(v):
    square = v * v
    t = jnp.tanh(GELU_C * (v + GELU_A * (square * v)))
    half = 0.5 * (1.0 + t)
    slope = half + 0.5 * v * (1.0 - t * t) * (GELU_C * (1.0 + 3.0 * GELU_A * square))
    return v * half, slope


def minus_expm1(v):
    acc = 1.0 + v * (1.0 / 8.0)
    for n in (7.0, 6.0, 5.0, 4.0, 3.0, 2.0):
        acc = 1.0 + v * (1.0 / n) * acc
    return -v * acc


def softplus_small(v):
    u = jnp.exp(v)
    acc = 1.0 / 6.0 - u * (1.0 / 7.0)
    for n in (5.0, 4.0, 3.0, 2.0):
        acc = 1.0 / n - u * acc
    return u * (1.0 - u * acc)


def scan_tile(decay, value, reverse):
    row = lax.broadcasted_iota(jnp.int32, decay.shape, 0)
    for k in (1, 2, 4):
        shift = 8 - k if reverse else k
        valid = row < 8 - k if reverse else row >= k
        decay_k = pltpu.roll(decay, shift, 0)
        value_k = pltpu.roll(value, shift, 0)
        value = jnp.where(valid, decay * value_k + value, value)
        decay = jnp.where(valid, decay * decay_k, decay)
    return decay, value


def fold8(v):
    return v[0:8] + v[8:16]


def layout(dims):
    d = dims
    T, D, L, LP, F, FB, DC = d.T, d.D, d.L, d.LP, d.F, d.FB, d.DC
    B, G, HW = d.B, d.G, d.HW
    outs = dict(
        k_block=((T, D), F32),
        k_gin=((T, D), F32),
        k_small=((8, LP), F32),
        k_gain=((8, DC), F32),
        k_gates=((2, d.GR, L), F32),
        own_f=((6, DC, FB), BF16),
        own_o=((DC, LP), BF16),
        own_d=((3, DC, FB), BF16),
        own_r=((2, DC, LP), BF16),
        land_f=((6, 2 * (d.nz - 1), DC, FB), BF16),
        land_o=((2 * (d.nz - 1), DC, LP), BF16),
        xr_d=((3, d.nx - 1, DC, FB), BF16),
        xr_r=((2, d.nx - 1, DC, LP), BF16),
        hz_d=((3, d.nz, T, FB), BF16),
        hz_r=((2, d.nz, T, LP), BF16),
    )
    scratch = dict(
        x_v=((T, D), BF16),
        cot_v=((T, D), BF16),
        xh=((B * 16, D), BF16),
        scm=((T, 128), F32),
        scf=((T, 128), F32),
        idp=((8, 2 * G), jnp.int32),
        mk=((B, G + 8, 128), F32),
        rv=((8, L), F32),
        wl=((2, HW, L), BF16),
        wo=((2, LP, L), BF16),
        wr=((2, HW, L), BF16),
        extp=((B, 16 + G, L), F32),
        cv=((T, LP), BF16),
        st_l=((T, HW), BF16),
        st_r=((T, HW), BF16),
        hl=((T, HW), BF16),
        hr=((T, HW), BF16),
        pre_gel=((T, L), F32),
        recur=((T, L), F32),
        inj=((T, L), F32),
        cfp=((B, G + 8, L), F32),
        aloc=((T, L), F32),
        stp=((B, 8 + G, L), F32),
        pk=((2, 2 * B, L), F32),
        pf=((2, d.nseq, 2 * B, L), F32),
        resid=((T, D), F32),
        csend=((d.nb, T, d.CB), F32),
        cland=((d.nb, T, d.CB), F32),
        tot=((2 * d.nb, T, d.CB), F32),
        yl=((2, d.ny, d.nb, T, d.CB), BF16),
        fo=((2 * d.nb, T, d.CB), BF16),
        hd=((3, T, FB), BF16),
        gp=((6, d.nx, T, FB), BF16),
        mx=((d.nx, T, LP), BF16),
        gpg=((T, LP), BF16),
        gpr=((T, LP), BF16),
        nmT=((d.nz, d.nx, DC, T), BF16),
        cotT=((d.nz, d.nx, DC, T), BF16),
        nfT=((d.nz, d.nx, DC, T), BF16),
        gbT=((d.nz, d.nx, DC, T), BF16),
        ez=((2, d.nx, DC, d.nz * T), BF16),
        ex=((2, d.nz, DC, d.nx * T), BF16),
        vecs=((8, L), F32),
        gains=((8, D), F32),
        gacc=((16, D), F32),
        gsend=((d.nseq, 8, DC), F32),
        gland=((d.nseq, 8, DC), F32),
        sacc=((8, 8, L), F32),
        smv=((8, L), F32),
        smx=((d.nx, 8, L), F32),
        smz=((d.nz, 8, L), F32),
        gt=((d.nz, d.nx, 2, d.GR, L), BF16),
        gtx=((d.nx, d.nz, 2, d.GR, L), BF16),
        gtz=((d.nz, 2, d.GR, L), BF16),
        gts=((d.nz, 2, d.GR, L), BF16),
        gs_l=((T, HW), BF16),
        gs_r=((T, HW), BF16),
        gi_l=((T, HW), BF16),
        gi_r=((T, HW), BF16),
        sp_s=((B * 8, L), F32),
        sp_r=((B * 8, L), F32),
    )
    sems = dict(
        ld=(16,),
        halo_s=(B,),
        halo_r=(B,),
        ex_s=(4 * B,),
        ex_r=(4 * B,),
        gi_s=(2,),
        gi_rs=(2,),
        pf_s=(2, d.nseq),
        pf_r=(2, d.nseq),
        c_s=(4, d.nb),
        c_r=(4, d.nb),
        y_s=(4, d.ny, d.nb),
        y_r=(4, d.ny, d.nb),
        a_s=(4, d.nb),
        a_r=(4, d.nb),
        ez_s=(2, d.nz),
        ez_r=(2, d.nz),
        ezc_s=(2, d.nz),
        ezc_r=(2, d.nz),
        ex_xs=(2, d.nx),
        ex_xr=(2, d.nx),
        exc_s=(2, d.nx),
        exc_r=(2, d.nx),
        own_l=(4,),
        hz_s=(5, d.nz, 2),
        hz_rs=(5, d.nz),
        hx_s=(7, d.nx),
        hx_r=(7, d.nx),
        xr_s=(5, d.nx),
        xr_rs=(5, d.nx),
        p_s=(7, d.nz),
        p_r=(7, 2 * (d.nz - 1)),
        smx_s=(d.nx,),
        smx_r=(d.nx,),
        smz_s=(d.nz,),
        smz_r=(d.nz,),
        ga_s=(d.nseq,),
        ga_r=(d.nseq,),
        gtx_s=(d.nx,),
        gtx_r=(d.nx,),
        gtz_s=(d.nz,),
        gtz_r=(d.nz,),
        sp_ss=(1,),
        sp_rs=(1,),
        pl_s=(2,),
        ow=(16,),
    )
    return outs, scratch, sems


def body(d, r):
    T, D, L, LP, F, FB, DC = d.T, d.D, d.L, d.LP, d.F, d.FB, d.DC
    B, G, HW, CB, nb = d.B, d.G, d.HW, d.CB, d.nb
    nseq, nz, nx, ny, nm = d.nseq, d.nz, d.nx, d.ny, d.nm
    s, m = lax.axis_index("seq"), lax.axis_index("mp")
    z, x = lax.div(s, nx), lax.rem(s, nx)
    y, c = lax.div(m, CORES), lax.rem(m, CORES)
    partner = (s, y * CORES + 1 - c)
    left_m, right_m = lax.rem(m + nm - 1, nm), lax.rem(m + 1, nm)
    pending = []

    def later(make, when=None):
        pending.append((make, when))

    def start(make, when=None):
        if when is None:
            make().start()
        else:
            pl.when(when())(lambda: make().start())
        pending.append((make, when))

    barrier = pltpu.get_barrier_semaphore()
    for k in range(1, nseq):
        pl.semaphore_signal(
            barrier, inc=1, device_id=(lax.rem(s + k, nseq), m), device_id_type=MESH
        )
    for k in range(1, nm):
        pl.semaphore_signal(barrier, inc=1, device_id=(s, lax.rem(m + k, nm)), device_id_type=MESH)

    def local(src, dst, i):
        copy = pltpu.make_async_copy(src, dst, r.ld.at[i])
        copy.start()
        return copy

    ld_x = local(r.x_in, r.x_v, 0)
    ld_cot = local(r.cot, r.cot_v, 8)

    half = nb * CB

    def psum_start(k, part):
        par = k % 2

        def send_half(j):
            r.csend[j] = part((1 - c) * half + j * CB)
            remote(r.csend.at[j], r.cland.at[j], r.c_s.at[k, j], r.c_r.at[k, j], partner).start()

        loop(nb, send_half)

        def own_half(j):
            v = part(c * half + j * CB)
            remote(
                r.csend.at[j], r.cland.at[j], r.c_s.at[k, j], r.c_r.at[k, j], partner
            ).wait_recv()
            r.yl[par, y, j] = (v + r.cland[j]).astype(BF16)
            for q in range(1, ny):
                to = lax.rem(y + q, ny)
                remote(
                    r.yl.at[par, y, j],
                    r.yl.at[par, y, j],
                    r.y_s.at[k, q, j],
                    r.y_r.at[k, q, j],
                    (s, to * CORES + c),
                ).start()

        loop(nb, own_half)

    def psum_finish(k):
        par = k % 2

        def total(j):
            for q in range(1, ny):
                src = lax.rem(y + ny - q, ny)
                remote(
                    r.yl.at[par, src, j],
                    r.yl.at[par, src, j],
                    r.y_s.at[k, q, j],
                    r.y_r.at[k, q, j],
                    partner,
                ).wait_recv()
            v = r.yl[par, 0, j].astype(F32)
            for q in range(1, ny):
                v = v + r.yl[par, q, j].astype(F32)
            at = c * nb + j
            r.tot[at] = v
            remote(r.tot.at[at], r.tot.at[at], r.a_s.at[k, j], r.a_r.at[k, j], partner).start()

        loop(nb, total)

        def close(j):
            at = (1 - c) * nb + j
            remote(
                r.tot.at[at], r.tot.at[at], r.a_s.at[k, j], r.a_r.at[k, j], partner
            ).wait()
            remote(
                r.csend.at[j], r.cland.at[j], r.c_s.at[k, j], r.c_r.at[k, j], partner
            ).wait_send()
            for q in range(1, ny):
                remote(
                    r.yl.at[par, y, j],
                    r.yl.at[par, y, j],
                    r.y_s.at[k, q, j],
                    r.y_r.at[k, q, j],
                    partner,
                ).wait_send()

        loop(nb, close)

    def pairs_send(k):
        for q in range(1, nseq):
            start(
                lambda q=q: remote(
                    r.pk.at[k],
                    r.pf.at[k, s],
                    r.pf_s.at[k, q],
                    r.pf_r.at[k, q],
                    (s + q if k == 0 else s - q, m),
                ),
                lambda q=q: s + q < nseq if k == 0 else s - q >= 0,
            )

    def pairs_enter(k, reverse):
        for q in range(1, nseq):
            src = s + q if reverse else s - q

            @pl.when(src < nseq if reverse else src >= 0)
            def _(q=q, src=src):
                remote(
                    r.pk.at[k], r.pf.at[k, src], r.pf_s.at[k, q], r.pf_r.at[k, q], partner
                ).wait_recv()

        value = jnp.zeros((B, L), F32)
        for q in range(nseq - 1):
            at = nseq - 1 - q if reverse else q
            pair = r.pf[k, at]
            new = pair[0:B] * value + pair[B : 2 * B]
            value = jnp.where(at > s if reverse else at < s, new, value)
        return value

    def transposed(src, dst):
        def one(j):
            dst[lax.div(j, nx), lax.rem(j, nx)] = src[:, pl.ds(pl.multiple_of(j * DC, DC), DC)].T

        loop(nseq, one)

    def lanes(i):
        return pl.ds(pl.multiple_of(i * T, T), T)

    ez_half, ex_half = DC // CORES, nz // CORES

    def ez_part(e, src_z, core):
        rows = pl.ds(pl.multiple_of(core * ez_half, ez_half), ez_half)
        return r.ez.at[e, :, rows, lanes(src_z)]

    def ez_own(e):
        src = r.nmT if e else r.cotT
        return pltpu.make_async_copy(src.at[z], r.ez.at[e, :, :, lanes(z)], r.own_l.at[e])

    def ez_copy(e, k):
        to = lax.rem(z + k, nz)
        rows = pl.ds(pl.multiple_of(c * ez_half, ez_half), ez_half)
        return remote(
            (r.nmT if e else r.cotT).at[to, :, rows],
            ez_part(e, z, c),
            r.ez_s.at[e, k],
            r.ez_r.at[e, k],
            (to * nx + x, m),
        )

    def ez_relay_copy(e, k):
        part = ez_part(e, lax.rem(z + nz - k, nz), c)
        return remote(part, part, r.ezc_s.at[e, k], r.ezc_r.at[e, k], partner)

    def ez_send(e, left):
        for k in range(1, nz):
            if left:
                start(functools.partial(ez_copy, e, k), lambda k=k: z + k >= nz)
            else:
                start(functools.partial(ez_copy, e, k), lambda k=k: z + k < nz)

    def ez_relay(e):
        for k in range(1, nz):
            part = ez_part(e, lax.rem(z + nz - k, nz), c)
            remote(part, part, r.ez_s.at[e, k], r.ez_r.at[e, k], partner).wait_recv()
            start(functools.partial(ez_relay_copy, e, k))

    def ez_wait(e):
        ez_own(e).wait()
        for k in range(1, nz):
            part = ez_part(e, lax.rem(z + nz - k, nz), 1 - c)
            remote(part, part, r.ezc_s.at[e, k], r.ezc_r.at[e, k], partner).wait_recv()

    def ex_part(e, src_x, core):
        return r.ex.at[e, pl.ds(core * ex_half, ex_half), :, lanes(src_x)]

    def ex_own(e):
        src = r.gbT if e else r.nfT
        return pltpu.make_async_copy(src.at[:, x], r.ex.at[e, :, :, lanes(x)], r.own_l.at[2 + e])

    def ex_copy(e, k):
        to = lax.rem(x + k, nx)
        return remote(
            (r.gbT if e else r.nfT).at[pl.ds(c * ex_half, ex_half), to],
            ex_part(e, x, c),
            r.ex_xs.at[e, k],
            r.ex_xr.at[e, k],
            (z * nx + to, m),
        )

    def ex_relay_copy(e, k):
        part = ex_part(e, lax.rem(x + nx - k, nx), c)
        return remote(part, part, r.exc_s.at[e, k], r.exc_r.at[e, k], partner)

    def ex_send(e):
        ex_own(e).start()
        for k in range(1, nx):
            start(functools.partial(ex_copy, e, k))

    def ex_relay(e):
        for k in range(1, nx):
            part = ex_part(e, lax.rem(x + nx - k, nx), c)
            remote(part, part, r.ex_xs.at[e, k], r.ex_xr.at[e, k], partner).wait_recv()
            start(functools.partial(ex_relay_copy, e, k))

    def ex_wait(e):
        ex_own(e).wait()
        for k in range(1, nx):
            part = ex_part(e, lax.rem(x + nx - k, nx), 1 - c)
            remote(part, part, r.exc_s.at[e, k], r.exc_r.at[e, k], partner).wait_recv()

    def q_own(qb):
        return r.hd.at[qb] if qb < 3 else (r.gpg if qb == 3 else r.gpr)

    def q_land(qb, zo):
        return r.hz_d.at[qb, zo] if qb < 3 else r.hz_r.at[qb - 3, zo]

    def q_copy(qb, src, zo, way):
        to = s + nx if way == 0 else s - nx
        return remote(src, q_land(qb, zo), r.hz_s.at[qb, zo, way], r.hz_rs.at[qb, zo], (to, m))

    def q_send(qb):
        start(lambda: q_copy(qb, q_own(qb), z, 0), lambda: z < nz - 1)
        start(lambda: q_copy(qb, q_own(qb), z, 1), lambda: z > 0)

    def hx_ref(pb):
        return r.gp.at[pb] if pb < 6 else r.mx

    def hx_send(pb):
        def copy(k):
            to = lax.rem(x + k, nx)
            return remote(
                hx_ref(pb).at[x],
                hx_ref(pb).at[x],
                r.hx_s.at[pb, k],
                r.hx_r.at[pb, k],
                (z * nx + to, m),
            )

        for k in range(1, nx):
            start(functools.partial(copy, k))

    def hx_wait(pb):
        for k in range(1, nx):
            src = lax.rem(x + nx - k, nx)
            remote(
                hx_ref(pb).at[src],
                hx_ref(pb).at[src],
                r.hx_s.at[pb, k],
                r.hx_r.at[pb, k],
                partner,
            ).wait_recv()

    r.vecs[0 : d.taps] = r.conv_weight[...]
    for row, vector in enumerate((r.conv_bias, r.bias_a, r.bias_x, r.log_rate)):
        r.vecs[d.taps + row : d.taps + row + 1] = vector[...].reshape(1, L)
    r.gains[0:1] = r.gain_mix[...].reshape(1, D)
    r.gains[1:2] = r.gain_ffn[...].reshape(1, D)
    own_ids = r.ids[:, pl.ds(pl.multiple_of(s * G, G), G)]
    before = r.ids[:, pl.ds(pl.multiple_of(jnp.maximum(s - 1, 0) * G, G), G)]
    r.idp[...] = jnp.zeros((8, 2 * G), jnp.int32)
    r.idp[0:B, 0:G] = jnp.where(s > 0, before, -1)
    r.idp[0:B, G : 2 * G] = own_ids
    both = r.idp[...]
    square_row = lax.broadcasted_iota(jnp.int32, (G, G), 0)
    same = [
        jnp.where(pltpu.roll(both, k, 1)[:, G:] == both[:, G:], 1.0, 0.0) for k in range(1, d.taps)
    ]
    for b in range(B):
        square = jnp.zeros((G, G), F32)
        for k in range(1, d.taps):
            square = jnp.where(
                square_row == k, jnp.broadcast_to(same[k - 1][b : b + 1], (G, G)), square
            )
        r.mk[b, 0:G, :] = square.T
        r.mk[b, G : G + 8, :] = jnp.zeros((8, 128), F32)
    rates = r.vecs[7:8]
    r.rv[0:1] = -RATE_SCALE * softplus_small(rates)
    r.rv[1:2] = -RATE_SCALE * jax.nn.sigmoid(rates)
    r.sacc[...] = jnp.zeros((8, 8, L), F32)

    base = L * m + HW // 4
    shift = HW.bit_length() - 1
    turn = lax.rem(base, HW)
    turn_right = lax.rem(base + L, HW)

    def head_mask(first, count):
        row = lax.broadcasted_iota(jnp.int32, (count, L), 0) + first
        col = lax.broadcasted_iota(jnp.int32, (count, L), 1) + base
        return lax.shift_right_arithmetic(row, shift) == lax.shift_right_arithmetic(col, shift)

    pieces = [(p, min(HW, LP - p)) for p in range(0, LP, HW)]

    def recurrent_forward(wrec_v, wgel_v, wout_v, nm_v, nmh, pa, px, g2):
        ld_gel = local(r.w_gel, wgel_v, 1)
        ld_rec = local(r.w_rec, wrec_v, 2)
        ld_g = [
            local(gate, g2.at[i, pl.ds(at * HW, HW)], 3 + 2 * i + at)
            for i, gate in enumerate((r.gate_a, r.gate_x))
            for at in range(2)
        ]
        ld_out = local(r.w_out, wout_v, 7)
        ld_x.wait()

        def norm(i):
            at = rows16(i)
            v = r.x_v[at, :].astype(F32)
            scale = lax.rsqrt(jnp.mean(v * v, axis=1, keepdims=True) + EPS)
            nm_v[at, :] = (v * scale * r.gains[0:1]).astype(BF16)
            r.scm[at, :] = jnp.broadcast_to(scale, (16, 128))

        loop(T // 16, norm)
        ld_gel.wait()
        r.pre_gel[...] = dot(nm_v[...], wgel_v[...])
        ld_rec.wait()
        main = dot(nm_v[...], wrec_v[...]).astype(BF16).astype(F32)
        for b in range(B):
            r.extp[b, 16 : 16 + G, :] = main[b * G : (b + 1) * G]

        if LP > L:
            for wide in (r.cv, r.gpg, r.gpr, r.mx.at[x]):
                wide[:, L:] = jnp.zeros((T, LP - L), BF16)

        def conv(i):
            for b in range(B):
                window = r.extp[b, pl.ds(pl.multiple_of(i * 16 + 8, 8), 24), :]
                keep = r.mk[b, rows16(i), :]
                acc = r.vecs[4:5] + r.vecs[0:1] * window[8:24]
                for k in range(1, d.taps):
                    acc = acc + r.vecs[k : k + 1] * (keep[:, k : k + 1] * window[8 - k : 24 - k])
                at = rows16(i, b * G)
                r.cv[at, 0:L] = acc.astype(BF16)
                r.st_l[at, :] = acc[:, :HW].astype(BF16)
                r.st_r[at, :] = acc[:, L - HW :].astype(BF16)

        def neighbours(b, side, first):
            rows = pl.ds(b * G, 16) if first else pl.ds(b * G + 16, G - 16)
            src, dst, to = (r.st_r, r.hl, right_m) if side else (r.st_l, r.hr, left_m)
            i = 4 * b + 2 * side + first
            return remote(src.at[rows], dst.at[rows], r.ex_s.at[i], r.ex_r.at[i], (s, to))

        loop(G // 16 - 1, lambda i: conv(i + 1))
        ld_cot.wait()
        transposed(r.cot_v, r.cotT)
        pl.semaphore_wait(barrier, nseq - 1 + nm - 1)

        for b in range(B):
            start(
                lambda b=b: remote(
                    r.x_in.at[pl.ds(b * G + G - 16, 16)],
                    r.xh.at[pl.ds(b * 16, 16)],
                    r.halo_s.at[b],
                    r.halo_r.at[b],
                    (s + 1, m),
                ),
                lambda: s < nseq - 1,
            )

        for b in range(B):
            for side in range(2):
                start(functools.partial(neighbours, b, side, 0))

        @pl.when(s > 0)
        def _():
            for b in range(B):
                remote(
                    r.x_in.at[pl.ds(b * G + G - 16, 16)],
                    r.xh.at[pl.ds(b * 16, 16)],
                    r.halo_s.at[b],
                    r.halo_r.at[b],
                    partner,
                ).wait_recv()

        @pl.when(s == 0)
        def _():
            r.xh[...] = jnp.zeros((B * 16, D), BF16)

        for b in range(B):
            v = r.xh[b * 16 : (b + 1) * 16, :].astype(F32)
            scale = lax.rsqrt(jnp.mean(v * v, axis=1, keepdims=True) + EPS)
            nmh[b * 16 : (b + 1) * 16, :] = (v * scale * r.gains[0:1]).astype(BF16)
        rim = dot(nmh[...], wrec_v[...]).astype(BF16).astype(F32)
        for b in range(B):
            r.extp[b, 0:16, :] = rim[b * 16 : (b + 1) * 16]

        conv(0)
        for b in range(B):
            for side in range(2):
                start(functools.partial(neighbours, b, side, 1))

        for copy in ld_g:
            copy.wait()
        for i in range(2):
            table = g2[i, pl.ds(pl.multiple_of(turn, HW // 4), HW), :].astype(F32)
            table_right = g2[i, pl.ds(pl.multiple_of(turn_right, HW // 4), HW), :].astype(F32)
            r.wl[i] = jnp.where(head_mask(base - HW, HW), table, 0.0).astype(BF16)
            r.wr[i] = jnp.where(head_mask(base + L, HW), table_right, 0.0).astype(BF16)
            for p, n in pieces:
                r.wo[i, p : p + n, :] = jnp.where(head_mask(base + p, n), table[:n], 0.0).astype(
                    BF16
                )
        pa[...] = dot(r.cv[...], r.wo[0]) + r.vecs[5:6]
        px[...] = dot(r.cv[...], r.wo[1]) + r.vecs[6:7]
        for i in range(4 * B):
            neighbours(i // 4, i // 2 % 2, i % 2).wait_recv()
        pa[...] += dot(r.hl[...], r.wl[0]) + dot(r.hr[...], r.wr[0])
        px[...] += dot(r.hl[...], r.wl[1]) + dot(r.hr[...], r.wr[1])

        def scan(i, carry):
            out = []
            for b in range(B):
                decay_in, state_in = carry[2 * b], carry[2 * b + 1]
                at = rows16(i, b * G)
                recur = jax.nn.sigmoid(pa[at, :])
                inject = jax.nn.sigmoid(px[at, :])
                log_decay = r.rv[0:1] * recur
                decay = jnp.exp(log_decay)
                spread = jnp.sqrt(minus_expm1(2.0 * log_decay))
                drive = spread * inject * r.cv[at, 0:L].astype(F32)
                coeff = decay * r.mk[b, rows16(i), :][:, 1:2]
                r.recur[at, :] = recur
                r.inj[at, :] = inject
                r.cfp[b, rows16(i), :] = coeff
                for h in range(2):
                    a, v = scan_tile(
                        coeff[8 * h : 8 * h + 8], drive[8 * h : 8 * h + 8], reverse=False
                    )
                    v = v + a * state_in
                    a = a * decay_in
                    decay_in, state_in = a[7:8], v[7:8]
                    r.aloc[pl.ds(pl.multiple_of(b * G + i * 16 + 8 * h, 8), 8), :] = a
                    r.stp[b, pl.ds(pl.multiple_of(8 + i * 16 + 8 * h, 8), 8), :] = v
                out += [decay_in, state_in]
            return tuple(out)

        one, zero = jnp.ones((1, L), F32), jnp.zeros((1, L), F32)
        ends = lax.fori_loop(0, G // 16, scan, (one, zero) * B)
        for b in range(B):
            r.pk[0, b : b + 1, :] = ends[2 * b]
            r.pk[0, B + b : B + b + 1, :] = ends[2 * b + 1]
            r.cfp[b, G : G + 8, :] = jnp.ones((8, L), F32)
        pairs_send(0)
        transposed(nm_v, r.nmT)
        for e in range(2):
            ez_own(e).start()
            ez_send(e, True)
        entered = pairs_enter(0, False)
        for b in range(B):
            r.stp[b, 0:8, :] = jnp.broadcast_to(entered[b : b + 1], (8, L))

        def states(i):
            for b in range(B):
                at = rows16(i, b * G)
                here = pl.ds(pl.multiple_of(8 + i * 16, 8), 16)
                state = r.stp[b, here, :] + r.aloc[at, :] * r.stp[b, 7:8, :]
                r.stp[b, here, :] = state
                r.mx[x, at, 0:L] = (state * gelu_tanh(r.pre_gel[at, :])).astype(BF16)

        loop(G // 16, states)
        ld_out.wait()
        psum_start(
            0,
            lambda col: dot(r.mx[x, :, 0:L], wout_v[:, pl.ds(pl.multiple_of(col, CB), CB)]),
        )
        hx_send(6)

    pl.run_scoped(
        recurrent_forward,
        pltpu.VMEM((D, L), BF16),
        pltpu.VMEM((D, L), BF16),
        pltpu.VMEM((L, D), BF16),
        pltpu.VMEM((T, D), BF16),
        pltpu.VMEM((B * 16, D), BF16),
        pltpu.VMEM((T, L), F32),
        pltpu.VMEM((T, L), F32),
        pltpu.VMEM((2, 2 * HW, L), BF16),
    )

    def feed_forward(wd_v, wg_v, wu_v, nf, gh, pg, pu):
        ld_d = [local(r.w_down.at[pl.ds(i * FB, FB)], wd_v.at[i], i) for i in range(3)]
        ld_g = [local(r.w_gate.at[:, pl.ds(i * FB, FB)], wg_v.at[i], 3 + i) for i in range(3)]
        ld_u = [local(r.w_up.at[:, pl.ds(i * FB, FB)], wu_v.at[i], 6 + i) for i in range(3)]
        for i in range(3):
            ld_d[i].wait()

        def hidden_grad(i):
            gh[i] = dot_nt(r.cot_v[...], wd_v[i])

        loop(3, hidden_grad)
        for e in range(2):
            ez_send(e, False)
        psum_finish(0)

        def residual(i):
            at = rows16(i)
            parts = [
                r.tot[j, at, :] + r.x_v[at, j * CB : (j + 1) * CB].astype(F32)
                for j in range(2 * nb)
            ]
            square = parts[0] * parts[0]
            for v in parts[1:]:
                square = square + v * v
            scale = lax.rsqrt(jnp.sum(square, axis=1, keepdims=True) / D + EPS)
            for j, v in enumerate(parts):
                cols = slice(j * CB, (j + 1) * CB)
                r.resid[at, cols] = v
                nf[at, cols] = (v * scale * r.gains[1:2, cols]).astype(BF16)
            r.scf[at, :] = jnp.broadcast_to(scale, (16, 128))

        loop(T // 16, residual)
        for i in range(3):
            ld_g[i].wait()
            ld_u[i].wait()

        for i in range(3):
            pg[...] = dot(nf[...], wg_v[i])
            pu[...] = dot(nf[...], wu_v[i])

            def units(t, i=i):
                at = rows16(t)
                up, back = pu[at, :], gh[i, at, :]
                active, slope = gelu_and_slope(pg[at, :])
                r.hd[i, at, :] = (active * up).astype(BF16)
                r.gp[2 * i, x, at, :] = (back * up * slope).astype(BF16)
                r.gp[2 * i + 1, x, at, :] = (back * active).astype(BF16)

            loop(T // 16, units)
            q_send(i)
            if i == 0:
                transposed(nf, r.nfT)
                ex_send(0)
            if i < 2:
                hx_send(2 * i)
            if i == 0:
                hx_send(1)

        def back_input(col):
            at = pl.ds(pl.multiple_of(col, CB), CB)
            v = dot_nt(r.gp[0, x], wg_v[0, at, :]) + dot_nt(r.gp[1, x], wu_v[0, at, :])
            for i in range(1, 3):
                v = v + dot_nt(r.gp[2 * i, x], wg_v[i, at, :])
                v = v + dot_nt(r.gp[2 * i + 1, x], wu_v[i, at, :])
            return v

        psum_start(1, back_input)

        def ffn_term(j):
            at = pl.ds(pl.multiple_of(j * CB, CB), CB)
            v = dot(r.hd[0], wd_v[0, :, at])
            for i in range(1, 3):
                v = v + dot(r.hd[i], wd_v[i, :, at])
            r.fo[j] = v.astype(BF16)

        loop(2 * nb, ffn_term)
        ex_relay(0)
        ez_relay(0)
        ez_relay(1)

    pl.run_scoped(
        feed_forward,
        pltpu.VMEM((3, FB, D), BF16),
        pltpu.VMEM((3, D, FB), BF16),
        pltpu.VMEM((3, D, FB), BF16),
        pltpu.VMEM((T, D), BF16),
        pltpu.VMEM((3, T, FB), F32),
        pltpu.VMEM((T, FB), F32),
        pltpu.VMEM((T, FB), F32),
    )

    def gain_rows(which):
        total = jnp.sum(r.gacc[...], axis=0, keepdims=True)
        for q in range(nseq):
            r.gsend[q, which : which + 1, :] = total[:, q * DC : (q + 1) * DC]

    def after_feed_forward(stage_f, load_f, own_st, hload, qstage):
        tail = []
        seen = [dict() for _ in range(nz)]

        def once(zz, *what):
            first = what not in seen[zz]
            seen[zz][what] = True
            return first

        def at_end(zz, make):
            seen[zz].setdefault("sent", []).append(make)

        def sized(ref, n):
            return ref if n == ref.shape[-1] else ref.at[:, pl.ds(0, n)]

        def own_write(zz, src, ref):
            turn_ = seen[zz].get("turn", 0)
            seen[zz]["turn"] = turn_ + 1
            at, n = turn_ % 2, src.shape[-1]

            def copy():
                return pltpu.make_async_copy(sized(own_st.at[at], n), ref(), r.ow.at[4 + at])

            held = seen[zz].setdefault("held", {})
            if at in held:
                held[at]().wait()
            sized(own_st.at[at], n)[...] = src.astype(BF16)
            copy().start()
            held[at] = copy

        def p_width(b):
            return FB if b < 6 else LP

        def p_stage(zz, b, zc):
            at = zc if zc < zz else zc - 1
            return stage_f.at[b % RING, at] if b < 6 else tail[0].at[at]

        def p_land(b, place):
            return r.land_f.at[b, place] if b < 6 else r.land_o.at[place]

        def p_part(zz, b, zc):
            if once(zz, "hx", b):
                hx_wait(b)
            e = 0 if b < 6 else 1
            if once(zz, "ex", e):
                ex_wait(e)
            return dot(r.ex[e, zc], hx_ref(b)[...].reshape(nx * T, p_width(b)))

        def p_copy(zz, b, zc, place, to):
            return remote(
                p_stage(zz, b, zc), p_land(b, place), r.p_s.at[b, zc], r.p_r.at[b, place], (to, m)
            )

        def do_p(zz, b, way, zc):
            right = way > 0
            has_input = zz > 0 if right else zz < nz - 1
            place = abs(zc - zz) + (0 if right else nz - 1)
            load = load_f if b < 6 else tail[1]
            if has_input:
                fetch = pltpu.make_async_copy(p_land(b, place), load, r.pl_s.at[0])
                p_copy(zz, b, zc, place, s).wait_recv()
                fetch.start()
            v = p_part(zz, b, zc)
            if has_input:
                fetch.wait()
                v = v + load[...].astype(F32)
            if RING <= b < 6:
                p_copy(zz, b - RING, zc, 0, s).wait_send()
            p_stage(zz, b, zc)[...] = v.astype(BF16)
            p_copy(zz, b, zc, place - 1, s + nx if right else s - nx).start()
            if b >= 6 - RING:
                at_end(zz, lambda: p_copy(zz, b, zc, 0, s).wait_send())

        def do_own(zz, b):
            own_write(zz, p_part(zz, b, zz), lambda: r.own_f.at[b] if b < 6 else r.own_o)

        def q_arrived(zz, qb, zo):
            if once(zz, "hz", qb, zo):
                q_copy(qb, q_land(qb, zo), zo, 0 if zo < zz else 1).wait_recv()

        def do_forward(zz, qb, zo):
            q_arrived(zz, qb, zo)
            way, to = (0, zz + 1) if zo < zz else (1, zz - 1)
            if 0 <= to < nz:
                q_copy(qb, q_land(qb, zo), zo, way).start()
                at_end(zz, lambda: q_copy(qb, q_land(qb, zo), zo, way).wait_send())

        def q_exchange(qb, k, n):
            to = lax.rem(x + k, nx)
            land = r.xr_d.at[qb, nx - k - 1] if qb < 3 else r.xr_r.at[qb - 3, nx - k - 1]
            return remote(
                sized(qstage.at[qb, k - 1], n),
                land,
                r.xr_s.at[qb, k],
                r.xr_rs.at[qb, k],
                (z * nx + to, m),
            )

        def do_q(zz, qb):
            e, n, own = (0, FB, q_own(qb)) if qb < 3 else (1, LP, q_own(qb))

            def piece(zo):
                return hload.at[zo] if n == d.W else hload.at[zo, :, pl.ds(0, n)]

            def fetch(zo):
                src = own if zo == zz else q_land(qb, zo)
                return pltpu.make_async_copy(src, piece(zo), r.ow.at[8 + zo])

            for zo in range(nz):
                if zo != zz:
                    q_arrived(zz, qb, zo)
                fetch(zo).start()
            if once(zz, "ez", e):
                ez_wait(e)
            for zo in range(nz):
                fetch(zo).wait()
            gathered = hload[:, :, 0:n].reshape(nz * T, n)
            for k in range(1, nx):
                v = dot(r.ez[e, lax.rem(x + k, nx)], gathered)
                sized(qstage.at[qb, k - 1], n)[...] = v.astype(BF16)
                q_exchange(qb, k, n).start()
            at_end(zz, lambda: [q_exchange(qb, k, n).wait_send() for k in range(1, nx)])
            own_write(
                zz,
                dot(r.ez[e, x], gathered),
                lambda: r.own_d.at[qb] if qb < 3 else r.own_r.at[qb - 3],
            )

        def work(point):
            for zz in range(nz):

                @pl.when(z == zz)
                def _(zz=zz):
                    for op in SCHEDULE[point][zz]:
                        kind, rest = op[0], op[1:]
                        {"F": do_forward, "P": do_p, "O": do_own, "Q": do_q}[kind](zz, *rest)

        def close():
            for zz in range(nz):

                @pl.when(z == zz)
                def _(zz=zz):
                    for copy in seen[zz].get("held", {}).values():
                        copy().wait()
                    for make in seen[zz].get("sent", []):
                        make()
                    for b in range(7):
                        for place, there in ((0, zz > 0), (nz - 1, zz < nz - 1)):
                            if there:
                                p_copy(zz, b, (zz + 1) % nz, place, s).wait_recv()
                    for qb in range(5):
                        for k in range(1, nx):
                            q_exchange(qb, k, FB if qb < 3 else LP).wait_recv()

        def recurrent_backward(
            w_v, wout_v, gr, gb, gm, gcd, gcp, gmel, gpa, gpx, adj, t2
        ):
            ld_gel = local(r.w_gel, w_v, 2)
            ld_out = local(r.w_out, wout_v, 3)
            r.gsend[...] = jnp.zeros((nseq, 8, DC), F32)
            work(1)
            psum_finish(1)
            r.gacc[...] = jnp.zeros((16, D), F32)

            def norm_back(i):
                at = rows16(i)
                scale = r.scf[at, :][:, 0:1]
                inner = jnp.zeros((16, CB), F32)
                for j in range(2 * nb):
                    cols = slice(j * CB, (j + 1) * CB)
                    inner = inner + r.tot[j, at, :] * r.gains[1:2, cols] * r.resid[at, cols]
                factor = (scale * scale * scale) * (jnp.sum(inner, axis=1, keepdims=True) / D)
                for j in range(2 * nb):
                    cols = slice(j * CB, (j + 1) * CB)
                    n, v = r.tot[j, at, :], r.resid[at, cols]
                    r.gacc[:, cols] += n * v * scale
                    grad = r.cot_v[at, cols].astype(F32) + (
                        scale * (n * r.gains[1:2, cols]) - v * factor
                    )
                    gr[at, cols] = grad
                    gb[at, cols] = grad.astype(BF16)

            loop(T // 16, norm_back)
            gain_rows(1)
            ld_out.wait()
            gm[...] = dot_nt(gb[...], wout_v[...])

            def scan(t, carry):
                i = G // 16 - 1 - t
                out = []
                for b in range(B):
                    decay_in, value_in = carry[2 * b], carry[2 * b + 1]
                    at = rows16(i, b * G)
                    gate, slope = gelu_and_slope(r.pre_gel[at, :])
                    g = gm[at, :]
                    state = r.stp[b, pl.ds(pl.multiple_of(8 + i * 16, 8), 16), :]
                    r.gpg[at, 0:L] = (g * state * slope).astype(BF16)
                    value16 = g * gate
                    following = r.cfp[b, pl.ds(pl.multiple_of(i * 16, 16), 24), :][1:17]
                    for h in (1, 0):
                        a, v = scan_tile(
                            following[8 * h : 8 * h + 8], value16[8 * h : 8 * h + 8], reverse=True
                        )
                        v = v + a * value_in
                        a = a * decay_in
                        decay_in, value_in = a[0:1], v[0:1]
                        here = pl.ds(pl.multiple_of(b * G + i * 16 + 8 * h, 8), 8)
                        r.aloc[here, :] = a
                        adj[here, :] = v
                    out += [decay_in, value_in]
                return tuple(out)

            one, zero = jnp.ones((1, L), F32), jnp.zeros((1, L), F32)
            ends = lax.fori_loop(0, G // 16, scan, (one, zero) * B)
            for b in range(B):
                first = r.cfp[b, 0:1, :]
                r.pk[1, b : b + 1, :] = first * ends[2 * b]
                r.pk[1, B + b : B + b + 1, :] = first * ends[2 * b + 1]
            pairs_send(1)
            for b in (3, 4, 5):
                hx_send(b)
            q_send(3)
            ld_gel.wait()

            def gel_term(j):
                at = pl.ds(pl.multiple_of(j * CB, CB), CB)
                gmel[j] = dot_nt(r.gpg[:, 0:L], w_v[at, :])

            loop(2 * nb, gel_term)
            ld_rec = local(r.w_rec, w_v, 1)
            transposed(gb, r.gbT)
            ex_send(1)
            work(2)
            outer = pairs_enter(1, True)

            def gate_back(i):
                for b in range(B):
                    at = rows16(i, b * G)
                    adjoint = adj[at, :] + r.aloc[at, :] * outer[b : b + 1]
                    recur, inject = r.recur[at, :], r.inj[at, :]
                    log_decay = r.rv[0:1] * recur
                    decay = jnp.exp(log_decay)
                    value = r.cv[at, 0:L].astype(F32)
                    spread = jnp.sqrt(minus_expm1(2.0 * log_decay))
                    prior = r.stp[b, pl.ds(pl.multiple_of(i * 16, 16), 24), :][7:23]
                    keep = r.mk[b, rows16(i), :][:, 1:2]
                    grad_log = (
                        adjoint * inject * value * (-(decay * decay) / spread)
                        + adjoint * prior * keep * decay
                    )
                    ga = (grad_log * r.rv[0:1] * recur * (1.0 - recur)).astype(BF16)
                    direct = adjoint * spread * inject
                    gx = (adjoint * spread * value * inject * (1.0 - inject)).astype(BF16)
                    gpa[at, :] = ga
                    gpx[at, :] = gx
                    gcd[at, :] = direct
                    r.sacc[5] += fold8(ga.astype(F32))
                    r.sacc[6] += fold8(gx.astype(F32))
                    r.sacc[7] += fold8(grad_log * recur)

            loop(G // 16, gate_back)
            r.gs_l[...] = (dot_nt(gpa[...], r.wl[0]) + dot_nt(gpx[...], r.wl[1])).astype(BF16)

            def to_left():
                return remote(r.gs_l, r.gi_r, r.gi_s.at[0], r.gi_rs.at[0], (s, left_m))

            start(to_left)
            r.gs_r[...] = (dot_nt(gpa[...], r.wr[0]) + dot_nt(gpx[...], r.wr[1])).astype(BF16)

            def to_right():
                return remote(r.gs_r, r.gi_l, r.gi_s.at[1], r.gi_rs.at[1], (s, right_m))

            start(to_right)
            own = dot_nt(gpa[...], r.wo[0]) + dot_nt(gpx[...], r.wo[1])
            gcd[...] += own[:, 0:L]

            for i, grad in enumerate((gpa, gpx)):
                turned = jnp.where(head_mask(base - HW, HW), dot(r.hl[...].T, grad[...]), 0.0)
                t2[0:HW, :] = turned
                for p, n in pieces:
                    part = dot(r.cv[:, p : p + n].T, grad[...])
                    t2[0:n, :] += jnp.where(head_mask(base + p, n), part, 0.0)
                t2[HW : 2 * HW, :] = t2[0:HW, :]
                back = pl.multiple_of(lax.rem(HW - turn, HW), HW // 4)
                table = t2[pl.ds(back, HW), :]
                right = jnp.where(head_mask(base + L, HW), dot(r.hr[...].T, grad[...]), 0.0)
                t2[0:HW, :] = right
                t2[HW : 2 * HW, :] = right
                back = pl.multiple_of(lax.rem(HW - turn_right, HW), HW // 4)
                table = (table + t2[pl.ds(back, HW), :]).astype(BF16)
                for q in range(nseq):
                    r.gt[q // nx, q % nx, i] = table[q * d.GR : (q + 1) * d.GR]

            work(3)
            to_left().wait_recv()
            to_right().wait_recv()
            gcd[:, 0:HW] += r.gi_l[...].astype(F32)
            gcd[:, L - HW : L] += r.gi_r[...].astype(F32)
            for b in range(B):
                gcp[b, 0:G, :] = gcd[b * G : (b + 1) * G, :]
                gcp[b, G : G + 8, :] = jnp.zeros((8, L), F32)

            for b in range(B):
                top, keep = gcp[b, 0:8, :], r.mk[b, 0:8, :]
                spill = jnp.zeros((8, L), F32)
                row = lax.broadcasted_iota(jnp.int32, (8, L), 0)
                for k in range(1, d.taps):
                    moved = pltpu.roll(r.vecs[k : k + 1] * (keep[:, k : k + 1] * top), 8 - k, 0)
                    spill = spill + jnp.where(row >= 8 - k, moved, 0.0)
                r.sp_s[b * 8 : (b + 1) * 8, :] = spill

            def spilled():
                return remote(r.sp_s, r.sp_r, r.sp_ss.at[0], r.sp_rs.at[0], (s - 1, m))

            start(spilled, lambda: s > 0)

            @pl.when(s == nseq - 1)
            def _():
                r.sp_r[...] = jnp.zeros((B * 8, L), F32)

            def conv_back(i, spill):
                for b in range(B):
                    grads = gcp[b, pl.ds(pl.multiple_of(i * 16, 16), 24), :]
                    keep = r.mk[b, pl.ds(pl.multiple_of(i * 16, 16), 24), :]
                    window = r.extp[b, pl.ds(pl.multiple_of(i * 16 + 8, 8), 24), :]
                    here = grads[0:16]
                    out = r.vecs[0:1] * here
                    if not spill:
                        r.sacc[4] += fold8(here)
                        r.sacc[0] += fold8(here * window[8:24])
                    for k in range(1, d.taps):
                        masked = keep[:, k : k + 1] * grads
                        out = out + r.vecs[k : k + 1] * masked[k : k + 16]
                        if not spill:
                            r.sacc[k] += fold8(masked[0:16] * window[8 - k : 24 - k])
                    if spill:
                        extra = r.sp_r[b * 8 : (b + 1) * 8, :]
                        out = out + jnp.concatenate([jnp.zeros((8, L), F32), extra], axis=0)
                    r.gpr[rows16(i, b * G), 0:L] = out.astype(BF16)

            loop(G // 16, lambda i: conv_back(i, False))
            for k in range(8):
                r.smv[k : k + 1, :] = jnp.sum(r.sacc[k], axis=0, keepdims=True)

            work(4)

            @pl.when(s < nseq - 1)
            def _():
                spilled().wait_recv()

            conv_back(G // 16 - 1, True)
            q_send(4)
            ld_rec.wait()

            def mix_term(col):
                at = pl.ds(pl.multiple_of(col, CB), CB)
                return dot_nt(r.gpr[:, 0:L], w_v[at, :]) + gmel[lax.div(col, CB)]

            psum_start(2, mix_term)

            def small_x(k):
                to = lax.rem(x + k, nx)
                return remote(
                    r.smv, r.smx.at[x], r.smx_s.at[k], r.smx_r.at[k], (z * nx + to, m)
                )

            def gates_x(k):
                to = lax.rem(x + k, nx)
                return remote(
                    r.gt.at[:, to], r.gtx.at[x], r.gtx_s.at[k], r.gtx_r.at[k], (z * nx + to, m)
                )

            def small_z(k):
                to = lax.rem(z + k, nz)
                return remote(
                    r.smv, r.smz.at[z], r.smz_s.at[k], r.smz_r.at[k], (to * nx + x, m)
                )

            def gates_z(k):
                to = lax.rem(z + k, nz)
                return remote(
                    r.gts.at[to], r.gtz.at[z], r.gtz_s.at[k], r.gtz_r.at[k], (to * nx + x, m)
                )

            def gain_copy(q):
                to = lax.rem(s + q, nseq)
                return remote(r.gsend.at[to], r.gland.at[s], r.ga_s.at[q], r.ga_r.at[q], (to, m))

            for k in range(1, nx):
                small_x(k).start()
                gates_x(k).start()
            ex_relay(1)
            work(5)
            psum_finish(2)

            r.gacc[...] = jnp.zeros((16, D), F32)

            def norm_back_mix(i):
                at = rows16(i)
                scale = r.scm[at, :][:, 0:1]
                inner = jnp.zeros((16, CB), F32)
                for j in range(2 * nb):
                    cols = slice(j * CB, (j + 1) * CB)
                    v = r.x_v[at, cols].astype(F32)
                    inner = inner + r.tot[j, at, :] * r.gains[0:1, cols] * v
                factor = (scale * scale * scale) * (jnp.sum(inner, axis=1, keepdims=True) / D)
                for j in range(2 * nb):
                    cols = slice(j * CB, (j + 1) * CB)
                    n, v = r.tot[j, at, :], r.x_v[at, cols].astype(F32)
                    r.gacc[:, cols] += n * v * scale
                    gr[at, cols] = gr[at, cols] + (scale * (n * r.gains[0:1, cols]) - v * factor)

            loop(T // 16, norm_back_mix)
            out_gin = pltpu.make_async_copy(gr, r.k_gin, r.ow.at[0])
            out_gin.start()
            gain_rows(0)
            for q in range(1, nseq):
                start(functools.partial(gain_copy, q))

            psum_start(3, lambda col: r.fo[lax.div(col, CB)].astype(F32))
            small, gates = r.smv[...], r.gt[:, x].astype(F32)
            for k in range(1, nx):
                src = lax.rem(x + nx - k, nx)
                remote(r.smv, r.smx.at[src], r.smx_s.at[k], r.smx_r.at[k], partner).wait_recv()
                remote(r.gt.at[:, x], r.gtx.at[src], r.gtx_s.at[k], r.gtx_r.at[k], partner).wait()
                small_x(k).wait_send()
            for k in range(1, nx):
                src = lax.rem(x + nx - k, nx)
                small = small + r.smx[src]
                gates = gates + r.gtx[src].astype(F32)
            r.smv[...] = small
            r.gts[...] = gates.astype(BF16)
            for k in range(1, nz):
                start(functools.partial(small_z, k))
                start(functools.partial(gates_z, k))
            work(6)
            psum_finish(3)

            def block_out(i):
                at = rows16(i)
                for j in range(2 * nb):
                    cols = slice(j * CB, (j + 1) * CB)
                    r.resid[at, cols] += r.tot[j, at, :]

            loop(T // 16, block_out)
            out_block = pltpu.make_async_copy(r.resid, r.k_block, r.ow.at[1])
            out_block.start()

            out_gin.wait()
            out_block.wait()

        pl.run_scoped(
            recurrent_backward,
            pltpu.VMEM((D, L), BF16),
            pltpu.VMEM((L, D), BF16),
            pltpu.VMEM((T, D), F32),
            pltpu.VMEM((T, D), BF16),
            pltpu.VMEM((T, L), F32),
            pltpu.VMEM((T, L), F32),
            pltpu.VMEM((B, G + 8, L), F32),
            pltpu.VMEM((2 * nb, T, CB), F32),
            pltpu.VMEM((T, L), BF16),
            pltpu.VMEM((T, L), BF16),
            pltpu.VMEM((T, L), F32),
            pltpu.VMEM((2 * HW, L), F32),
        )


        def rest(stage_o, load_o):
            tail.extend((stage_o, load_o))
            work(7)
            close()

        pl.run_scoped(rest, pltpu.VMEM((nz - 1, DC, LP), BF16), pltpu.VMEM((DC, LP), BF16))

        for q in range(1, nseq):
            src = lax.rem(s + nseq - q, nseq)
            remote(
                r.gsend.at[src], r.gland.at[src], r.ga_s.at[q], r.ga_r.at[q], partner
            ).wait_recv()
        for k in range(1, nz):
            src = lax.rem(z + nz - k, nz)
            remote(r.smv, r.smz.at[src], r.smz_s.at[k], r.smz_r.at[k], partner).wait_recv()
            remote(
                r.gts.at[src], r.gtz.at[src], r.gtz_s.at[k], r.gtz_r.at[k], partner
            ).wait_recv()
        r.gland[s] = r.gsend[s]
        r.smz[z] = r.smv[...]
        r.gtz[z] = r.gts[z]
        small, gates, gain = r.smz[0], r.gtz[0].astype(F32), r.gland[0]
        for q in range(1, nz):
            small = small + r.smz[q]
            gates = gates + r.gtz[q].astype(F32)
        for q in range(1, nseq):
            gain = gain + r.gland[q]
        r.k_small[...] = jnp.zeros((8, LP), F32)
        r.k_small[:, 0:L] = small
        r.k_small[7:8, 0:L] = small[7:8, :] * r.rv[1:2, :]
        r.k_gain[...] = gain
        r.k_gates[...] = gates

        for make, when in pending:
            if when is None:
                make().wait_send()
            else:
                pl.when(when())(lambda make=make: make().wait_send())

    pl.run_scoped(
        after_feed_forward,
        pltpu.VMEM((RING, nz - 1, DC, FB), BF16),
        pltpu.VMEM((DC, FB), BF16),
        pltpu.VMEM((2, DC, d.W), BF16),
        pltpu.VMEM((nz, T, d.W), BF16),
        pltpu.VMEM((5, nx - 1, DC, d.W), BF16),
    )


def finish(d, r):
    L, LP, FB, DC, nseq, nz, nx = d.L, d.LP, d.FB, d.DC, d.nseq, d.nz, d.nx
    s = lax.axis_index("seq")
    z = lax.div(s, nx)
    copies, loads, used = [], [], [0]

    def copy(src, dst):
        used[0] += 1
        return pltpu.make_async_copy(src, dst, r.sem.at[used[0] - 1])

    def load(*pairs):
        group = [copy(*pair) for pair in pairs]
        for one in group:
            one.start()
        loads.append(group)

    far = nz - 1
    for b in range(6):
        load((r.own_f.at[b], r.a_f.at[b]), (r.land_f.at[b, 0], r.b_f.at[b]), (r.land_f.at[b, far], r.c_f.at[b]))
    load((r.own_o, r.a_o), (r.land_o.at[0], r.b_o), (r.land_o.at[far], r.c_o))
    for qb in range(3):
        load((r.own_d.at[qb], r.a_d.at[qb]), (r.xr_d.at[qb], r.b_d.at[qb]))
    for qb in range(2):
        load((r.own_r.at[qb], r.a_r.at[qb]), (r.xr_r.at[qb], r.b_r.at[qb]))
    load((r.k_block, r.w_block))
    load((r.k_gin, r.w_gin))

    def write(buf, ref):
        one = copy(buf, ref)
        one.start()
        copies.append(one)

    def emit(value, buf, ref):
        buf[...] = value
        write(buf, ref)

    def chained(a, left, right):
        v = a.astype(F32) + jnp.where(z > 0, left.astype(F32), 0.0)
        return v + jnp.where(z < nz - 1, right.astype(F32), 0.0)

    def arrived(i):
        for one in loads[i]:
            one.wait()

    for b in range(6):
        arrived(b)
        ref = r.o_wup if b % 2 else r.o_wgate
        v = chained(r.a_f[b], r.b_f[b], r.c_f[b])
        emit(v, r.v_f.at[b], ref.at[:, b // 2 * FB : (b // 2 + 1) * FB])
    arrived(6)
    emit(chained(r.a_o[...], r.b_o[...], r.c_o[...]).T[0:L], r.v_o, r.o_wout)
    for qb in range(5):
        arrived(7 + qb)
        a, b = (r.a_d[qb], r.b_d[qb]) if qb < 3 else (r.a_r[qb - 3], r.b_r[qb - 3])
        v = a.astype(F32)
        for k in range(nx - 1):
            v = v + b[k].astype(F32)
        if qb < 3:
            emit(v.T, r.v_d.at[qb], r.o_wdown.at[qb * FB : (qb + 1) * FB])
        else:
            emit(v[:, 0:L], r.v_r.at[qb - 3], r.o_wgel if qb == 3 else r.o_wrec)

    arrived(12)
    write(r.w_block, r.o_block)
    arrived(13)
    write(r.w_gin, r.o_gin)
    part = L // nseq
    small = pltpu.roll(r.k_small[...], lax.rem(LP - s * part, LP), 1)
    r.o_cw[...] = small[0:4, 0:part]
    r.o_cb[...] = small[4, 0:part]
    r.o_ba[...] = small[5, 0:part]
    r.o_bx[...] = small[6, 0:part]
    r.o_lr[...] = small[7, 0:part]
    r.o_gm[...] = r.k_gain[0, :]
    r.o_gf[...] = r.k_gain[1, :]
    r.o_ga[...] = r.k_gates[0]
    r.o_gx[...] = r.k_gates[1]
    for one in copies:
        one.wait()


IN_ANY = ("x_in", "w_rec", "w_gel", "w_out", "gate_a", "gate_x", "w_gate", "w_up", "w_down", "cot")
IN_VMEM = (
    "ids", "gain_mix", "gain_ffn", "conv_weight", "conv_bias", "bias_a", "bias_x", "log_rate"
)
MID_VMEM = ("k_small", "k_gain", "k_gates")
LIMIT = 62 * 2**20


def space(in_vmem):
    return pl.BlockSpec(memory_space=pltpu.VMEM if in_vmem else pl.ANY)


def on_device(nseq, nm, *args):
    (
        block_input,
        segment_ids,
        gain_mix,
        w_rec,
        w_gel,
        conv_weight,
        conv_bias,
        gate_a,
        gate_x,
        bias_a,
        bias_x,
        log_rate,
        w_out,
        gain_ffn,
        w_gate,
        w_up,
        w_down,
        cotangent,
    ) = args
    B, G, D = block_input.shape
    T, L, F = B * G, w_rec.shape[1], w_gate.shape[1]
    nz = Z_CHIPS
    d = types.SimpleNamespace(
        B=B, G=G, T=T, D=D, L=L, F=F, LP=-(-L // 128) * 128, FB=F // 3, HW=gate_a.shape[0],
        DC=D // nseq, nseq=nseq, nm=nm, nz=nz, nx=nseq // nz, ny=nm // CORES, CB=256,
        nb=D // CORES // 256, taps=conv_weight.shape[0], GR=gate_a.shape[0] // nseq,
    )
    d.W = max(d.FB, d.LP)
    outs, scratch, sems = layout(d)
    feed = dict(
        x_in=block_input.reshape(T, D), w_rec=w_rec, w_gel=w_gel, w_out=w_out, gate_a=gate_a,
        gate_x=gate_x, w_gate=w_gate, w_up=w_up, w_down=w_down, cot=cotangent.reshape(T, D),
        ids=segment_ids, gain_mix=gain_mix, gain_ffn=gain_ffn, conv_weight=conv_weight,
        conv_bias=conv_bias, bias_a=bias_a, bias_x=bias_x, log_rate=log_rate,
    )
    names_in = IN_ANY + IN_VMEM
    names = names_in + tuple(outs) + tuple(scratch) + tuple(sems)

    def kernel(*refs):
        body(d, types.SimpleNamespace(**dict(zip(names, refs))))

    mid = pl.pallas_call(
        kernel,
        out_shape=[jax.ShapeDtypeStruct(*v) for v in outs.values()],
        in_specs=[space(n in IN_VMEM) for n in names_in],
        out_specs=[space(n in MID_VMEM) for n in outs],
        scratch_shapes=[pltpu.VMEM(*v) for v in scratch.values()]
        + [pltpu.SemaphoreType.DMA(v) for v in sems.values()],
        compiler_params=pltpu.CompilerParams(
            collective_id=0, has_side_effects=True, vmem_limit_bytes=LIMIT
        ),
        name="block",
    )(*[feed[n] for n in names_in])
    mid = dict(zip(outs, mid))
    for n in ("hz_d", "hz_r"):
        mid.pop(n)
    DC, FB, LP, GR, part = d.DC, d.FB, d.LP, d.GR, L // nseq
    last = dict(
        o_block=(T, D), o_gin=(T, D), o_gm=(DC,), o_wrec=(DC, L), o_wgel=(DC, L),
        o_cw=(d.taps, part), o_cb=(part,), o_ga=(GR, L), o_gx=(GR, L), o_ba=(part,), o_bx=(part,),
        o_lr=(part,), o_wout=(L, DC), o_gf=(DC,), o_wgate=(DC, F), o_wup=(DC, F), o_wdown=(F, DC),
    )
    large = ("o_block", "o_gin", "o_wrec", "o_wgel", "o_wout", "o_wgate", "o_wup", "o_wdown")
    buffers = dict(
        a_f=((6, DC, FB), BF16), b_f=((6, DC, FB), BF16), c_f=((6, DC, FB), BF16),
        a_o=((DC, LP), BF16), b_o=((DC, LP), BF16), c_o=((DC, LP), BF16),
        a_d=((3, DC, FB), BF16), b_d=((3, d.nx - 1, DC, FB), BF16),
        a_r=((2, DC, LP), BF16), b_r=((2, d.nx - 1, DC, LP), BF16),
        w_block=((T, D), F32), w_gin=((T, D), F32),
        v_f=((6, DC, FB), F32), v_o=((L, DC), F32), v_d=((3, FB, DC), F32), v_r=((2, DC, L), F32),
    )
    names_last = tuple(mid) + tuple(last) + tuple(buffers) + ("sem",)

    def last_kernel(*refs):
        finish(d, types.SimpleNamespace(**dict(zip(names_last, refs))))

    results = pl.pallas_call(
        last_kernel,
        out_shape=[jax.ShapeDtypeStruct(v, F32) for v in last.values()],
        in_specs=[space(n in MID_VMEM) for n in mid],
        out_specs=[space(n not in large) for n in last],
        scratch_shapes=[pltpu.VMEM(*v) for v in buffers.values()] + [pltpu.SemaphoreType.DMA((64,))],
        compiler_params=pltpu.CompilerParams(vmem_limit_bytes=LIMIT),
        name="finish",
    )(*mid.values())
    results = list(results)
    results[0] = results[0].reshape(B, G, D)
    results[1] = results[1].reshape(B, G, D)
    return tuple(results)


def solution(mesh):
    nseq, nm = mesh.shape["seq"], mesh.shape["mp"]
    rows, cols, both = P(None, "seq", None), P(None, "mp"), P(("mp", "seq"))
    part = P("seq", "mp")
    in_specs = (
        rows, P(), P(), cols, cols, cols, P("mp"), cols, cols, P("mp"), P("mp"), P("mp"),
        P("mp", None), P(), cols, cols, P("mp", None), rows,
    )
    out_specs = (
        rows, rows, P("seq"), part, part, P(None, ("mp", "seq")), both, part, part, both, both,
        both, P("mp", "seq"), P("seq"), part, part, P("mp", "seq"),
    )

    def step(*args):
        return on_device(nseq, nm, *args)

    return jax.shard_map(step, mesh=mesh, in_specs=in_specs, out_specs=out_specs, check_vma=False)
```

```python
import functools
import types

import jax
import jax.numpy as jnp
from jax import lax
from jax.experimental import pallas as pl
from jax.experimental.pallas import tpu as pltpu
from jax.sharding import PartitionSpec as P

EPS = 1e-06
RATE_SCALE = 8.0
Z_CHIPS = 4
CORES = 2
RING = 3
PAIRED = (1, 2)
GELU_C = 0.7978845608028654
GELU_A = 0.044715
MESH = pl.DeviceIdType.MESH
F32 = jnp.float32
BF16 = jnp.bfloat16

SCHEDULE = (
    (
        (),
        (),
        (),
        (),
    ),
    (
        (("P", 0, 1, 3), ("P", 0, 1, 2), ("P", 0, 1, 1),),
        (("F", 0, 0), ("F", 0, 2), ("F", 1, 0), ("F", 1, 2), ("F", 2, 0), ("F", 2, 2),),
        (("F", 0, 1), ("F", 0, 3), ("F", 1, 1), ("F", 1, 3), ("F", 2, 1), ("F", 2, 3),),
        (("P", 0, -1, 0), ("P", 0, -1, 1), ("P", 0, -1, 2),),
    ),
    (
        (("H", 1), ("H", 2), ("P", 3, 1, 3),),
        (("F", 0, 3), ("F", 1, 3), ("P", 0, 1, 3), ("P", 0, 1, 2), ("F", 2, 3), ("F", 3, 2),),
        (("F", 0, 0), ("F", 1, 0), ("P", 0, -1, 0), ("P", 0, -1, 1), ("F", 2, 0),),
        (("H", 1), ("H", 2),),
    ),
    (
        (("P", 3, 1, 2), ("P", 3, 1, 1),),
        (("F", 3, 0), ("P", 0, -1, 0), ("H", 1),),
        (("F", 3, 1),),
        (),
    ),
    (
        (("P", 4, 1, 3), ("P", 4, 1, 2), ("P", 4, 1, 1), ("P", 5, 1, 3), ("P", 5, 1, 2),),
        (("H", 2), ("P", 1, 1, 3), ("P", 1, 1, 2),),
        (("P", 0, 1, 3), ("F", 3, 3), ("H", 1), ("F", 3, 0), ("H", 2),),
        (("P", 3, -1, 0), ("P", 3, -1, 1), ("P", 3, -1, 2),),
    ),
    (
        (("P", 5, 1, 1),),
        (("F", 3, 3), ("P", 2, 1, 3), ("P", 2, 1, 2), ("P", 3, 1, 3), ("P", 3, 1, 2), ("F", 4, 2),),
        (("P", 1, 1, 3), ("P", 1, -1, 0), ("P", 1, -1, 1), ("P", 2, -1, 0), ("P", 2, -1, 1), ("P", 3, -1, 0), ("P", 3, -1, 1), ("F", 4, 1),),
        (("P", 4, -1, 0),),
    ),
    (
        (("Q", 0), ("Q", 1), ("Q", 2), ("O", 0), ("O", 1), ("O", 2), ("O", 3),),
        (("P", 4, 1, 3), ("P", 4, 1, 2), ("P", 1, -1, 0), ("P", 2, -1, 0), ("Q", 0), ("Q", 1), ("P", 5, 1, 3), ("Q", 2),),
        (("F", 4, 3), ("P", 2, 1, 3), ("Q", 0), ("P", 4, -1, 0), ("Q", 1), ("P", 3, 1, 3), ("Q", 2), ("O", 0),),
        (("P", 4, -1, 1), ("Q", 0), ("Q", 1), ("P", 4, -1, 2), ("Q", 2), ("O", 0), ("P", 5, -1, 0), ("O", 1), ("O", 2),),
    ),
    (
        (("P", 6, 1, 3), ("P", 6, 1, 2), ("P", 6, 1, 1), ("Q", 3), ("O", 4), ("O", 5), ("O", 6), ("Q", 4),),
        (("P", 5, 1, 2), ("P", 3, -1, 0), ("Q", 3), ("F", 4, 0), ("O", 0), ("O", 1), ("O", 2), ("O", 3), ("O", 4), ("O", 5), ("O", 6), ("F", 4, 3), ("Q", 4), ("P", 6, 1, 3), ("P", 4, -1, 0), ("P", 6, 1, 2), ("P", 5, -1, 0), ("P", 6, -1, 0),),
        (("P", 4, -1, 1), ("Q", 3), ("O", 1), ("O", 2), ("O", 3), ("P", 4, 1, 3), ("O", 4), ("O", 5), ("P", 5, -1, 0), ("O", 6), ("P", 5, -1, 1), ("P", 5, 1, 3), ("P", 6, -1, 0), ("F", 4, 0), ("P", 6, 1, 3), ("P", 6, -1, 1), ("Q", 4),),
        (("P", 5, -1, 1), ("P", 5, -1, 2), ("P", 6, -1, 0), ("P", 6, -1, 1), ("P", 6, -1, 2), ("Q", 3), ("O", 3), ("O", 4), ("O", 5), ("O", 6), ("Q", 4),),
    ),
)


def dot(left, right):
    return jnp.dot(left, right, preferred_element_type=F32)


def dot_nt(left, right):
    return lax.dot_general(left, right, (((1,), (1,)), ((), ())), preferred_element_type=F32)


def remote(src, dst, send_sem, recv_sem, device):
    return pltpu.make_async_remote_copy(
        src_ref=src,
        dst_ref=dst,
        send_sem=send_sem,
        recv_sem=recv_sem,
        device_id=device,
        device_id_type=MESH,
    )


def loop(count, body):
    def step(i, carry):
        body(i)
        return carry

    lax.fori_loop(0, count, step, 0)


def rows16(i, offset=0):
    return pl.ds(pl.multiple_of(i * 16 + offset, 16), 16)


def gelu_tanh(v):
    t = jnp.tanh(GELU_C * (v + GELU_A * (v * v * v)))
    return 0.5 * v * (1.0 + t)


def gelu_and_slope(v):
    square = v * v
    t = jnp.tanh(GELU_C * (v + GELU_A * (square * v)))
    half = 0.5 * (1.0 + t)
    slope = half + 0.5 * v * (1.0 - t * t) * (GELU_C * (1.0 + 3.0 * GELU_A * square))
    return v * half, slope


def minus_expm1(v):
    acc = 1.0 + v * (1.0 / 8.0)
    for n in (7.0, 6.0, 5.0, 4.0, 3.0, 2.0):
        acc = 1.0 + v * (1.0 / n) * acc
    return -v * acc


def softplus_small(v):
    u = jnp.exp(v)
    acc = 1.0 / 6.0 - u * (1.0 / 7.0)
    for n in (5.0, 4.0, 3.0, 2.0):
        acc = 1.0 / n - u * acc
    return u * (1.0 - u * acc)


def scan_tile(decay, value, reverse):
    row = lax.broadcasted_iota(jnp.int32, decay.shape, 0)
    for k in (1, 2, 4):
        shift = 8 - k if reverse else k
        valid = row < 8 - k if reverse else row >= k
        decay_k = pltpu.roll(decay, shift, 0)
        value_k = pltpu.roll(value, shift, 0)
        value = jnp.where(valid, decay * value_k + value, value)
        decay = jnp.where(valid, decay * decay_k, decay)
    return decay, value


def fold8(v):
    return v[0:8] + v[8:16]


def layout(dims):
    d = dims
    T, D, L, LP, F, FB, DC = d.T, d.D, d.L, d.LP, d.F, d.FB, d.DC
    B, G, HW = d.B, d.G, d.HW
    outs = dict(
        k_block=((T, D), BF16),
        k_gin=((T, D), BF16),
        k_small=((8, LP), F32),
        k_gain=((8, DC), F32),
        k_gates=((2, d.GR, L), F32),
        own_f=((6, DC, FB), BF16),
        own_o=((DC, LP), BF16),
        own_d=((3, DC, FB), BF16),
        own_r=((2, DC, LP), BF16),
        land_f=((6, 2 * (d.nz - 1), DC, FB), BF16),
        land_o=((2 * (d.nz - 1), DC, LP), BF16),
        xr_d=((3, d.nx - 1, DC, FB), BF16),
        xr_r=((2, d.nx - 1, DC, LP), BF16),
        hz_d=((3, d.nz, T, FB), BF16),
        hz_r=((2, d.nz, T, LP), BF16),
    )
    scratch = dict(
        x_v=((T, D), BF16),
        cot_v=((T, D), BF16),
        xh=((B * 16, D), BF16),
        scm=((T, 128), F32),
        scf=((T, 128), F32),
        idp=((8, 2 * G), jnp.int32),
        mk=((B, G + 8, 128), F32),
        rv=((8, L), F32),
        wl=((2, HW, L), BF16),
        wo=((2, LP, L), BF16),
        wr=((2, HW, L), BF16),
        extp=((B, 16 + G, L), F32),
        cv=((T, LP), BF16),
        st_l=((T, HW), BF16),
        st_r=((T, HW), BF16),
        hl=((T, HW), BF16),
        hr=((T, HW), BF16),
        pre_gel=((T, L), F32),
        recur=((T, L), F32),
        inj=((T, L), F32),
        cfp=((B, G + 8, L), F32),
        aloc=((T, L), F32),
        stp=((B, 8 + G, L), F32),
        pk=((2, 2 * B, L), F32),
        pf=((2, d.nseq, 2 * B, L), F32),
        resid=((T, D), F32),
        csend=((d.nb, T, d.CB), F32),
        cland=((d.nb, T, d.CB), F32),
        tot=((2 * d.nb, T, d.CB), F32),
        yl=((2, d.ny, d.nb, T, d.CB), BF16),
        fo=((2 * d.nb, T, d.CB), BF16),
        hd=((3, T, FB), BF16),
        gp=((6, d.nx, T, FB), BF16),
        mx=((d.nx, T, LP), BF16),
        gpg=((T, LP), BF16),
        gpr=((T, LP), BF16),
        nmT=((d.nz, d.nx, DC, T), BF16),
        cotT=((d.nz, d.nx, DC, T), BF16),
        nfT=((d.nz, d.nx, DC, T), BF16),
        gbT=((d.nz, d.nx, DC, T), BF16),
        ez=((2, d.nx, DC, d.nz * T), BF16),
        ex=((2, d.nz, DC, d.nx * T), BF16),
        vecs=((8, L), F32),
        gains=((8, D), F32),
        he=((len(PAIRED), d.nx, T, FB), BF16),
        ee=((d.nz - 1, DC, d.nx * T), BF16),
        gacc=((16, D), F32),
        gsend=((d.nseq, 8, DC), F32),
        gland=((d.nseq, 8, DC), F32),
        sacc=((8, 8, L), F32),
        smv=((8, L), F32),
        smx=((d.nx, 8, L), F32),
        smz=((d.nz, 8, L), F32),
        gt=((d.nz, d.nx, 2, d.GR, L), BF16),
        gtx=((d.nx, d.nz, 2, d.GR, L), BF16),
        gtz=((d.nz, 2, d.GR, L), BF16),
        gts=((d.nz, 2, d.GR, L), BF16),
        gs_l=((T, HW), BF16),
        gs_r=((T, HW), BF16),
        gi_l=((T, HW), BF16),
        gi_r=((T, HW), BF16),
        sp_s=((B * 8, L), F32),
        sp_r=((B * 8, L), F32),
    )
    sems = dict(
        ld=(16,),
        halo_s=(B,),
        halo_r=(B,),
        ex_s=(4 * B,),
        ex_r=(4 * B,),
        gi_s=(2,),
        gi_rs=(2,),
        pf_s=(2, d.nseq),
        pf_r=(2, d.nseq),
        c_s=(4, d.nb),
        c_r=(4, d.nb),
        y_s=(4, d.ny, d.nb),
        y_r=(4, d.ny, d.nb),
        a_s=(4, d.nb),
        a_r=(4, d.nb),
        ez_s=(2, d.nz),
        ez_r=(2, d.nz),
        ezc_s=(2, d.nz),
        ezc_r=(2, d.nz),
        ex_xs=(2, d.nx),
        ex_xr=(2, d.nx),
        exc_s=(2, d.nx),
        exc_r=(2, d.nx),
        own_l=(4,),
        ee_s=(d.nx,),
        ee_r=(d.nx,),
        eec_s=(d.nx,),
        eec_r=(d.nx,),
        he_s=(len(PAIRED), d.nx),
        he_r=(len(PAIRED), d.nx),
        hz_s=(5, d.nz, 2),
        hz_rs=(5, d.nz),
        hx_s=(7, d.nx),
        hx_r=(7, d.nx),
        xr_s=(5, d.nx),
        xr_rs=(5, d.nx),
        p_s=(7, d.nz),
        p_r=(7, 2 * (d.nz - 1)),
        smx_s=(d.nx,),
        smx_r=(d.nx,),
        smz_s=(d.nz,),
        smz_r=(d.nz,),
        ga_s=(d.nseq,),
        ga_r=(d.nseq,),
        gtx_s=(d.nx,),
        gtx_r=(d.nx,),
        gtz_s=(d.nz,),
        gtz_r=(d.nz,),
        sp_ss=(1,),
        sp_rs=(1,),
        pl_s=(2,),
        ow=(16,),
    )
    return outs, scratch, sems


def body(d, r):
    T, D, L, LP, F, FB, DC = d.T, d.D, d.L, d.LP, d.F, d.FB, d.DC
    B, G, HW, CB, nb = d.B, d.G, d.HW, d.CB, d.nb
    nseq, nz, nx, ny, nm = d.nseq, d.nz, d.nx, d.ny, d.nm
    s, m = lax.axis_index("seq"), lax.axis_index("mp")
    z, x = lax.div(s, nx), lax.rem(s, nx)
    y, c = lax.div(m, CORES), lax.rem(m, CORES)
    partner = (s, y * CORES + 1 - c)
    left_m, right_m = lax.rem(m + nm - 1, nm), lax.rem(m + 1, nm)
    pending = []

    def later(make, when=None):
        pending.append((make, when))

    def start(make, when=None):
        if when is None:
            make().start()
        else:
            pl.when(when())(lambda: make().start())
        pending.append((make, when))

    barrier = pltpu.get_barrier_semaphore()
    for k in range(1, nseq):
        pl.semaphore_signal(
            barrier, inc=1, device_id=(lax.rem(s + k, nseq), m), device_id_type=MESH
        )
    for k in range(1, nm):
        pl.semaphore_signal(barrier, inc=1, device_id=(s, lax.rem(m + k, nm)), device_id_type=MESH)

    def local(src, dst, i):
        copy = pltpu.make_async_copy(src, dst, r.ld.at[i])
        copy.start()
        return copy

    ld_x = local(r.x_in, r.x_v, 0)
    ld_cot = local(r.cot, r.cot_v, 8)

    half = nb * CB

    def psum_start(k, part):
        par = k % 2

        def send_half(j):
            r.csend[j] = part((1 - c) * half + j * CB)
            remote(r.csend.at[j], r.cland.at[j], r.c_s.at[k, j], r.c_r.at[k, j], partner).start()

        loop(nb, send_half)

        def own_half(j):
            v = part(c * half + j * CB)
            remote(
                r.csend.at[j], r.cland.at[j], r.c_s.at[k, j], r.c_r.at[k, j], partner
            ).wait_recv()
            r.yl[par, y, j] = (v + r.cland[j]).astype(BF16)
            for q in range(1, ny):
                to = lax.rem(y + q, ny)
                remote(
                    r.yl.at[par, y, j],
                    r.yl.at[par, y, j],
                    r.y_s.at[k, q, j],
                    r.y_r.at[k, q, j],
                    (s, to * CORES + c),
                ).start()

        loop(nb, own_half)

    def psum_finish(k):
        par = k % 2

        def total(j):
            for q in range(1, ny):
                src = lax.rem(y + ny - q, ny)
                remote(
                    r.yl.at[par, src, j],
                    r.yl.at[par, src, j],
                    r.y_s.at[k, q, j],
                    r.y_r.at[k, q, j],
                    partner,
                ).wait_recv()
            v = r.yl[par, 0, j].astype(F32)
            for q in range(1, ny):
                v = v + r.yl[par, q, j].astype(F32)
            at = c * nb + j
            r.tot[at] = v
            remote(r.tot.at[at], r.tot.at[at], r.a_s.at[k, j], r.a_r.at[k, j], partner).start()

        loop(nb, total)

        def close(j):
            at = (1 - c) * nb + j
            remote(
                r.tot.at[at], r.tot.at[at], r.a_s.at[k, j], r.a_r.at[k, j], partner
            ).wait()
            remote(
                r.csend.at[j], r.cland.at[j], r.c_s.at[k, j], r.c_r.at[k, j], partner
            ).wait_send()
            for q in range(1, ny):
                remote(
                    r.yl.at[par, y, j],
                    r.yl.at[par, y, j],
                    r.y_s.at[k, q, j],
                    r.y_r.at[k, q, j],
                    partner,
                ).wait_send()

        loop(nb, close)

    def pairs_send(k):
        for q in range(1, nseq):
            start(
                lambda q=q: remote(
                    r.pk.at[k],
                    r.pf.at[k, s],
                    r.pf_s.at[k, q],
                    r.pf_r.at[k, q],
                    (s + q if k == 0 else s - q, m),
                ),
                lambda q=q: s + q < nseq if k == 0 else s - q >= 0,
            )

    def pairs_enter(k, reverse):
        for q in range(1, nseq):
            src = s + q if reverse else s - q

            @pl.when(src < nseq if reverse else src >= 0)
            def _(q=q, src=src):
                remote(
                    r.pk.at[k], r.pf.at[k, src], r.pf_s.at[k, q], r.pf_r.at[k, q], partner
                ).wait_recv()

        value = jnp.zeros((B, L), F32)
        for q in range(nseq - 1):
            at = nseq - 1 - q if reverse else q
            pair = r.pf[k, at]
            new = pair[0:B] * value + pair[B : 2 * B]
            value = jnp.where(at > s if reverse else at < s, new, value)
        return value

    def transposed(src, dst):
        def one(j):
            dst[lax.div(j, nx), lax.rem(j, nx)] = src[:, pl.ds(pl.multiple_of(j * DC, DC), DC)].T

        loop(nseq, one)

    def lanes(i):
        return pl.ds(pl.multiple_of(i * T, T), T)

    ez_half, ex_half = DC // CORES, nz // CORES

    def ez_part(e, src_z, core):
        rows = pl.ds(pl.multiple_of(core * ez_half, ez_half), ez_half)
        return r.ez.at[e, :, rows, lanes(src_z)]

    def ez_own(e):
        src = r.nmT if e else r.cotT
        return pltpu.make_async_copy(src.at[z], r.ez.at[e, :, :, lanes(z)], r.own_l.at[e])

    def ez_copy(e, k):
        to = lax.rem(z + k, nz)
        rows = pl.ds(pl.multiple_of(c * ez_half, ez_half), ez_half)
        return remote(
            (r.nmT if e else r.cotT).at[to, :, rows],
            ez_part(e, z, c),
            r.ez_s.at[e, k],
            r.ez_r.at[e, k],
            (to * nx + x, m),
        )

    def ez_relay_copy(e, k):
        part = ez_part(e, lax.rem(z + nz - k, nz), c)
        return remote(part, part, r.ezc_s.at[e, k], r.ezc_r.at[e, k], partner)

    def ez_send(e, left):
        for k in range(1, nz):
            if left:
                start(functools.partial(ez_copy, e, k), lambda k=k: z + k >= nz)
            else:
                start(functools.partial(ez_copy, e, k), lambda k=k: z + k < nz)

    def ez_relay(e):
        for k in range(1, nz):
            part = ez_part(e, lax.rem(z + nz - k, nz), c)
            remote(part, part, r.ez_s.at[e, k], r.ez_r.at[e, k], partner).wait_recv()
            start(functools.partial(ez_relay_copy, e, k))

    def ez_wait(e):
        ez_own(e).wait()
        for k in range(1, nz):
            part = ez_part(e, lax.rem(z + nz - k, nz), 1 - c)
            remote(part, part, r.ezc_s.at[e, k], r.ezc_r.at[e, k], partner).wait_recv()

    def ex_part(e, src_x, core):
        return r.ex.at[e, pl.ds(core * ex_half, ex_half), :, lanes(src_x)]

    def ex_own(e):
        src = r.gbT if e else r.nfT
        return pltpu.make_async_copy(src.at[:, x], r.ex.at[e, :, :, lanes(x)], r.own_l.at[2 + e])

    def ex_copy(e, k):
        to = lax.rem(x + k, nx)
        return remote(
            (r.gbT if e else r.nfT).at[pl.ds(c * ex_half, ex_half), to],
            ex_part(e, x, c),
            r.ex_xs.at[e, k],
            r.ex_xr.at[e, k],
            (z * nx + to, m),
        )

    def ex_relay_copy(e, k):
        part = ex_part(e, lax.rem(x + nx - k, nx), c)
        return remote(part, part, r.exc_s.at[e, k], r.exc_r.at[e, k], partner)

    def ex_send(e):
        ex_own(e).start()
        for k in range(1, nx):
            start(functools.partial(ex_copy, e, k))

    def ex_relay(e):
        for k in range(1, nx):
            part = ex_part(e, lax.rem(x + nx - k, nx), c)
            remote(part, part, r.ex_xs.at[e, k], r.ex_xr.at[e, k], partner).wait_recv()
            start(functools.partial(ex_relay_copy, e, k))

    def ex_wait(e):
        ex_own(e).wait()
        for k in range(1, nx):
            part = ex_part(e, lax.rem(x + nx - k, nx), 1 - c)
            remote(part, part, r.exc_s.at[e, k], r.exc_r.at[e, k], partner).wait_recv()

    at_end_of_line = (z == 0) | (z == nz - 1)
    inner = jnp.where(z == 0, 1, nz - 2)

    def ee_part(src_x, core):
        rows = pl.ds(pl.multiple_of(core * ez_half, ez_half), ez_half)
        return r.ee.at[:, rows, lanes(src_x)]

    def ee_copy(to_x):
        rows = pl.ds(pl.multiple_of(c * ez_half, ez_half), ez_half)
        chunks = pl.ds(jnp.where(z == 0, 1, 0), nz - 1)
        return remote(
            r.nfT.at[chunks, to_x, rows],
            ee_part(x, c),
            r.ee_s.at[to_x],
            r.ee_r.at[x],
            (inner * nx + to_x, m),
        )

    def ee_relay_copy(src_x):
        part = ee_part(src_x, c)
        return remote(part, part, r.eec_s.at[src_x], r.eec_r.at[src_x], partner)

    def ee_send():
        for to_x in range(nx):
            start(functools.partial(ee_copy, to_x), lambda: at_end_of_line)

    def ee_relay(src_x):
        part = ee_part(src_x, c)
        remote(part, part, r.ee_s.at[src_x], r.ee_r.at[src_x], partner).wait_recv()
        ee_relay_copy(src_x).start()

    def ee_wait():
        for src_x in range(nx):
            part = ee_part(src_x, 1 - c)
            remote(part, part, r.eec_s.at[src_x], r.eec_r.at[src_x], partner).wait_recv()

    def q_own(qb):
        return r.hd.at[qb] if qb < 3 else (r.gpg if qb == 3 else r.gpr)

    def q_land(qb, zo):
        return r.hz_d.at[qb, zo] if qb < 3 else r.hz_r.at[qb - 3, zo]

    def q_copy(qb, src, zo, way):
        to = s + nx if way == 0 else s - nx
        return remote(src, q_land(qb, zo), r.hz_s.at[qb, zo, way], r.hz_rs.at[qb, zo], (to, m))

    def q_send(qb):
        start(lambda: q_copy(qb, q_own(qb), z, 0), lambda: z < nz - 1)
        start(lambda: q_copy(qb, q_own(qb), z, 1), lambda: z > 0)

    def hx_ref(pb):
        return r.gp.at[pb] if pb < 6 else r.mx

    def hx_send(pb):
        def copy(k):
            to = lax.rem(x + k, nx)
            return remote(
                hx_ref(pb).at[x],
                hx_ref(pb).at[x],
                r.hx_s.at[pb, k],
                r.hx_r.at[pb, k],
                (z * nx + to, m),
            )

        for k in range(1, nx):
            start(functools.partial(copy, k))

    def hx_wait(pb):
        for k in range(1, nx):
            src = lax.rem(x + nx - k, nx)
            remote(
                hx_ref(pb).at[src],
                hx_ref(pb).at[src],
                r.hx_s.at[pb, k],
                r.hx_r.at[pb, k],
                partner,
            ).wait_recv()

    r.vecs[0 : d.taps] = r.conv_weight[...]
    for row, vector in enumerate((r.conv_bias, r.bias_a, r.bias_x, r.log_rate)):
        r.vecs[d.taps + row : d.taps + row + 1] = vector[...].reshape(1, L)
    r.gains[0:1] = r.gain_mix[...].reshape(1, D)
    r.gains[1:2] = r.gain_ffn[...].reshape(1, D)
    own_ids = r.ids[:, pl.ds(pl.multiple_of(s * G, G), G)]
    before = r.ids[:, pl.ds(pl.multiple_of(jnp.maximum(s - 1, 0) * G, G), G)]
    r.idp[...] = jnp.zeros((8, 2 * G), jnp.int32)
    r.idp[0:B, 0:G] = jnp.where(s > 0, before, -1)
    r.idp[0:B, G : 2 * G] = own_ids
    both = r.idp[...]
    square_row = lax.broadcasted_iota(jnp.int32, (G, G), 0)
    same = [
        jnp.where(pltpu.roll(both, k, 1)[:, G:] == both[:, G:], 1.0, 0.0) for k in range(1, d.taps)
    ]
    for b in range(B):
        square = jnp.zeros((G, G), F32)
        for k in range(1, d.taps):
            square = jnp.where(
                square_row == k, jnp.broadcast_to(same[k - 1][b : b + 1], (G, G)), square
            )
        r.mk[b, 0:G, :] = square.T
        r.mk[b, G : G + 8, :] = jnp.zeros((8, 128), F32)
    rates = r.vecs[7:8]
    r.rv[0:1] = -RATE_SCALE * softplus_small(rates)
    r.rv[1:2] = -RATE_SCALE * jax.nn.sigmoid(rates)
    r.sacc[...] = jnp.zeros((8, 8, L), F32)

    base = L * m + HW // 4
    shift = HW.bit_length() - 1
    turn = lax.rem(base, HW)
    turn_right = lax.rem(base + L, HW)

    def head_mask(first, count):
        row = lax.broadcasted_iota(jnp.int32, (count, L), 0) + first
        col = lax.broadcasted_iota(jnp.int32, (count, L), 1) + base
        return lax.shift_right_arithmetic(row, shift) == lax.shift_right_arithmetic(col, shift)

    pieces = [(p, min(HW, LP - p)) for p in range(0, LP, HW)]

    def recurrent_forward(wrec_v, wgel_v, wout_v, nm_v, nmh, pa, px, g2):
        ld_gel = local(r.w_gel, wgel_v, 1)
        ld_rec = local(r.w_rec, wrec_v, 2)
        ld_g = [
            local(gate, g2.at[i, pl.ds(at * HW, HW)], 3 + 2 * i + at)
            for i, gate in enumerate((r.gate_a, r.gate_x))
            for at in range(2)
        ]
        ld_out = local(r.w_out, wout_v, 7)
        ld_x.wait()

        def norm(i):
            at = rows16(i)
            v = r.x_v[at, :].astype(F32)
            scale = lax.rsqrt(jnp.mean(v * v, axis=1, keepdims=True) + EPS)
            nm_v[at, :] = (v * scale * r.gains[0:1]).astype(BF16)
            r.scm[at, :] = jnp.broadcast_to(scale, (16, 128))

        loop(T // 16, norm)
        ld_gel.wait()
        r.pre_gel[...] = dot(nm_v[...], wgel_v[...])
        ld_rec.wait()
        main = dot(nm_v[...], wrec_v[...]).astype(BF16).astype(F32)
        for b in range(B):
            r.extp[b, 16 : 16 + G, :] = main[b * G : (b + 1) * G]

        if LP > L:
            for wide in (r.cv, r.gpg, r.gpr, r.mx.at[x]):
                wide[:, L:] = jnp.zeros((T, LP - L), BF16)

        def conv(i):
            for b in range(B):
                window = r.extp[b, pl.ds(pl.multiple_of(i * 16 + 8, 8), 24), :]
                keep = r.mk[b, rows16(i), :]
                acc = r.vecs[4:5] + r.vecs[0:1] * window[8:24]
                for k in range(1, d.taps):
                    acc = acc + r.vecs[k : k + 1] * (keep[:, k : k + 1] * window[8 - k : 24 - k])
                at = rows16(i, b * G)
                r.cv[at, 0:L] = acc.astype(BF16)
                r.st_l[at, :] = acc[:, :HW].astype(BF16)
                r.st_r[at, :] = acc[:, L - HW :].astype(BF16)

        def neighbours(b, side, first):
            rows = pl.ds(b * G, 16) if first else pl.ds(b * G + 16, G - 16)
            src, dst, to = (r.st_r, r.hl, right_m) if side else (r.st_l, r.hr, left_m)
            i = 4 * b + 2 * side + first
            return remote(src.at[rows], dst.at[rows], r.ex_s.at[i], r.ex_r.at[i], (s, to))

        loop(G // 16 - 1, lambda i: conv(i + 1))
        ld_cot.wait()
        transposed(r.cot_v, r.cotT)
        pl.semaphore_wait(barrier, nseq - 1 + nm - 1)

        for b in range(B):
            start(
                lambda b=b: remote(
                    r.x_in.at[pl.ds(b * G + G - 16, 16)],
                    r.xh.at[pl.ds(b * 16, 16)],
                    r.halo_s.at[b],
                    r.halo_r.at[b],
                    (s + 1, m),
                ),
                lambda: s < nseq - 1,
            )

        for b in range(B):
            for side in range(2):
                start(functools.partial(neighbours, b, side, 0))

        @pl.when(s > 0)
        def _():
            for b in range(B):
                remote(
                    r.x_in.at[pl.ds(b * G + G - 16, 16)],
                    r.xh.at[pl.ds(b * 16, 16)],
                    r.halo_s.at[b],
                    r.halo_r.at[b],
                    partner,
                ).wait_recv()

        @pl.when(s == 0)
        def _():
            r.xh[...] = jnp.zeros((B * 16, D), BF16)

        for b in range(B):
            v = r.xh[b * 16 : (b + 1) * 16, :].astype(F32)
            scale = lax.rsqrt(jnp.mean(v * v, axis=1, keepdims=True) + EPS)
            nmh[b * 16 : (b + 1) * 16, :] = (v * scale * r.gains[0:1]).astype(BF16)
        rim = dot(nmh[...], wrec_v[...]).astype(BF16).astype(F32)
        for b in range(B):
            r.extp[b, 0:16, :] = rim[b * 16 : (b + 1) * 16]

        conv(0)
        for b in range(B):
            for side in range(2):
                start(functools.partial(neighbours, b, side, 1))

        for copy in ld_g:
            copy.wait()
        for i in range(2):
            table = g2[i, pl.ds(pl.multiple_of(turn, HW // 4), HW), :].astype(F32)
            table_right = g2[i, pl.ds(pl.multiple_of(turn_right, HW // 4), HW), :].astype(F32)
            r.wl[i] = jnp.where(head_mask(base - HW, HW), table, 0.0).astype(BF16)
            r.wr[i] = jnp.where(head_mask(base + L, HW), table_right, 0.0).astype(BF16)
            for p, n in pieces:
                r.wo[i, p : p + n, :] = jnp.where(head_mask(base + p, n), table[:n], 0.0).astype(
                    BF16
                )
        pa[...] = dot(r.cv[...], r.wo[0]) + r.vecs[5:6]
        px[...] = dot(r.cv[...], r.wo[1]) + r.vecs[6:7]
        for i in range(4 * B):
            neighbours(i // 4, i // 2 % 2, i % 2).wait_recv()
        pa[...] += dot(r.hl[...], r.wl[0]) + dot(r.hr[...], r.wr[0])
        px[...] += dot(r.hl[...], r.wl[1]) + dot(r.hr[...], r.wr[1])

        def scan(i, carry):
            out = []
            for b in range(B):
                decay_in, state_in = carry[2 * b], carry[2 * b + 1]
                at = rows16(i, b * G)
                recur = jax.nn.sigmoid(pa[at, :])
                inject = jax.nn.sigmoid(px[at, :])
                log_decay = r.rv[0:1] * recur
                decay = jnp.exp(log_decay)
                spread = jnp.sqrt(minus_expm1(2.0 * log_decay))
                drive = spread * inject * r.cv[at, 0:L].astype(F32)
                coeff = decay * r.mk[b, rows16(i), :][:, 1:2]
                r.recur[at, :] = recur
                r.inj[at, :] = inject
                r.cfp[b, rows16(i), :] = coeff
                for h in range(2):
                    a, v = scan_tile(
                        coeff[8 * h : 8 * h + 8], drive[8 * h : 8 * h + 8], reverse=False
                    )
                    v = v + a * state_in
                    a = a * decay_in
                    decay_in, state_in = a[7:8], v[7:8]
                    r.aloc[pl.ds(pl.multiple_of(b * G + i * 16 + 8 * h, 8), 8), :] = a
                    r.stp[b, pl.ds(pl.multiple_of(8 + i * 16 + 8 * h, 8), 8), :] = v
                out += [decay_in, state_in]
            return tuple(out)

        one, zero = jnp.ones((1, L), F32), jnp.zeros((1, L), F32)
        ends = lax.fori_loop(0, G // 16, scan, (one, zero) * B)
        for b in range(B):
            r.pk[0, b : b + 1, :] = ends[2 * b]
            r.pk[0, B + b : B + b + 1, :] = ends[2 * b + 1]
            r.cfp[b, G : G + 8, :] = jnp.ones((8, L), F32)
        pairs_send(0)
        transposed(nm_v, r.nmT)
        for e in range(2):
            ez_own(e).start()
            ez_send(e, True)
        entered = pairs_enter(0, False)
        for b in range(B):
            r.stp[b, 0:8, :] = jnp.broadcast_to(entered[b : b + 1], (8, L))

        def states(i):
            for b in range(B):
                at = rows16(i, b * G)
                here = pl.ds(pl.multiple_of(8 + i * 16, 8), 16)
                state = r.stp[b, here, :] + r.aloc[at, :] * r.stp[b, 7:8, :]
                r.stp[b, here, :] = state
                r.mx[x, at, 0:L] = (state * gelu_tanh(r.pre_gel[at, :])).astype(BF16)

        loop(G // 16, states)
        ld_out.wait()
        psum_start(
            0,
            lambda col: dot(r.mx[x, :, 0:L], wout_v[:, pl.ds(pl.multiple_of(col, CB), CB)]),
        )
        hx_send(6)

    pl.run_scoped(
        recurrent_forward,
        pltpu.VMEM((D, L), BF16),
        pltpu.VMEM((D, L), BF16),
        pltpu.VMEM((L, D), BF16),
        pltpu.VMEM((T, D), BF16),
        pltpu.VMEM((B * 16, D), BF16),
        pltpu.VMEM((T, L), F32),
        pltpu.VMEM((T, L), F32),
        pltpu.VMEM((2, 2 * HW, L), BF16),
    )

    def feed_forward(wd_v, wg_v, wu_v, nf, gh, pg, pu):
        ld_d = [local(r.w_down.at[pl.ds(i * FB, FB)], wd_v.at[i], i) for i in range(3)]
        ld_g = [local(r.w_gate.at[:, pl.ds(i * FB, FB)], wg_v.at[i], 3 + i) for i in range(3)]
        ld_u = [local(r.w_up.at[:, pl.ds(i * FB, FB)], wu_v.at[i], 6 + i) for i in range(3)]
        for i in range(3):
            ld_d[i].wait()

        def hidden_grad(i):
            gh[i] = dot_nt(r.cot_v[...], wd_v[i])

        loop(3, hidden_grad)
        for e in range(2):
            ez_send(e, False)
        psum_finish(0)

        def residual(i):
            at = rows16(i)
            parts = [
                r.tot[j, at, :] + r.x_v[at, j * CB : (j + 1) * CB].astype(F32)
                for j in range(2 * nb)
            ]
            square = parts[0] * parts[0]
            for v in parts[1:]:
                square = square + v * v
            scale = lax.rsqrt(jnp.sum(square, axis=1, keepdims=True) / D + EPS)
            for j, v in enumerate(parts):
                cols = slice(j * CB, (j + 1) * CB)
                r.resid[at, cols] = v
                nf[at, cols] = (v * scale * r.gains[1:2, cols]).astype(BF16)
            r.scf[at, :] = jnp.broadcast_to(scale, (16, 128))

        loop(T // 16, residual)
        for i in range(3):
            ld_g[i].wait()
            ld_u[i].wait()

        for i in range(3):
            pg[...] = dot(nf[...], wg_v[i])
            pu[...] = dot(nf[...], wu_v[i])

            def units(t, i=i):
                at = rows16(t)
                up, back = pu[at, :], gh[i, at, :]
                active, slope = gelu_and_slope(pg[at, :])
                r.hd[i, at, :] = (active * up).astype(BF16)
                r.gp[2 * i, x, at, :] = (back * up * slope).astype(BF16)
                r.gp[2 * i + 1, x, at, :] = (back * active).astype(BF16)

            loop(T // 16, units)
            q_send(i)
            if i == 0:
                transposed(nf, r.nfT)
                ex_send(0)
            if i < 2:
                hx_send(2 * i)
            if i == 0:
                hx_send(1)

        def back_input(col):
            at = pl.ds(pl.multiple_of(col, CB), CB)
            v = dot_nt(r.gp[0, x], wg_v[0, at, :]) + dot_nt(r.gp[1, x], wu_v[0, at, :])
            for i in range(1, 3):
                v = v + dot_nt(r.gp[2 * i, x], wg_v[i, at, :])
                v = v + dot_nt(r.gp[2 * i + 1, x], wu_v[i, at, :])
            return v

        psum_start(1, back_input)

        def ffn_term(j):
            at = pl.ds(pl.multiple_of(j * CB, CB), CB)
            v = dot(r.hd[0], wd_v[0, :, at])
            for i in range(1, 3):
                v = v + dot(r.hd[i], wd_v[i, :, at])
            r.fo[j] = v.astype(BF16)

        loop(2 * nb, ffn_term)
        ex_relay(0)
        ez_relay(0)
        ez_relay(1)

    pl.run_scoped(
        feed_forward,
        pltpu.VMEM((3, FB, D), BF16),
        pltpu.VMEM((3, D, FB), BF16),
        pltpu.VMEM((3, D, FB), BF16),
        pltpu.VMEM((T, D), BF16),
        pltpu.VMEM((3, T, FB), F32),
        pltpu.VMEM((T, FB), F32),
        pltpu.VMEM((T, FB), F32),
    )

    def gain_rows(which):
        total = jnp.sum(r.gacc[...], axis=0, keepdims=True)
        for q in range(nseq):
            r.gsend[q, which : which + 1, :] = total[:, q * DC : (q + 1) * DC]

    def after_feed_forward(stage_f, load_f, own_st, hload, qstage):
        tail = []
        seen = [dict() for _ in range(nz)]

        def once(zz, *what):
            first = what not in seen[zz]
            seen[zz][what] = True
            return first

        def at_end(zz, make):
            seen[zz].setdefault("sent", []).append(make)

        def sized(ref, n):
            return ref if n == ref.shape[-1] else ref.at[:, pl.ds(0, n)]

        def own_write(zz, src, ref):
            turn_ = seen[zz].get("turn", 0)
            seen[zz]["turn"] = turn_ + 1
            at, n = turn_ % 2, src.shape[-1]

            def copy():
                return pltpu.make_async_copy(sized(own_st.at[at], n), ref(), r.ow.at[4 + at])

            held = seen[zz].setdefault("held", {})
            if at in held:
                held[at]().wait()
            sized(own_st.at[at], n)[...] = src.astype(BF16)
            copy().start()
            held[at] = copy

        def p_width(b):
            return FB if b < 6 else LP

        def p_stage(zz, b, zc):
            at = zc if zc < zz else zc - 1
            return stage_f.at[b % RING, at] if b < 6 else tail[0].at[at]

        def p_land(b, place):
            return r.land_f.at[b, place] if b < 6 else r.land_o.at[place]

        def p_part(zz, b, zc):
            if once(zz, "hx", b):
                hx_wait(b)
            e = 0 if b < 6 else 1
            if once(zz, "ex", e):
                ex_wait(e)
            v = dot(r.ex[e, zc], hx_ref(b)[...].reshape(nx * T, p_width(b)))
            if b in PAIRED and 0 < zz < nz - 1:
                end_side = zc >= zz if zz == 1 else zc <= zz
                if end_side:
                    for k in range(1, nx):
                        if once(zz, "he", b, k):
                            src = lax.rem(x + nx - k, nx)
                            he_forward(b, k, src).wait_recv()
                    if once(zz, "ee"):
                        for src_x in range(nx):
                            ee_relay(src_x)
                            at_end(zz, lambda k=src_x: ee_relay_copy(k).wait_send())
                        ee_wait()
                    v = v + dot(
                        r.ee[zc - 1 if zz == 1 else zc],
                        r.he[PAIRED.index(b)].reshape(nx * T, FB),
                    )
            return v

        def he_copy(b):
            block = PAIRED.index(b)
            return remote(
                r.gp.at[b, x],
                r.he.at[block, x],
                r.he_s.at[block, 0],
                r.he_r.at[block, 0],
                (inner * nx + x, m),
            )

        def he_forward(b, k, src):
            block = PAIRED.index(b)
            to = lax.rem(x + k, nx)
            return remote(
                r.he.at[block, src],
                r.he.at[block, src],
                r.he_s.at[block, k],
                r.he_r.at[block, k],
                (z * nx + to, m),
            )

        def do_operand(zz, b):
            if zz in (0, nz - 1):
                he_copy(b).start()
                at_end(zz, lambda: he_copy(b).wait_send())
            else:
                he_copy(b).wait_recv()
                for k in range(1, nx):
                    he_forward(b, k, x).start()
                    at_end(zz, lambda k=k: he_forward(b, k, x).wait_send())

        def p_copy(zz, b, zc, place, to):
            return remote(
                p_stage(zz, b, zc), p_land(b, place), r.p_s.at[b, zc], r.p_r.at[b, place], (to, m)
            )

        def do_p(zz, b, way, zc):
            right = way > 0
            has_input = zz > 0 if right else zz < nz - 1
            if b in PAIRED and zz == (1 if right else nz - 2):
                has_input = False
            place = abs(zc - zz) + (0 if right else nz - 1)
            load = load_f if b < 6 else tail[1]
            if has_input:
                fetch = pltpu.make_async_copy(p_land(b, place), load, r.pl_s.at[0])
                p_copy(zz, b, zc, place, s).wait_recv()
                fetch.start()
            v = p_part(zz, b, zc)
            if has_input:
                fetch.wait()
                v = v + load[...].astype(F32)
            if ("out", b - RING, zc) in seen[zz]:
                p_copy(zz, b - RING, zc, 0, s).wait_send()
                seen[zz]["sent", b - RING, zc] = True
            p_stage(zz, b, zc)[...] = v.astype(BF16)
            p_copy(zz, b, zc, place - 1, s + nx if right else s - nx).start()
            seen[zz]["out", b, zc] = True

        def do_own(zz, b):
            own_write(zz, p_part(zz, b, zz), lambda: r.own_f.at[b] if b < 6 else r.own_o)

        def q_arrived(zz, qb, zo):
            if once(zz, "hz", qb, zo):
                q_copy(qb, q_land(qb, zo), zo, 0 if zo < zz else 1).wait_recv()

        def do_forward(zz, qb, zo):
            q_arrived(zz, qb, zo)
            way, to = (0, zz + 1) if zo < zz else (1, zz - 1)
            if 0 <= to < nz:
                q_copy(qb, q_land(qb, zo), zo, way).start()
                at_end(zz, lambda: q_copy(qb, q_land(qb, zo), zo, way).wait_send())

        def q_exchange(qb, k, n):
            to = lax.rem(x + k, nx)
            land = r.xr_d.at[qb, nx - k - 1] if qb < 3 else r.xr_r.at[qb - 3, nx - k - 1]
            return remote(
                sized(qstage.at[qb, k - 1], n),
                land,
                r.xr_s.at[qb, k],
                r.xr_rs.at[qb, k],
                (z * nx + to, m),
            )

        def do_q(zz, qb):
            e, n, own = (0, FB, q_own(qb)) if qb < 3 else (1, LP, q_own(qb))

            def piece(zo):
                return hload.at[zo] if n == d.W else hload.at[zo, :, pl.ds(0, n)]

            def fetch(zo):
                src = own if zo == zz else q_land(qb, zo)
                return pltpu.make_async_copy(src, piece(zo), r.ow.at[8 + zo])

            for zo in range(nz):
                if zo != zz:
                    q_arrived(zz, qb, zo)
                fetch(zo).start()
            if once(zz, "ez", e):
                ez_wait(e)
            for zo in range(nz):
                fetch(zo).wait()
            gathered = hload[:, :, 0:n].reshape(nz * T, n)
            for k in range(1, nx):
                v = dot(r.ez[e, lax.rem(x + k, nx)], gathered)
                sized(qstage.at[qb, k - 1], n)[...] = v.astype(BF16)
                q_exchange(qb, k, n).start()
            at_end(zz, lambda: [q_exchange(qb, k, n).wait_send() for k in range(1, nx)])
            own_write(
                zz,
                dot(r.ez[e, x], gathered),
                lambda: r.own_d.at[qb] if qb < 3 else r.own_r.at[qb - 3],
            )

        def work(point):
            for zz in range(nz):

                @pl.when(z == zz)
                def _(zz=zz):
                    for op in SCHEDULE[point][zz]:
                        kind, rest = op[0], op[1:]
                        {"F": do_forward, "P": do_p, "O": do_own, "Q": do_q, "H": do_operand}[kind](zz, *rest)

        def close():
            for zz in range(nz):

                @pl.when(z == zz)
                def _(zz=zz):
                    for copy in seen[zz].get("held", {}).values():
                        copy().wait()
                    for make in seen[zz].get("sent", []):
                        make()
                    for what in list(seen[zz]):
                        if what[0] == "out" and ("sent", *what[1:]) not in seen[zz]:
                            p_copy(zz, what[1], what[2], 0, s).wait_send()
                    for b in range(7):
                        paired = b in PAIRED
                        from_left = zz > (1 if paired else 0)
                        from_right = zz < nz - (2 if paired else 1)
                        for place, there in ((0, from_left), (nz - 1, from_right)):
                            if there:
                                p_copy(zz, b, (zz + 1) % nz, place, s).wait_recv()
                    for qb in range(5):
                        for k in range(1, nx):
                            q_exchange(qb, k, FB if qb < 3 else LP).wait_recv()

        def recurrent_backward(
            w_v, wout_v, gr, gb, gm, gcd, gcp, gmel, gpa, gpx, adj, t2
        ):
            ld_gel = local(r.w_gel, w_v, 2)
            ld_out = local(r.w_out, wout_v, 3)
            r.gsend[...] = jnp.zeros((nseq, 8, DC), F32)
            work(1)
            psum_finish(1)
            r.gacc[...] = jnp.zeros((16, D), F32)

            def norm_back(i):
                at = rows16(i)
                scale = r.scf[at, :][:, 0:1]
                inner = jnp.zeros((16, CB), F32)
                for j in range(2 * nb):
                    cols = slice(j * CB, (j + 1) * CB)
                    inner = inner + r.tot[j, at, :] * r.gains[1:2, cols] * r.resid[at, cols]
                factor = (scale * scale * scale) * (jnp.sum(inner, axis=1, keepdims=True) / D)
                for j in range(2 * nb):
                    cols = slice(j * CB, (j + 1) * CB)
                    n, v = r.tot[j, at, :], r.resid[at, cols]
                    r.gacc[:, cols] += n * v * scale
                    grad = r.cot_v[at, cols].astype(F32) + (
                        scale * (n * r.gains[1:2, cols]) - v * factor
                    )
                    gr[at, cols] = grad
                    gb[at, cols] = grad.astype(BF16)

            loop(T // 16, norm_back)
            gain_rows(1)
            ld_out.wait()
            gm[...] = dot_nt(gb[...], wout_v[...])

            def scan(t, carry):
                i = G // 16 - 1 - t
                out = []
                for b in range(B):
                    decay_in, value_in = carry[2 * b], carry[2 * b + 1]
                    at = rows16(i, b * G)
                    gate, slope = gelu_and_slope(r.pre_gel[at, :])
                    g = gm[at, :]
                    state = r.stp[b, pl.ds(pl.multiple_of(8 + i * 16, 8), 16), :]
                    r.gpg[at, 0:L] = (g * state * slope).astype(BF16)
                    value16 = g * gate
                    following = r.cfp[b, pl.ds(pl.multiple_of(i * 16, 16), 24), :][1:17]
                    for h in (1, 0):
                        a, v = scan_tile(
                            following[8 * h : 8 * h + 8], value16[8 * h : 8 * h + 8], reverse=True
                        )
                        v = v + a * value_in
                        a = a * decay_in
                        decay_in, value_in = a[0:1], v[0:1]
                        here = pl.ds(pl.multiple_of(b * G + i * 16 + 8 * h, 8), 8)
                        r.aloc[here, :] = a
                        adj[here, :] = v
                    out += [decay_in, value_in]
                return tuple(out)

            one, zero = jnp.ones((1, L), F32), jnp.zeros((1, L), F32)
            ends = lax.fori_loop(0, G // 16, scan, (one, zero) * B)
            for b in range(B):
                first = r.cfp[b, 0:1, :]
                r.pk[1, b : b + 1, :] = first * ends[2 * b]
                r.pk[1, B + b : B + b + 1, :] = first * ends[2 * b + 1]
            pairs_send(1)
            for b in (3, 4, 5):
                hx_send(b)
            ee_send()
            q_send(3)
            ld_gel.wait()

            def gel_term(j):
                at = pl.ds(pl.multiple_of(j * CB, CB), CB)
                gmel[j] = dot_nt(r.gpg[:, 0:L], w_v[at, :]).astype(BF16)

            loop(2 * nb, gel_term)
            ld_rec = local(r.w_rec, w_v, 1)
            transposed(gb, r.gbT)
            ex_send(1)
            work(2)
            outer = pairs_enter(1, True)

            def gate_back(i):
                for b in range(B):
                    at = rows16(i, b * G)
                    adjoint = adj[at, :] + r.aloc[at, :] * outer[b : b + 1]
                    recur, inject = r.recur[at, :], r.inj[at, :]
                    log_decay = r.rv[0:1] * recur
                    decay = jnp.exp(log_decay)
                    value = r.cv[at, 0:L].astype(F32)
                    spread = jnp.sqrt(minus_expm1(2.0 * log_decay))
                    prior = r.stp[b, pl.ds(pl.multiple_of(i * 16, 16), 24), :][7:23]
                    keep = r.mk[b, rows16(i), :][:, 1:2]
                    grad_log = (
                        adjoint * inject * value * (-(decay * decay) / spread)
                        + adjoint * prior * keep * decay
                    )
                    ga = (grad_log * r.rv[0:1] * recur * (1.0 - recur)).astype(BF16)
                    direct = adjoint * spread * inject
                    gx = (adjoint * spread * value * inject * (1.0 - inject)).astype(BF16)
                    gpa[at, :] = ga
                    gpx[at, :] = gx
                    gcd[at, :] = direct
                    r.sacc[5] += fold8(ga.astype(F32))
                    r.sacc[6] += fold8(gx.astype(F32))
                    r.sacc[7] += fold8(grad_log * recur)

            loop(G // 16, gate_back)
            r.gs_l[...] = (dot_nt(gpa[...], r.wl[0]) + dot_nt(gpx[...], r.wl[1])).astype(BF16)

            def to_left():
                return remote(r.gs_l, r.gi_r, r.gi_s.at[0], r.gi_rs.at[0], (s, left_m))

            start(to_left)
            r.gs_r[...] = (dot_nt(gpa[...], r.wr[0]) + dot_nt(gpx[...], r.wr[1])).astype(BF16)

            def to_right():
                return remote(r.gs_r, r.gi_l, r.gi_s.at[1], r.gi_rs.at[1], (s, right_m))

            start(to_right)
            own = dot_nt(gpa[...], r.wo[0]) + dot_nt(gpx[...], r.wo[1])
            gcd[...] += own[:, 0:L]

            for i, grad in enumerate((gpa, gpx)):
                turned = jnp.where(head_mask(base - HW, HW), dot(r.hl[...].T, grad[...]), 0.0)
                t2[0:HW, :] = turned
                for p, n in pieces:
                    part = dot(r.cv[:, p : p + n].T, grad[...])
                    t2[0:n, :] += jnp.where(head_mask(base + p, n), part, 0.0)
                t2[HW : 2 * HW, :] = t2[0:HW, :]
                back = pl.multiple_of(lax.rem(HW - turn, HW), HW // 4)
                table = t2[pl.ds(back, HW), :]
                right = jnp.where(head_mask(base + L, HW), dot(r.hr[...].T, grad[...]), 0.0)
                t2[0:HW, :] = right
                t2[HW : 2 * HW, :] = right
                back = pl.multiple_of(lax.rem(HW - turn_right, HW), HW // 4)
                table = (table + t2[pl.ds(back, HW), :]).astype(BF16)
                for q in range(nseq):
                    r.gt[q // nx, q % nx, i] = table[q * d.GR : (q + 1) * d.GR]

            work(3)
            to_left().wait_recv()
            to_right().wait_recv()
            gcd[:, 0:HW] += r.gi_l[...].astype(F32)
            gcd[:, L - HW : L] += r.gi_r[...].astype(F32)
            for b in range(B):
                gcp[b, 0:G, :] = gcd[b * G : (b + 1) * G, :]
                gcp[b, G : G + 8, :] = jnp.zeros((8, L), F32)

            for b in range(B):
                top, keep = gcp[b, 0:8, :], r.mk[b, 0:8, :]
                spill = jnp.zeros((8, L), F32)
                row = lax.broadcasted_iota(jnp.int32, (8, L), 0)
                for k in range(1, d.taps):
                    moved = pltpu.roll(r.vecs[k : k + 1] * (keep[:, k : k + 1] * top), 8 - k, 0)
                    spill = spill + jnp.where(row >= 8 - k, moved, 0.0)
                r.sp_s[b * 8 : (b + 1) * 8, :] = spill

            def spilled():
                return remote(r.sp_s, r.sp_r, r.sp_ss.at[0], r.sp_rs.at[0], (s - 1, m))

            start(spilled, lambda: s > 0)

            @pl.when(s == nseq - 1)
            def _():
                r.sp_r[...] = jnp.zeros((B * 8, L), F32)

            def conv_back(i, spill):
                for b in range(B):
                    grads = gcp[b, pl.ds(pl.multiple_of(i * 16, 16), 24), :]
                    keep = r.mk[b, pl.ds(pl.multiple_of(i * 16, 16), 24), :]
                    window = r.extp[b, pl.ds(pl.multiple_of(i * 16 + 8, 8), 24), :]
                    here = grads[0:16]
                    out = r.vecs[0:1] * here
                    if not spill:
                        r.sacc[4] += fold8(here)
                        r.sacc[0] += fold8(here * window[8:24])
                    for k in range(1, d.taps):
                        masked = keep[:, k : k + 1] * grads
                        out = out + r.vecs[k : k + 1] * masked[k : k + 16]
                        if not spill:
                            r.sacc[k] += fold8(masked[0:16] * window[8 - k : 24 - k])
                    if spill:
                        extra = r.sp_r[b * 8 : (b + 1) * 8, :]
                        out = out + jnp.concatenate([jnp.zeros((8, L), F32), extra], axis=0)
                    r.gpr[rows16(i, b * G), 0:L] = out.astype(BF16)

            loop(G // 16, lambda i: conv_back(i, False))
            for k in range(8):
                r.smv[k : k + 1, :] = jnp.sum(r.sacc[k], axis=0, keepdims=True)

            work(4)

            @pl.when(s < nseq - 1)
            def _():
                spilled().wait_recv()

            conv_back(G // 16 - 1, True)
            q_send(4)
            ld_rec.wait()

            def mix_term(col):
                at = pl.ds(pl.multiple_of(col, CB), CB)
                return dot_nt(r.gpr[:, 0:L], w_v[at, :]) + gmel[lax.div(col, CB)].astype(F32)

            psum_start(2, mix_term)

            def small_x(k):
                to = lax.rem(x + k, nx)
                return remote(
                    r.smv, r.smx.at[x], r.smx_s.at[k], r.smx_r.at[k], (z * nx + to, m)
                )

            def gates_x(k):
                to = lax.rem(x + k, nx)
                return remote(
                    r.gt.at[:, to], r.gtx.at[x], r.gtx_s.at[k], r.gtx_r.at[k], (z * nx + to, m)
                )

            def small_z(k):
                to = lax.rem(z + k, nz)
                return remote(
                    r.smv, r.smz.at[z], r.smz_s.at[k], r.smz_r.at[k], (to * nx + x, m)
                )

            def gates_z(k):
                to = lax.rem(z + k, nz)
                return remote(
                    r.gts.at[to], r.gtz.at[z], r.gtz_s.at[k], r.gtz_r.at[k], (to * nx + x, m)
                )

            def gain_copy(q):
                to = lax.rem(s + q, nseq)
                return remote(r.gsend.at[to], r.gland.at[s], r.ga_s.at[q], r.ga_r.at[q], (to, m))

            for k in range(1, nx):
                small_x(k).start()
                gates_x(k).start()
            ex_relay(1)
            work(5)
            psum_finish(2)

            r.gacc[...] = jnp.zeros((16, D), F32)

            def norm_back_mix(i):
                at = rows16(i)
                scale = r.scm[at, :][:, 0:1]
                inner = jnp.zeros((16, CB), F32)
                for j in range(2 * nb):
                    cols = slice(j * CB, (j + 1) * CB)
                    v = r.x_v[at, cols].astype(F32)
                    inner = inner + r.tot[j, at, :] * r.gains[0:1, cols] * v
                factor = (scale * scale * scale) * (jnp.sum(inner, axis=1, keepdims=True) / D)
                for j in range(2 * nb):
                    cols = slice(j * CB, (j + 1) * CB)
                    n, v = r.tot[j, at, :], r.x_v[at, cols].astype(F32)
                    r.gacc[:, cols] += n * v * scale
                    gb[at, cols] = (
                        gr[at, cols] + (scale * (n * r.gains[0:1, cols]) - v * factor)
                    ).astype(BF16)

            loop(T // 16, norm_back_mix)
            out_gin = pltpu.make_async_copy(gb, r.k_gin, r.ow.at[0])
            out_gin.start()
            gain_rows(0)
            for q in range(1, nseq):
                start(functools.partial(gain_copy, q))

            psum_start(3, lambda col: r.fo[lax.div(col, CB)].astype(F32))
            small, gates = r.smv[...], r.gt[:, x].astype(F32)
            for k in range(1, nx):
                src = lax.rem(x + nx - k, nx)
                remote(r.smv, r.smx.at[src], r.smx_s.at[k], r.smx_r.at[k], partner).wait_recv()
                remote(r.gt.at[:, x], r.gtx.at[src], r.gtx_s.at[k], r.gtx_r.at[k], partner).wait()
                small_x(k).wait_send()
            for k in range(1, nx):
                src = lax.rem(x + nx - k, nx)
                small = small + r.smx[src]
                gates = gates + r.gtx[src].astype(F32)
            r.smv[...] = small
            r.gts[...] = gates.astype(BF16)
            for k in range(1, nz):
                start(functools.partial(small_z, k))
                start(functools.partial(gates_z, k))
            work(6)
            psum_finish(3)

            def block_out(i):
                at = rows16(i)
                for j in range(2 * nb):
                    cols = slice(j * CB, (j + 1) * CB)
                    r.cot_v[at, cols] = (r.resid[at, cols] + r.tot[j, at, :]).astype(BF16)

            loop(T // 16, block_out)
            out_block = pltpu.make_async_copy(r.cot_v, r.k_block, r.ow.at[1])
            out_block.start()

            out_gin.wait()
            out_block.wait()

        pl.run_scoped(
            recurrent_backward,
            pltpu.VMEM((D, L), BF16),
            pltpu.VMEM((L, D), BF16),
            pltpu.VMEM((T, D), F32),
            pltpu.VMEM((T, D), BF16),
            pltpu.VMEM((T, L), F32),
            pltpu.VMEM((T, L), F32),
            pltpu.VMEM((B, G + 8, L), F32),
            pltpu.VMEM((2 * nb, T, CB), BF16),
            pltpu.VMEM((T, L), BF16),
            pltpu.VMEM((T, L), BF16),
            pltpu.VMEM((T, L), F32),
            pltpu.VMEM((2 * HW, L), F32),
        )


        def rest(stage_o, load_o):
            tail.extend((stage_o, load_o))
            work(7)
            close()

        pl.run_scoped(rest, pltpu.VMEM((nz - 1, DC, LP), BF16), pltpu.VMEM((DC, LP), BF16))

        for q in range(1, nseq):
            src = lax.rem(s + nseq - q, nseq)
            remote(
                r.gsend.at[src], r.gland.at[src], r.ga_s.at[q], r.ga_r.at[q], partner
            ).wait_recv()
        for k in range(1, nz):
            src = lax.rem(z + nz - k, nz)
            remote(r.smv, r.smz.at[src], r.smz_s.at[k], r.smz_r.at[k], partner).wait_recv()
            remote(
                r.gts.at[src], r.gtz.at[src], r.gtz_s.at[k], r.gtz_r.at[k], partner
            ).wait_recv()
        r.gland[s] = r.gsend[s]
        r.smz[z] = r.smv[...]
        r.gtz[z] = r.gts[z]
        small, gates, gain = r.smz[0], r.gtz[0].astype(F32), r.gland[0]
        for q in range(1, nz):
            small = small + r.smz[q]
            gates = gates + r.gtz[q].astype(F32)
        for q in range(1, nseq):
            gain = gain + r.gland[q]
        r.k_small[...] = jnp.zeros((8, LP), F32)
        r.k_small[:, 0:L] = small
        r.k_small[7:8, 0:L] = small[7:8, :] * r.rv[1:2, :]
        r.k_gain[...] = gain
        r.k_gates[...] = gates

        for make, when in pending:
            if when is None:
                make().wait_send()
            else:
                pl.when(when())(lambda make=make: make().wait_send())

    pl.run_scoped(
        after_feed_forward,
        pltpu.VMEM((RING, nz - 1, DC, FB), BF16),
        pltpu.VMEM((DC, FB), BF16),
        pltpu.VMEM((2, DC, d.W), BF16),
        pltpu.VMEM((nz, T, d.W), BF16),
        pltpu.VMEM((5, nx - 1, DC, d.W), BF16),
    )


def finish(d, r):
    L, LP, FB, DC, nseq, nz, nx = d.L, d.LP, d.FB, d.DC, d.nseq, d.nz, d.nx
    s = lax.axis_index("seq")
    z = lax.div(s, nx)
    copies, loads, used = [], [], [0]

    def copy(src, dst):
        used[0] += 1
        return pltpu.make_async_copy(src, dst, r.sem.at[used[0] - 1])

    def load(*pairs):
        group = [copy(*pair) for pair in pairs]
        for one in group:
            one.start()
        loads.append(group)

    far = nz - 1
    for b in range(6):
        load((r.own_f.at[b], r.a_f.at[b]), (r.land_f.at[b, 0], r.b_f.at[b]), (r.land_f.at[b, far], r.c_f.at[b]))
    load((r.own_o, r.a_o), (r.land_o.at[0], r.b_o), (r.land_o.at[far], r.c_o))
    for qb in range(3):
        load((r.own_d.at[qb], r.a_d.at[qb]), (r.xr_d.at[qb], r.b_d.at[qb]))
    for qb in range(2):
        load((r.own_r.at[qb], r.a_r.at[qb]), (r.xr_r.at[qb], r.b_r.at[qb]))
    load((r.k_block, r.w_block))
    load((r.k_gin, r.w_gin))

    def write(buf, ref):
        one = copy(buf, ref)
        one.start()
        copies.append(one)

    def emit(value, buf, ref):
        buf[...] = value
        write(buf, ref)

    def chained(a, left, right, paired=0):
        v = a.astype(F32) + jnp.where(z > paired, left.astype(F32), 0.0)
        return v + jnp.where(z < nz - 1 - paired, right.astype(F32), 0.0)

    def arrived(i):
        for one in loads[i]:
            one.wait()

    for b in range(6):
        arrived(b)
        ref = r.o_wup if b % 2 else r.o_wgate
        v = chained(r.a_f[b], r.b_f[b], r.c_f[b], 1 if b in PAIRED else 0)
        emit(v, r.v_f.at[b], ref.at[:, b // 2 * FB : (b // 2 + 1) * FB])
    arrived(6)
    emit(chained(r.a_o[...], r.b_o[...], r.c_o[...]).T[0:L], r.v_o, r.o_wout)
    for qb in range(5):
        arrived(7 + qb)
        a, b = (r.a_d[qb], r.b_d[qb]) if qb < 3 else (r.a_r[qb - 3], r.b_r[qb - 3])
        v = a.astype(F32)
        for k in range(nx - 1):
            v = v + b[k].astype(F32)
        if qb < 3:
            emit(v.T, r.v_d.at[qb], r.o_wdown.at[qb * FB : (qb + 1) * FB])
        else:
            emit(v[:, 0:L], r.v_r.at[qb - 3], r.o_wgel if qb == 3 else r.o_wrec)

    arrived(12)
    emit(r.w_block[...].astype(F32), r.u_block, r.o_block)
    arrived(13)
    emit(r.w_gin[...].astype(F32), r.u_gin, r.o_gin)
    part = L // nseq
    small = pltpu.roll(r.k_small[...], lax.rem(LP - s * part, LP), 1)
    r.o_cw[...] = small[0:4, 0:part]
    r.o_cb[...] = small[4, 0:part]
    r.o_ba[...] = small[5, 0:part]
    r.o_bx[...] = small[6, 0:part]
    r.o_lr[...] = small[7, 0:part]
    r.o_gm[...] = r.k_gain[0, :]
    r.o_gf[...] = r.k_gain[1, :]
    r.o_ga[...] = r.k_gates[0]
    r.o_gx[...] = r.k_gates[1]
    for one in copies:
        one.wait()


IN_ANY = ("x_in", "w_rec", "w_gel", "w_out", "gate_a", "gate_x", "w_gate", "w_up", "w_down", "cot")
IN_VMEM = (
    "ids", "gain_mix", "gain_ffn", "conv_weight", "conv_bias", "bias_a", "bias_x", "log_rate"
)
MID_VMEM = ("k_small", "k_gain", "k_gates")
LIMIT = 62 * 2**20


def space(in_vmem):
    return pl.BlockSpec(memory_space=pltpu.VMEM if in_vmem else pl.ANY)


def on_device(nseq, nm, *args):
    (
        block_input,
        segment_ids,
        gain_mix,
        w_rec,
        w_gel,
        conv_weight,
        conv_bias,
        gate_a,
        gate_x,
        bias_a,
        bias_x,
        log_rate,
        w_out,
        gain_ffn,
        w_gate,
        w_up,
        w_down,
        cotangent,
    ) = args
    B, G, D = block_input.shape
    T, L, F = B * G, w_rec.shape[1], w_gate.shape[1]
    nz = Z_CHIPS
    d = types.SimpleNamespace(
        B=B, G=G, T=T, D=D, L=L, F=F, LP=-(-L // 128) * 128, FB=F // 3, HW=gate_a.shape[0],
        DC=D // nseq, nseq=nseq, nm=nm, nz=nz, nx=nseq // nz, ny=nm // CORES, CB=256,
        nb=D // CORES // 256, taps=conv_weight.shape[0], GR=gate_a.shape[0] // nseq,
    )
    d.W = max(d.FB, d.LP)
    outs, scratch, sems = layout(d)
    feed = dict(
        x_in=block_input.reshape(T, D), w_rec=w_rec, w_gel=w_gel, w_out=w_out, gate_a=gate_a,
        gate_x=gate_x, w_gate=w_gate, w_up=w_up, w_down=w_down, cot=cotangent.reshape(T, D),
        ids=segment_ids, gain_mix=gain_mix, gain_ffn=gain_ffn, conv_weight=conv_weight,
        conv_bias=conv_bias, bias_a=bias_a, bias_x=bias_x, log_rate=log_rate,
    )
    names_in = IN_ANY + IN_VMEM
    names = names_in + tuple(outs) + tuple(scratch) + tuple(sems)

    def kernel(*refs):
        body(d, types.SimpleNamespace(**dict(zip(names, refs))))

    mid = pl.pallas_call(
        kernel,
        out_shape=[jax.ShapeDtypeStruct(*v) for v in outs.values()],
        in_specs=[space(n in IN_VMEM) for n in names_in],
        out_specs=[space(n in MID_VMEM) for n in outs],
        scratch_shapes=[pltpu.VMEM(*v) for v in scratch.values()]
        + [pltpu.SemaphoreType.DMA(v) for v in sems.values()],
        compiler_params=pltpu.CompilerParams(
            collective_id=0, has_side_effects=True, vmem_limit_bytes=LIMIT
        ),
        name="block",
    )(*[feed[n] for n in names_in])
    mid = dict(zip(outs, mid))
    for n in ("hz_d", "hz_r"):
        mid.pop(n)
    DC, FB, LP, GR, part = d.DC, d.FB, d.LP, d.GR, L // nseq
    last = dict(
        o_block=(T, D), o_gin=(T, D), o_gm=(DC,), o_wrec=(DC, L), o_wgel=(DC, L),
        o_cw=(d.taps, part), o_cb=(part,), o_ga=(GR, L), o_gx=(GR, L), o_ba=(part,), o_bx=(part,),
        o_lr=(part,), o_wout=(L, DC), o_gf=(DC,), o_wgate=(DC, F), o_wup=(DC, F), o_wdown=(F, DC),
    )
    large = ("o_block", "o_gin", "o_wrec", "o_wgel", "o_wout", "o_wgate", "o_wup", "o_wdown")
    buffers = dict(
        a_f=((6, DC, FB), BF16), b_f=((6, DC, FB), BF16), c_f=((6, DC, FB), BF16),
        a_o=((DC, LP), BF16), b_o=((DC, LP), BF16), c_o=((DC, LP), BF16),
        a_d=((3, DC, FB), BF16), b_d=((3, d.nx - 1, DC, FB), BF16),
        a_r=((2, DC, LP), BF16), b_r=((2, d.nx - 1, DC, LP), BF16),
        w_block=((T, D), BF16), w_gin=((T, D), BF16),
        u_block=((T, D), F32), u_gin=((T, D), F32),
        v_f=((6, DC, FB), F32), v_o=((L, DC), F32), v_d=((3, FB, DC), F32), v_r=((2, DC, L), F32),
    )
    names_last = tuple(mid) + tuple(last) + tuple(buffers) + ("sem",)

    def last_kernel(*refs):
        finish(d, types.SimpleNamespace(**dict(zip(names_last, refs))))

    results = pl.pallas_call(
        last_kernel,
        out_shape=[jax.ShapeDtypeStruct(v, F32) for v in last.values()],
        in_specs=[space(n in MID_VMEM) for n in mid],
        out_specs=[space(n not in large) for n in last],
        scratch_shapes=[pltpu.VMEM(*v) for v in buffers.values()] + [pltpu.SemaphoreType.DMA((64,))],
        compiler_params=pltpu.CompilerParams(vmem_limit_bytes=LIMIT),
        name="finish",
    )(*mid.values())
    results = list(results)
    results[0] = results[0].reshape(B, G, D)
    results[1] = results[1].reshape(B, G, D)
    return tuple(results)


def solution(mesh):
    nseq, nm = mesh.shape["seq"], mesh.shape["mp"]
    rows, cols, both = P(None, "seq", None), P(None, "mp"), P(("mp", "seq"))
    part = P("seq", "mp")
    in_specs = (
        rows, P(), P(), cols, cols, cols, P("mp"), cols, cols, P("mp"), P("mp"), P("mp"),
        P("mp", None), P(), cols, cols, P("mp", None), rows,
    )
    out_specs = (
        rows, rows, P("seq"), part, part, P(None, ("mp", "seq")), both, part, part, both, both,
        both, P("mp", "seq"), P("seq"), part, part, P("mp", "seq"),
    )

    def step(*args):
        return on_device(nseq, nm, *args)

    return jax.shard_map(step, mesh=mesh, in_specs=in_specs, out_specs=out_specs, check_vma=False)
```

```python
import functools
import types

import jax
import jax.numpy as jnp
from jax import lax
from jax.experimental import pallas as pl
from jax.experimental.pallas import tpu as pltpu
from jax.sharding import PartitionSpec as P

EPS = 1e-06
RATE_SCALE = 8.0
Z_CHIPS = 4
CORES = 2
RING = 3
GELU_C = 0.7978845608028654
GELU_A = 0.044715
MESH = pl.DeviceIdType.MESH
F32 = jnp.float32
BF16 = jnp.bfloat16

SCHEDULE = (
    (
        (),
        (),
        (),
        (),
    ),
    (
        (("P", 0, 1, 3), ("P", 0, 1, 2), ("P", 0, 1, 1),),
        (("F", 0, 0), ("F", 0, 2), ("F", 1, 0), ("F", 1, 2), ("F", 2, 0),),
        (("F", 0, 1), ("F", 0, 3), ("F", 1, 1), ("F", 1, 3), ("F", 2, 1),),
        (("P", 0, -1, 0), ("P", 0, -1, 1), ("P", 0, -1, 2),),
    ),
    (
        (("P", 1, 1, 3), ("P", 1, 1, 2), ("P", 1, 1, 1), ("P", 2, 1, 3), ("P", 2, 1, 2), ("P", 2, 1, 1),),
        (("F", 0, 3), ("F", 2, 2), ("P", 0, 1, 3), ("P", 0, 1, 2), ("F", 1, 3), ("F", 3, 0), ("F", 3, 2),),
        (("F", 0, 0), ("F", 1, 0), ("F", 2, 3), ("P", 0, -1, 0), ("P", 0, -1, 1), ("F", 2, 0),),
        (),
    ),
    (
        (("P", 3, 1, 3), ("P", 3, 1, 2), ("P", 3, 1, 1),),
        (("P", 1, 1, 3), ("F", 2, 3),),
        (("F", 3, 1), ("P", 0, 1, 3), ("F", 3, 3),),
        (("P", 1, -1, 0), ("P", 1, -1, 1), ("P", 1, -1, 2), ("P", 2, -1, 0),),
    ),
    (
        (("P", 4, 1, 3), ("P", 4, 1, 2),),
        (("P", 1, 1, 2), ("P", 0, -1, 0), ("P", 2, 1, 3), ("F", 3, 3),),
        (("P", 1, -1, 0), ("P", 1, -1, 1), ("F", 3, 0), ("P", 1, 1, 3), ("P", 2, -1, 0),),
        (("P", 2, -1, 1), ("P", 2, -1, 2), ("P", 3, -1, 0),),
    ),
    (
        (("Q", 0), ("Q", 1), ("Q", 2), ("P", 4, 1, 1), ("O", 0), ("O", 1), ("O", 2), ("Q", 3), ("P", 5, 1, 3),),
        (("P", 2, 1, 2), ("Q", 0), ("P", 1, -1, 0), ("Q", 1), ("Q", 2), ("Q", 3), ("P", 3, 1, 3), ("O", 0),),
        (("Q", 0), ("P", 2, 1, 3), ("P", 2, -1, 1), ("Q", 1), ("Q", 2), ("Q", 3), ("F", 4, 1), ("O", 0), ("O", 1),),
        (("Q", 0), ("Q", 1), ("Q", 2), ("O", 0), ("P", 3, -1, 1), ("O", 1), ("O", 2), ("O", 3), ("O", 4), ("O", 5),),
    ),
    (
        (("O", 3), ("O", 4), ("O", 5), ("P", 5, 1, 2), ("P", 5, 1, 1),),
        (("F", 4, 2), ("P", 3, 1, 2), ("P", 2, -1, 0), ("O", 1), ("O", 2), ("O", 3), ("O", 4), ("P", 4, 1, 3), ("O", 5), ("P", 4, 1, 2),),
        (("F", 4, 3), ("P", 3, 1, 3), ("P", 3, -1, 0), ("O", 2), ("O", 3), ("O", 4), ("O", 5), ("P", 3, -1, 1),),
        (("P", 3, -1, 2), ("Q", 3), ("P", 4, -1, 0), ("P", 4, -1, 1),),
    ),
    (
        (("P", 6, 1, 3), ("P", 6, 1, 2), ("P", 6, 1, 1), ("O", 6), ("Q", 4),),
        (("O", 6), ("F", 4, 0), ("P", 5, 1, 3), ("F", 4, 3), ("P", 3, -1, 0), ("P", 5, 1, 2), ("P", 4, -1, 0), ("P", 6, 1, 3), ("P", 5, -1, 0), ("P", 6, 1, 2), ("P", 6, -1, 0), ("Q", 4),),
        (("O", 6), ("P", 4, -1, 0), ("P", 4, -1, 1), ("P", 4, 1, 3), ("P", 5, -1, 0), ("P", 5, -1, 1), ("F", 4, 0), ("P", 5, 1, 3), ("P", 6, -1, 0), ("P", 6, 1, 3), ("P", 6, -1, 1), ("Q", 4),),
        (("P", 4, -1, 2), ("P", 5, -1, 0), ("P", 5, -1, 1), ("P", 5, -1, 2), ("O", 6), ("P", 6, -1, 0), ("P", 6, -1, 1), ("P", 6, -1, 2), ("Q", 4),),
    ),
)


def dot(left, right):
    return jnp.dot(left, right, preferred_element_type=F32)


def dot_nt(left, right):
    return lax.dot_general(left, right, (((1,), (1,)), ((), ())), preferred_element_type=F32)


def remote(src, dst, send_sem, recv_sem, device):
    return pltpu.make_async_remote_copy(
        src_ref=src,
        dst_ref=dst,
        send_sem=send_sem,
        recv_sem=recv_sem,
        device_id=device,
        device_id_type=MESH,
    )


def loop(count, body):
    def step(i, carry):
        body(i)
        return carry

    lax.fori_loop(0, count, step, 0)


def rows16(i, offset=0):
    return pl.ds(pl.multiple_of(i * 16 + offset, 16), 16)


def gelu_tanh(v):
    t = jnp.tanh(GELU_C * (v + GELU_A * (v * v * v)))
    return 0.5 * v * (1.0 + t)


def gelu_and_slope(v):
    square = v * v
    t = jnp.tanh(GELU_C * (v + GELU_A * (square * v)))
    half = 0.5 * (1.0 + t)
    slope = half + 0.5 * v * (1.0 - t * t) * (GELU_C * (1.0 + 3.0 * GELU_A * square))
    return v * half, slope


def minus_expm1(v):
    acc = 1.0 + v * (1.0 / 8.0)
    for n in (7.0, 6.0, 5.0, 4.0, 3.0, 2.0):
        acc = 1.0 + v * (1.0 / n) * acc
    return -v * acc


def softplus_small(v):
    u = jnp.exp(v)
    acc = 1.0 / 6.0 - u * (1.0 / 7.0)
    for n in (5.0, 4.0, 3.0, 2.0):
        acc = 1.0 / n - u * acc
    return u * (1.0 - u * acc)


def scan_tile(decay, value, reverse):
    row = lax.broadcasted_iota(jnp.int32, decay.shape, 0)
    for k in (1, 2, 4):
        shift = 8 - k if reverse else k
        valid = row < 8 - k if reverse else row >= k
        decay_k = pltpu.roll(decay, shift, 0)
        value_k = pltpu.roll(value, shift, 0)
        value = jnp.where(valid, decay * value_k + value, value)
        decay = jnp.where(valid, decay * decay_k, decay)
    return decay, value


def fold8(v):
    return v[0:8] + v[8:16]


def layout(dims):
    d = dims
    T, D, L, LP, F, FB, DC = d.T, d.D, d.L, d.LP, d.F, d.FB, d.DC
    B, G, HW = d.B, d.G, d.HW
    outs = dict(
        k_block=((T, D), F32),
        k_gin=((T, D), F32),
        k_small=((8, LP), F32),
        k_gain=((8, DC), F32),
        k_gates=((2, d.GR, L), F32),
        own_f=((6, DC, FB), BF16),
        own_o=((DC, LP), BF16),
        own_d=((3, DC, FB), BF16),
        own_r=((2, DC, LP), BF16),
        land_f=((6, 2 * (d.nz - 1), DC, FB), BF16),
        land_o=((2 * (d.nz - 1), DC, LP), BF16),
        xr_d=((3, d.nx - 1, DC, FB), BF16),
        xr_r=((2, d.nx - 1, DC, LP), BF16),
        hz_d=((3, d.nz, T, FB), BF16),
        hz_r=((2, d.nz, T, LP), BF16),
    )
    scratch = dict(
        x_v=((T, D), BF16),
        cot_v=((T, D), BF16),
        xh=((B * 16, D), BF16),
        scm=((T, 128), F32),
        scf=((T, 128), F32),
        idp=((8, 2 * G), jnp.int32),
        mk=((B, G + 8, 128), F32),
        rv=((8, L), F32),
        wl=((2, HW, L), BF16),
        wo=((2, LP, L), BF16),
        wr=((2, HW, L), BF16),
        extp=((B, 16 + G, L), F32),
        cv=((T, LP), BF16),
        st_l=((T, HW), BF16),
        st_r=((T, HW), BF16),
        hl=((T, HW), BF16),
        hr=((T, HW), BF16),
        pre_gel=((T, L), F32),
        recur=((T, L), F32),
        inj=((T, L), F32),
        cfp=((B, G + 8, L), F32),
        aloc=((T, L), F32),
        stp=((B, 8 + G, L), F32),
        pk=((2, 2 * B, L), F32),
        pf=((2, d.nseq, 2 * B, L), F32),
        resid=((T, D), F32),
        csend=((d.nb, T, d.CB), F32),
        cland=((d.nb, T, d.CB), F32),
        tot=((2 * d.nb, T, d.CB), F32),
        yl=((2, d.ny, d.nb, T, d.CB), BF16),
        fo=((2 * d.nb, T, d.CB), BF16),
        hd=((3, T, FB), BF16),
        gp=((6, d.nx, T, FB), BF16),
        mx=((d.nx, T, LP), BF16),
        gpg=((T, LP), BF16),
        gpr=((T, LP), BF16),
        nmT=((d.nz, d.nx, DC, T), BF16),
        cotT=((d.nz, d.nx, DC, T), BF16),
        nfT=((d.nz, d.nx, DC, T), BF16),
        gbT=((d.nz, d.nx, DC, T), BF16),
        ez=((2, d.nx, DC, d.nz * T), BF16),
        ex=((2, d.nz, DC, d.nx * T), BF16),
        vecs=((8, L), F32),
        gains=((8, D), F32),
        gacc=((16, D), F32),
        gsend=((d.nseq, 8, DC), F32),
        gland=((d.nseq, 8, DC), F32),
        sacc=((8, 8, L), F32),
        smv=((8, L), F32),
        smx=((d.nx, 8, L), F32),
        smz=((d.nz, 8, L), F32),
        gt=((d.nz, d.nx, 2, d.GR, L), BF16),
        gtx=((d.nx, d.nz, 2, d.GR, L), BF16),
        gtz=((d.nz, 2, d.GR, L), BF16),
        gts=((d.nz, 2, d.GR, L), BF16),
        gs_l=((T, HW), BF16),
        gs_r=((T, HW), BF16),
        gi_l=((T, HW), BF16),
        gi_r=((T, HW), BF16),
        sp_s=((B * 8, L), F32),
        sp_r=((B * 8, L), F32),
    )
    sems = dict(
        ld=(16,),
        halo_s=(B,),
        halo_r=(B,),
        ex_s=(4 * B,),
        ex_r=(4 * B,),
        gi_s=(2,),
        gi_rs=(2,),
        pf_s=(2, d.nseq),
        pf_r=(2, d.nseq),
        c_s=(4, d.nb),
        c_r=(4, d.nb),
        y_s=(4, d.ny, d.nb),
        y_r=(4, d.ny, d.nb),
        a_s=(4, d.nb),
        a_r=(4, d.nb),
        ez_s=(2, d.nz),
        ez_r=(2, d.nz),
        ezc_s=(2, d.nz),
        ezc_r=(2, d.nz),
        ex_xs=(2, d.nx),
        ex_xr=(2, d.nx),
        exc_s=(2, d.nx),
        exc_r=(2, d.nx),
        own_l=(4,),
        hz_s=(5, d.nz, 2),
        hz_rs=(5, d.nz),
        hx_s=(7, d.nx),
        hx_r=(7, d.nx),
        xr_s=(5, d.nx),
        xr_rs=(5, d.nx),
        p_s=(7, d.nz),
        p_r=(7, 2 * (d.nz - 1)),
        smx_s=(d.nx,),
        smx_r=(d.nx,),
        smz_s=(d.nz,),
        smz_r=(d.nz,),
        ga_s=(d.nseq,),
        ga_r=(d.nseq,),
        gtx_s=(d.nx,),
        gtx_r=(d.nx,),
        gtz_s=(d.nz,),
        gtz_r=(d.nz,),
        sp_ss=(1,),
        sp_rs=(1,),
        pl_s=(2,),
        ow=(16,),
    )
    return outs, scratch, sems


def body(d, r):
    T, D, L, LP, F, FB, DC = d.T, d.D, d.L, d.LP, d.F, d.FB, d.DC
    B, G, HW, CB, nb = d.B, d.G, d.HW, d.CB, d.nb
    nseq, nz, nx, ny, nm = d.nseq, d.nz, d.nx, d.ny, d.nm
    s, m = lax.axis_index("seq"), lax.axis_index("mp")
    z, x = lax.div(s, nx), lax.rem(s, nx)
    y, c = lax.div(m, CORES), lax.rem(m, CORES)
    partner = (s, y * CORES + 1 - c)
    left_m, right_m = lax.rem(m + nm - 1, nm), lax.rem(m + 1, nm)
    pending = []

    def later(make, when=None):
        pending.append((make, when))

    def start(make, when=None):
        if when is None:
            make().start()
        else:
            pl.when(when())(lambda: make().start())
        pending.append((make, when))

    barrier = pltpu.get_barrier_semaphore()
    for k in range(1, nseq):
        pl.semaphore_signal(
            barrier, inc=1, device_id=(lax.rem(s + k, nseq), m), device_id_type=MESH
        )
    for k in range(1, nm):
        pl.semaphore_signal(barrier, inc=1, device_id=(s, lax.rem(m + k, nm)), device_id_type=MESH)

    def local(src, dst, i):
        copy = pltpu.make_async_copy(src, dst, r.ld.at[i])
        copy.start()
        return copy

    ld_x = local(r.x_in, r.x_v, 0)
    ld_cot = local(r.cot, r.cot_v, 8)

    half = nb * CB

    def psum_start(k, part):
        par = k % 2

        def send_half(j):
            r.csend[j] = part((1 - c) * half + j * CB)
            remote(r.csend.at[j], r.cland.at[j], r.c_s.at[k, j], r.c_r.at[k, j], partner).start()

        loop(nb, send_half)

        def own_half(j):
            v = part(c * half + j * CB)
            remote(
                r.csend.at[j], r.cland.at[j], r.c_s.at[k, j], r.c_r.at[k, j], partner
            ).wait_recv()
            r.yl[par, y, j] = (v + r.cland[j]).astype(BF16)
            for q in range(1, ny):
                to = lax.rem(y + q, ny)
                remote(
                    r.yl.at[par, y, j],
                    r.yl.at[par, y, j],
                    r.y_s.at[k, q, j],
                    r.y_r.at[k, q, j],
                    (s, to * CORES + c),
                ).start()

        loop(nb, own_half)

    def psum_finish(k):
        par = k % 2

        def total(j):
            for q in range(1, ny):
                src = lax.rem(y + ny - q, ny)
                remote(
                    r.yl.at[par, src, j],
                    r.yl.at[par, src, j],
                    r.y_s.at[k, q, j],
                    r.y_r.at[k, q, j],
                    partner,
                ).wait_recv()
            v = r.yl[par, 0, j].astype(F32)
            for q in range(1, ny):
                v = v + r.yl[par, q, j].astype(F32)
            at = c * nb + j
            r.tot[at] = v
            remote(r.tot.at[at], r.tot.at[at], r.a_s.at[k, j], r.a_r.at[k, j], partner).start()

        loop(nb, total)

        def close(j):
            at = (1 - c) * nb + j
            remote(
                r.tot.at[at], r.tot.at[at], r.a_s.at[k, j], r.a_r.at[k, j], partner
            ).wait()
            remote(
                r.csend.at[j], r.cland.at[j], r.c_s.at[k, j], r.c_r.at[k, j], partner
            ).wait_send()
            for q in range(1, ny):
                remote(
                    r.yl.at[par, y, j],
                    r.yl.at[par, y, j],
                    r.y_s.at[k, q, j],
                    r.y_r.at[k, q, j],
                    partner,
                ).wait_send()

        loop(nb, close)

    def pairs_send(k):
        for q in range(1, nseq):
            start(
                lambda q=q: remote(
                    r.pk.at[k],
                    r.pf.at[k, s],
                    r.pf_s.at[k, q],
                    r.pf_r.at[k, q],
                    (s + q if k == 0 else s - q, m),
                ),
                lambda q=q: s + q < nseq if k == 0 else s - q >= 0,
            )

    def pairs_enter(k, reverse):
        for q in range(1, nseq):
            src = s + q if reverse else s - q

            @pl.when(src < nseq if reverse else src >= 0)
            def _(q=q, src=src):
                remote(
                    r.pk.at[k], r.pf.at[k, src], r.pf_s.at[k, q], r.pf_r.at[k, q], partner
                ).wait_recv()

        value = jnp.zeros((B, L), F32)
        for q in range(nseq - 1):
            at = nseq - 1 - q if reverse else q
            pair = r.pf[k, at]
            new = pair[0:B] * value + pair[B : 2 * B]
            value = jnp.where(at > s if reverse else at < s, new, value)
        return value

    def transposed(src, dst):
        def one(j):
            dst[lax.div(j, nx), lax.rem(j, nx)] = src[:, pl.ds(pl.multiple_of(j * DC, DC), DC)].T

        loop(nseq, one)

    def lanes(i):
        return pl.ds(pl.multiple_of(i * T, T), T)

    ez_half, ex_half = DC // CORES, nz // CORES

    def ez_part(e, src_z, core):
        rows = pl.ds(pl.multiple_of(core * ez_half, ez_half), ez_half)
        return r.ez.at[e, :, rows, lanes(src_z)]

    def ez_own(e):
        src = r.nmT if e else r.cotT
        return pltpu.make_async_copy(src.at[z], r.ez.at[e, :, :, lanes(z)], r.own_l.at[e])

    def ez_copy(e, k):
        to = lax.rem(z + k, nz)
        rows = pl.ds(pl.multiple_of(c * ez_half, ez_half), ez_half)
        return remote(
            (r.nmT if e else r.cotT).at[to, :, rows],
            ez_part(e, z, c),
            r.ez_s.at[e, k],
            r.ez_r.at[e, k],
            (to * nx + x, m),
        )

    def ez_relay_copy(e, k):
        part = ez_part(e, lax.rem(z + nz - k, nz), c)
        return remote(part, part, r.ezc_s.at[e, k], r.ezc_r.at[e, k], partner)

    def ez_send(e, left):
        for k in range(1, nz):
            if left:
                start(functools.partial(ez_copy, e, k), lambda k=k: z + k >= nz)
            else:
                start(functools.partial(ez_copy, e, k), lambda k=k: z + k < nz)

    def ez_relay(e):
        for k in range(1, nz):
            part = ez_part(e, lax.rem(z + nz - k, nz), c)
            remote(part, part, r.ez_s.at[e, k], r.ez_r.at[e, k], partner).wait_recv()
            start(functools.partial(ez_relay_copy, e, k))

    def ez_wait(e):
        ez_own(e).wait()
        for k in range(1, nz):
            part = ez_part(e, lax.rem(z + nz - k, nz), 1 - c)
            remote(part, part, r.ezc_s.at[e, k], r.ezc_r.at[e, k], partner).wait_recv()

    def ex_part(e, src_x, core):
        return r.ex.at[e, pl.ds(core * ex_half, ex_half), :, lanes(src_x)]

    def ex_own(e):
        src = r.gbT if e else r.nfT
        return pltpu.make_async_copy(src.at[:, x], r.ex.at[e, :, :, lanes(x)], r.own_l.at[2 + e])

    def ex_copy(e, k):
        to = lax.rem(x + k, nx)
        return remote(
            (r.gbT if e else r.nfT).at[pl.ds(c * ex_half, ex_half), to],
            ex_part(e, x, c),
            r.ex_xs.at[e, k],
            r.ex_xr.at[e, k],
            (z * nx + to, m),
        )

    def ex_relay_copy(e, k):
        part = ex_part(e, lax.rem(x + nx - k, nx), c)
        return remote(part, part, r.exc_s.at[e, k], r.exc_r.at[e, k], partner)

    def ex_send(e):
        ex_own(e).start()
        for k in range(1, nx):
            start(functools.partial(ex_copy, e, k))

    def ex_relay(e):
        for k in range(1, nx):
            part = ex_part(e, lax.rem(x + nx - k, nx), c)
            remote(part, part, r.ex_xs.at[e, k], r.ex_xr.at[e, k], partner).wait_recv()
            start(functools.partial(ex_relay_copy, e, k))

    def ex_wait(e):
        ex_own(e).wait()
        for k in range(1, nx):
            part = ex_part(e, lax.rem(x + nx - k, nx), 1 - c)
            remote(part, part, r.exc_s.at[e, k], r.exc_r.at[e, k], partner).wait_recv()

    def q_own(qb):
        return r.hd.at[qb] if qb < 3 else (r.gpg if qb == 3 else r.gpr)

    def q_land(qb, zo):
        return r.hz_d.at[qb, zo] if qb < 3 else r.hz_r.at[qb - 3, zo]

    def q_copy(qb, src, zo, way):
        to = s + nx if way == 0 else s - nx
        return remote(src, q_land(qb, zo), r.hz_s.at[qb, zo, way], r.hz_rs.at[qb, zo], (to, m))

    def q_send(qb):
        start(lambda: q_copy(qb, q_own(qb), z, 0), lambda: z < nz - 1)
        start(lambda: q_copy(qb, q_own(qb), z, 1), lambda: z > 0)

    def hx_ref(pb):
        return r.gp.at[pb] if pb < 6 else r.mx

    def hx_send(pb):
        def copy(k):
            to = lax.rem(x + k, nx)
            return remote(
                hx_ref(pb).at[x],
                hx_ref(pb).at[x],
                r.hx_s.at[pb, k],
                r.hx_r.at[pb, k],
                (z * nx + to, m),
            )

        for k in range(1, nx):
            start(functools.partial(copy, k))

    def hx_wait(pb):
        for k in range(1, nx):
            src = lax.rem(x + nx - k, nx)
            remote(
                hx_ref(pb).at[src],
                hx_ref(pb).at[src],
                r.hx_s.at[pb, k],
                r.hx_r.at[pb, k],
                partner,
            ).wait_recv()

    r.vecs[0 : d.taps] = r.conv_weight[...]
    for row, vector in enumerate((r.conv_bias, r.bias_a, r.bias_x, r.log_rate)):
        r.vecs[d.taps + row : d.taps + row + 1] = vector[...].reshape(1, L)
    r.gains[0:1] = r.gain_mix[...].reshape(1, D)
    r.gains[1:2] = r.gain_ffn[...].reshape(1, D)
    own_ids = r.ids[:, pl.ds(pl.multiple_of(s * G, G), G)]
    before = r.ids[:, pl.ds(pl.multiple_of(jnp.maximum(s - 1, 0) * G, G), G)]
    r.idp[...] = jnp.zeros((8, 2 * G), jnp.int32)
    r.idp[0:B, 0:G] = jnp.where(s > 0, before, -1)
    r.idp[0:B, G : 2 * G] = own_ids
    both = r.idp[...]
    square_row = lax.broadcasted_iota(jnp.int32, (G, G), 0)
    same = [
        jnp.where(pltpu.roll(both, k, 1)[:, G:] == both[:, G:], 1.0, 0.0) for k in range(1, d.taps)
    ]
    for b in range(B):
        square = jnp.zeros((G, G), F32)
        for k in range(1, d.taps):
            square = jnp.where(
                square_row == k, jnp.broadcast_to(same[k - 1][b : b + 1], (G, G)), square
            )
        r.mk[b, 0:G, :] = square.T
        r.mk[b, G : G + 8, :] = jnp.zeros((8, 128), F32)
    rates = r.vecs[7:8]
    r.rv[0:1] = -RATE_SCALE * softplus_small(rates)
    r.rv[1:2] = -RATE_SCALE * jax.nn.sigmoid(rates)
    r.sacc[...] = jnp.zeros((8, 8, L), F32)

    base = L * m + HW // 4
    shift = HW.bit_length() - 1
    turn = lax.rem(base, HW)
    turn_right = lax.rem(base + L, HW)

    def head_mask(first, count):
        row = lax.broadcasted_iota(jnp.int32, (count, L), 0) + first
        col = lax.broadcasted_iota(jnp.int32, (count, L), 1) + base
        return lax.shift_right_arithmetic(row, shift) == lax.shift_right_arithmetic(col, shift)

    pieces = [(p, min(HW, LP - p)) for p in range(0, LP, HW)]

    def recurrent_forward(wrec_v, wgel_v, wout_v, nm_v, nmh, pa, px, g2):
        ld_gel = local(r.w_gel, wgel_v, 1)
        ld_rec = local(r.w_rec, wrec_v, 2)
        ld_g = [
            local(gate, g2.at[i, pl.ds(at * HW, HW)], 3 + 2 * i + at)
            for i, gate in enumerate((r.gate_a, r.gate_x))
            for at in range(2)
        ]
        ld_out = local(r.w_out, wout_v, 7)
        ld_x.wait()

        def norm(i):
            at = rows16(i)
            v = r.x_v[at, :].astype(F32)
            scale = lax.rsqrt(jnp.mean(v * v, axis=1, keepdims=True) + EPS)
            nm_v[at, :] = (v * scale * r.gains[0:1]).astype(BF16)
            r.scm[at, :] = jnp.broadcast_to(scale, (16, 128))

        loop(T // 16, norm)
        ld_gel.wait()
        r.pre_gel[...] = dot(nm_v[...], wgel_v[...])
        ld_rec.wait()
        main = dot(nm_v[...], wrec_v[...]).astype(BF16).astype(F32)
        for b in range(B):
            r.extp[b, 16 : 16 + G, :] = main[b * G : (b + 1) * G]

        if LP > L:
            for wide in (r.cv, r.gpg, r.gpr, r.mx.at[x]):
                wide[:, L:] = jnp.zeros((T, LP - L), BF16)

        def conv(i):
            for b in range(B):
                window = r.extp[b, pl.ds(pl.multiple_of(i * 16 + 8, 8), 24), :]
                keep = r.mk[b, rows16(i), :]
                acc = r.vecs[4:5] + r.vecs[0:1] * window[8:24]
                for k in range(1, d.taps):
                    acc = acc + r.vecs[k : k + 1] * (keep[:, k : k + 1] * window[8 - k : 24 - k])
                at = rows16(i, b * G)
                r.cv[at, 0:L] = acc.astype(BF16)
                r.st_l[at, :] = acc[:, :HW].astype(BF16)
                r.st_r[at, :] = acc[:, L - HW :].astype(BF16)

        def neighbours(b, side, first):
            rows = pl.ds(b * G, 16) if first else pl.ds(b * G + 16, G - 16)
            src, dst, to = (r.st_r, r.hl, right_m) if side else (r.st_l, r.hr, left_m)
            i = 4 * b + 2 * side + first
            return remote(src.at[rows], dst.at[rows], r.ex_s.at[i], r.ex_r.at[i], (s, to))

        loop(G // 16 - 1, lambda i: conv(i + 1))
        ld_cot.wait()
        transposed(r.cot_v, r.cotT)
        pl.semaphore_wait(barrier, nseq - 1 + nm - 1)

        for b in range(B):
            start(
                lambda b=b: remote(
                    r.x_in.at[pl.ds(b * G + G - 16, 16)],
                    r.xh.at[pl.ds(b * 16, 16)],
                    r.halo_s.at[b],
                    r.halo_r.at[b],
                    (s + 1, m),
                ),
                lambda: s < nseq - 1,
            )

        for b in range(B):
            for side in range(2):
                start(functools.partial(neighbours, b, side, 0))

        @pl.when(s > 0)
        def _():
            for b in range(B):
                remote(
                    r.x_in.at[pl.ds(b * G + G - 16, 16)],
                    r.xh.at[pl.ds(b * 16, 16)],
                    r.halo_s.at[b],
                    r.halo_r.at[b],
                    partner,
                ).wait_recv()

        @pl.when(s == 0)
        def _():
            r.xh[...] = jnp.zeros((B * 16, D), BF16)

        for b in range(B):
            v = r.xh[b * 16 : (b + 1) * 16, :].astype(F32)
            scale = lax.rsqrt(jnp.mean(v * v, axis=1, keepdims=True) + EPS)
            nmh[b * 16 : (b + 1) * 16, :] = (v * scale * r.gains[0:1]).astype(BF16)
        rim = dot(nmh[...], wrec_v[...]).astype(BF16).astype(F32)
        for b in range(B):
            r.extp[b, 0:16, :] = rim[b * 16 : (b + 1) * 16]

        conv(0)
        for b in range(B):
            for side in range(2):
                start(functools.partial(neighbours, b, side, 1))

        for copy in ld_g:
            copy.wait()
        for i in range(2):
            table = g2[i, pl.ds(pl.multiple_of(turn, HW // 4), HW), :].astype(F32)
            table_right = g2[i, pl.ds(pl.multiple_of(turn_right, HW // 4), HW), :].astype(F32)
            r.wl[i] = jnp.where(head_mask(base - HW, HW), table, 0.0).astype(BF16)
            r.wr[i] = jnp.where(head_mask(base + L, HW), table_right, 0.0).astype(BF16)
            for p, n in pieces:
                r.wo[i, p : p + n, :] = jnp.where(head_mask(base + p, n), table[:n], 0.0).astype(
                    BF16
                )
        pa[...] = dot(r.cv[...], r.wo[0]) + r.vecs[5:6]
        px[...] = dot(r.cv[...], r.wo[1]) + r.vecs[6:7]
        for i in range(4 * B):
            neighbours(i // 4, i // 2 % 2, i % 2).wait_recv()
        pa[...] += dot(r.hl[...], r.wl[0]) + dot(r.hr[...], r.wr[0])
        px[...] += dot(r.hl[...], r.wl[1]) + dot(r.hr[...], r.wr[1])

        def scan(i, carry):
            out = []
            for b in range(B):
                decay_in, state_in = carry[2 * b], carry[2 * b + 1]
                at = rows16(i, b * G)
                recur = jax.nn.sigmoid(pa[at, :])
                inject = jax.nn.sigmoid(px[at, :])
                log_decay = r.rv[0:1] * recur
                decay = jnp.exp(log_decay)
                spread = jnp.sqrt(minus_expm1(2.0 * log_decay))
                drive = spread * inject * r.cv[at, 0:L].astype(F32)
                coeff = decay * r.mk[b, rows16(i), :][:, 1:2]
                r.recur[at, :] = recur
                r.inj[at, :] = inject
                r.cfp[b, rows16(i), :] = coeff
                for h in range(2):
                    a, v = scan_tile(
                        coeff[8 * h : 8 * h + 8], drive[8 * h : 8 * h + 8], reverse=False
                    )
                    v = v + a * state_in
                    a = a * decay_in
                    decay_in, state_in = a[7:8], v[7:8]
                    r.aloc[pl.ds(pl.multiple_of(b * G + i * 16 + 8 * h, 8), 8), :] = a
                    r.stp[b, pl.ds(pl.multiple_of(8 + i * 16 + 8 * h, 8), 8), :] = v
                out += [decay_in, state_in]
            return tuple(out)

        one, zero = jnp.ones((1, L), F32), jnp.zeros((1, L), F32)
        ends = lax.fori_loop(0, G // 16, scan, (one, zero) * B)
        for b in range(B):
            r.pk[0, b : b + 1, :] = ends[2 * b]
            r.pk[0, B + b : B + b + 1, :] = ends[2 * b + 1]
            r.cfp[b, G : G + 8, :] = jnp.ones((8, L), F32)
        pairs_send(0)
        transposed(nm_v, r.nmT)
        for e in range(2):
            ez_own(e).start()
            ez_send(e, True)
        entered = pairs_enter(0, False)
        for b in range(B):
            r.stp[b, 0:8, :] = jnp.broadcast_to(entered[b : b + 1], (8, L))

        def states(i):
            for b in range(B):
                at = rows16(i, b * G)
                here = pl.ds(pl.multiple_of(8 + i * 16, 8), 16)
                state = r.stp[b, here, :] + r.aloc[at, :] * r.stp[b, 7:8, :]
                r.stp[b, here, :] = state
                r.mx[x, at, 0:L] = (state * gelu_tanh(r.pre_gel[at, :])).astype(BF16)

        loop(G // 16, states)
        ld_out.wait()
        psum_start(
            0,
            lambda col: dot(r.mx[x, :, 0:L], wout_v[:, pl.ds(pl.multiple_of(col, CB), CB)]),
        )
        hx_send(6)

    pl.run_scoped(
        recurrent_forward,
        pltpu.VMEM((D, L), BF16),
        pltpu.VMEM((D, L), BF16),
        pltpu.VMEM((L, D), BF16),
        pltpu.VMEM((T, D), BF16),
        pltpu.VMEM((B * 16, D), BF16),
        pltpu.VMEM((T, L), F32),
        pltpu.VMEM((T, L), F32),
        pltpu.VMEM((2, 2 * HW, L), BF16),
    )

    def feed_forward(wd_v, wg_v, wu_v, nf, gh, pg, pu):
        ld_d = [local(r.w_down.at[pl.ds(i * FB, FB)], wd_v.at[i], i) for i in range(3)]
        ld_g = [local(r.w_gate.at[:, pl.ds(i * FB, FB)], wg_v.at[i], 3 + i) for i in range(3)]
        ld_u = [local(r.w_up.at[:, pl.ds(i * FB, FB)], wu_v.at[i], 6 + i) for i in range(3)]
        for i in range(3):
            ld_d[i].wait()

        def hidden_grad(i):
            gh[i] = dot_nt(r.cot_v[...], wd_v[i])

        loop(3, hidden_grad)
        for e in range(2):
            ez_send(e, False)
        psum_finish(0)

        def residual(i):
            at = rows16(i)
            parts = [
                r.tot[j, at, :] + r.x_v[at, j * CB : (j + 1) * CB].astype(F32)
                for j in range(2 * nb)
            ]
            square = parts[0] * parts[0]
            for v in parts[1:]:
                square = square + v * v
            scale = lax.rsqrt(jnp.sum(square, axis=1, keepdims=True) / D + EPS)
            for j, v in enumerate(parts):
                cols = slice(j * CB, (j + 1) * CB)
                r.resid[at, cols] = v
                nf[at, cols] = (v * scale * r.gains[1:2, cols]).astype(BF16)
            r.scf[at, :] = jnp.broadcast_to(scale, (16, 128))

        loop(T // 16, residual)
        for i in range(3):
            ld_g[i].wait()
            ld_u[i].wait()

        for i in range(3):
            pg[...] = dot(nf[...], wg_v[i])
            pu[...] = dot(nf[...], wu_v[i])

            def units(t, i=i):
                at = rows16(t)
                up, back = pu[at, :], gh[i, at, :]
                active, slope = gelu_and_slope(pg[at, :])
                r.hd[i, at, :] = (active * up).astype(BF16)
                r.gp[2 * i, x, at, :] = (back * up * slope).astype(BF16)
                r.gp[2 * i + 1, x, at, :] = (back * active).astype(BF16)

            loop(T // 16, units)
            q_send(i)
            if i == 0:
                transposed(nf, r.nfT)
                ex_send(0)
            if i < 2:
                hx_send(2 * i)
            if i == 0:
                hx_send(1)

        def back_input(col):
            at = pl.ds(pl.multiple_of(col, CB), CB)
            v = dot_nt(r.gp[0, x], wg_v[0, at, :]) + dot_nt(r.gp[1, x], wu_v[0, at, :])
            for i in range(1, 3):
                v = v + dot_nt(r.gp[2 * i, x], wg_v[i, at, :])
                v = v + dot_nt(r.gp[2 * i + 1, x], wu_v[i, at, :])
            return v

        psum_start(1, back_input)

        def ffn_term(j):
            at = pl.ds(pl.multiple_of(j * CB, CB), CB)
            v = dot(r.hd[0], wd_v[0, :, at])
            for i in range(1, 3):
                v = v + dot(r.hd[i], wd_v[i, :, at])
            r.fo[j] = v.astype(BF16)

        loop(2 * nb, ffn_term)
        ex_relay(0)
        ez_relay(0)
        ez_relay(1)

    pl.run_scoped(
        feed_forward,
        pltpu.VMEM((3, FB, D), BF16),
        pltpu.VMEM((3, D, FB), BF16),
        pltpu.VMEM((3, D, FB), BF16),
        pltpu.VMEM((T, D), BF16),
        pltpu.VMEM((3, T, FB), F32),
        pltpu.VMEM((T, FB), F32),
        pltpu.VMEM((T, FB), F32),
    )

    def gain_rows(which):
        total = jnp.sum(r.gacc[...], axis=0, keepdims=True)
        for q in range(nseq):
            r.gsend[q, which : which + 1, :] = total[:, q * DC : (q + 1) * DC]

    def after_feed_forward(stage_f, load_f, own_st, hload, qstage):
        tail = []
        seen = [dict() for _ in range(nz)]

        def once(zz, *what):
            first = what not in seen[zz]
            seen[zz][what] = True
            return first

        def at_end(zz, make):
            seen[zz].setdefault("sent", []).append(make)

        def sized(ref, n):
            return ref if n == ref.shape[-1] else ref.at[:, pl.ds(0, n)]

        def own_write(zz, src, ref):
            turn_ = seen[zz].get("turn", 0)
            seen[zz]["turn"] = turn_ + 1
            at, n = turn_ % 2, src.shape[-1]

            def copy():
                return pltpu.make_async_copy(sized(own_st.at[at], n), ref(), r.ow.at[4 + at])

            held = seen[zz].setdefault("held", {})
            if at in held:
                held[at]().wait()
            sized(own_st.at[at], n)[...] = src.astype(BF16)
            copy().start()
            held[at] = copy

        def p_width(b):
            return FB if b < 6 else LP

        def p_stage(zz, b, zc):
            at = zc if zc < zz else zc - 1
            return stage_f.at[b % RING, at] if b < 6 else tail[0].at[at]

        def p_land(b, place):
            return r.land_f.at[b, place] if b < 6 else r.land_o.at[place]

        def p_part(zz, b, zc):
            if once(zz, "hx", b):
                hx_wait(b)
            e = 0 if b < 6 else 1
            if once(zz, "ex", e):
                ex_wait(e)
            return dot(r.ex[e, zc], hx_ref(b)[...].reshape(nx * T, p_width(b)))

        def p_copy(zz, b, zc, place, to):
            return remote(
                p_stage(zz, b, zc), p_land(b, place), r.p_s.at[b, zc], r.p_r.at[b, place], (to, m)
            )

        def do_p(zz, b, way, zc):
            right = way > 0
            has_input = zz > 0 if right else zz < nz - 1
            place = abs(zc - zz) + (0 if right else nz - 1)
            load = load_f if b < 6 else tail[1]
            if has_input:
                fetch = pltpu.make_async_copy(p_land(b, place), load, r.pl_s.at[0])
                p_copy(zz, b, zc, place, s).wait_recv()
                fetch.start()
            v = p_part(zz, b, zc)
            if has_input:
                fetch.wait()
                v = v + load[...].astype(F32)
            if RING <= b < 6:
                p_copy(zz, b - RING, zc, 0, s).wait_send()
            p_stage(zz, b, zc)[...] = v.astype(BF16)
            p_copy(zz, b, zc, place - 1, s + nx if right else s - nx).start()
            if b >= 6 - RING:
                at_end(zz, lambda: p_copy(zz, b, zc, 0, s).wait_send())

        def do_own(zz, b):
            own_write(zz, p_part(zz, b, zz), lambda: r.own_f.at[b] if b < 6 else r.own_o)

        def q_arrived(zz, qb, zo):
            if once(zz, "hz", qb, zo):
                q_copy(qb, q_land(qb, zo), zo, 0 if zo < zz else 1).wait_recv()

        def do_forward(zz, qb, zo):
            q_arrived(zz, qb, zo)
            way, to = (0, zz + 1) if zo < zz else (1, zz - 1)
            if 0 <= to < nz:
                q_copy(qb, q_land(qb, zo), zo, way).start()
                at_end(zz, lambda: q_copy(qb, q_land(qb, zo), zo, way).wait_send())

        def q_exchange(qb, k, n):
            to = lax.rem(x + k, nx)
            land = r.xr_d.at[qb, nx - k - 1] if qb < 3 else r.xr_r.at[qb - 3, nx - k - 1]
            return remote(
                sized(qstage.at[qb, k - 1], n),
                land,
                r.xr_s.at[qb, k],
                r.xr_rs.at[qb, k],
                (z * nx + to, m),
            )

        def do_q(zz, qb):
            e, n, own = (0, FB, q_own(qb)) if qb < 3 else (1, LP, q_own(qb))

            def piece(zo):
                return hload.at[zo] if n == d.W else hload.at[zo, :, pl.ds(0, n)]

            def fetch(zo):
                src = own if zo == zz else q_land(qb, zo)
                return pltpu.make_async_copy(src, piece(zo), r.ow.at[8 + zo])

            for zo in range(nz):
                if zo != zz:
                    q_arrived(zz, qb, zo)
                fetch(zo).start()
            if once(zz, "ez", e):
                ez_wait(e)
            for zo in range(nz):
                fetch(zo).wait()
            gathered = hload[:, :, 0:n].reshape(nz * T, n)
            for k in range(1, nx):
                v = dot(r.ez[e, lax.rem(x + k, nx)], gathered)
                sized(qstage.at[qb, k - 1], n)[...] = v.astype(BF16)
                q_exchange(qb, k, n).start()
            at_end(zz, lambda: [q_exchange(qb, k, n).wait_send() for k in range(1, nx)])
            own_write(
                zz,
                dot(r.ez[e, x], gathered),
                lambda: r.own_d.at[qb] if qb < 3 else r.own_r.at[qb - 3],
            )

        def work(point):
            for zz in range(nz):

                @pl.when(z == zz)
                def _(zz=zz):
                    for op in SCHEDULE[point][zz]:
                        kind, rest = op[0], op[1:]
                        {"F": do_forward, "P": do_p, "O": do_own, "Q": do_q}[kind](zz, *rest)

        def close():
            for zz in range(nz):

                @pl.when(z == zz)
                def _(zz=zz):
                    for copy in seen[zz].get("held", {}).values():
                        copy().wait()
                    for make in seen[zz].get("sent", []):
                        make()
                    for b in range(7):
                        for place, there in ((0, zz > 0), (nz - 1, zz < nz - 1)):
                            if there:
                                p_copy(zz, b, (zz + 1) % nz, place, s).wait_recv()
                    for qb in range(5):
                        for k in range(1, nx):
                            q_exchange(qb, k, FB if qb < 3 else LP).wait_recv()

        def recurrent_backward(
            w_v, wout_v, gr, gb, gm, gcd, gcp, gmel, gpa, gpx, adj, t2
        ):
            ld_gel = local(r.w_gel, w_v, 2)
            ld_out = local(r.w_out, wout_v, 3)
            r.gsend[...] = jnp.zeros((nseq, 8, DC), F32)
            work(1)
            psum_finish(1)
            r.gacc[...] = jnp.zeros((16, D), F32)

            def norm_back(i):
                at = rows16(i)
                scale = r.scf[at, :][:, 0:1]
                inner = jnp.zeros((16, CB), F32)
                for j in range(2 * nb):
                    cols = slice(j * CB, (j + 1) * CB)
                    inner = inner + r.tot[j, at, :] * r.gains[1:2, cols] * r.resid[at, cols]
                factor = (scale * scale * scale) * (jnp.sum(inner, axis=1, keepdims=True) / D)
                for j in range(2 * nb):
                    cols = slice(j * CB, (j + 1) * CB)
                    n, v = r.tot[j, at, :], r.resid[at, cols]
                    r.gacc[:, cols] += n * v * scale
                    grad = r.cot_v[at, cols].astype(F32) + (
                        scale * (n * r.gains[1:2, cols]) - v * factor
                    )
                    gr[at, cols] = grad
                    gb[at, cols] = grad.astype(BF16)

            loop(T // 16, norm_back)
            gain_rows(1)
            ld_out.wait()
            gm[...] = dot_nt(gb[...], wout_v[...])

            def scan(t, carry):
                i = G // 16 - 1 - t
                out = []
                for b in range(B):
                    decay_in, value_in = carry[2 * b], carry[2 * b + 1]
                    at = rows16(i, b * G)
                    gate, slope = gelu_and_slope(r.pre_gel[at, :])
                    g = gm[at, :]
                    state = r.stp[b, pl.ds(pl.multiple_of(8 + i * 16, 8), 16), :]
                    r.gpg[at, 0:L] = (g * state * slope).astype(BF16)
                    value16 = g * gate
                    following = r.cfp[b, pl.ds(pl.multiple_of(i * 16, 16), 24), :][1:17]
                    for h in (1, 0):
                        a, v = scan_tile(
                            following[8 * h : 8 * h + 8], value16[8 * h : 8 * h + 8], reverse=True
                        )
                        v = v + a * value_in
                        a = a * decay_in
                        decay_in, value_in = a[0:1], v[0:1]
                        here = pl.ds(pl.multiple_of(b * G + i * 16 + 8 * h, 8), 8)
                        r.aloc[here, :] = a
                        adj[here, :] = v
                    out += [decay_in, value_in]
                return tuple(out)

            one, zero = jnp.ones((1, L), F32), jnp.zeros((1, L), F32)
            ends = lax.fori_loop(0, G // 16, scan, (one, zero) * B)
            for b in range(B):
                first = r.cfp[b, 0:1, :]
                r.pk[1, b : b + 1, :] = first * ends[2 * b]
                r.pk[1, B + b : B + b + 1, :] = first * ends[2 * b + 1]
            pairs_send(1)
            for b in (3, 4, 5):
                hx_send(b)
            q_send(3)
            ld_gel.wait()

            def gel_term(j):
                at = pl.ds(pl.multiple_of(j * CB, CB), CB)
                gmel[j] = dot_nt(r.gpg[:, 0:L], w_v[at, :])

            loop(2 * nb, gel_term)
            ld_rec = local(r.w_rec, w_v, 1)
            transposed(gb, r.gbT)
            ex_send(1)
            work(2)
            outer = pairs_enter(1, True)

            def gate_back(i):
                for b in range(B):
                    at = rows16(i, b * G)
                    adjoint = adj[at, :] + r.aloc[at, :] * outer[b : b + 1]
                    recur, inject = r.recur[at, :], r.inj[at, :]
                    log_decay = r.rv[0:1] * recur
                    decay = jnp.exp(log_decay)
                    value = r.cv[at, 0:L].astype(F32)
                    spread = jnp.sqrt(minus_expm1(2.0 * log_decay))
                    prior = r.stp[b, pl.ds(pl.multiple_of(i * 16, 16), 24), :][7:23]
                    keep = r.mk[b, rows16(i), :][:, 1:2]
                    grad_log = (
                        adjoint * inject * value * (-(decay * decay) / spread)
                        + adjoint * prior * keep * decay
                    )
                    ga = (grad_log * r.rv[0:1] * recur * (1.0 - recur)).astype(BF16)
                    direct = adjoint * spread * inject
                    gx = (adjoint * spread * value * inject * (1.0 - inject)).astype(BF16)
                    gpa[at, :] = ga
                    gpx[at, :] = gx
                    gcd[at, :] = direct
                    r.sacc[5] += fold8(ga.astype(F32))
                    r.sacc[6] += fold8(gx.astype(F32))
                    r.sacc[7] += fold8(grad_log * recur)

            loop(G // 16, gate_back)
            r.gs_l[...] = (dot_nt(gpa[...], r.wl[0]) + dot_nt(gpx[...], r.wl[1])).astype(BF16)

            def to_left():
                return remote(r.gs_l, r.gi_r, r.gi_s.at[0], r.gi_rs.at[0], (s, left_m))

            start(to_left)
            r.gs_r[...] = (dot_nt(gpa[...], r.wr[0]) + dot_nt(gpx[...], r.wr[1])).astype(BF16)

            def to_right():
                return remote(r.gs_r, r.gi_l, r.gi_s.at[1], r.gi_rs.at[1], (s, right_m))

            start(to_right)
            own = dot_nt(gpa[...], r.wo[0]) + dot_nt(gpx[...], r.wo[1])
            gcd[...] += own[:, 0:L]

            for i, grad in enumerate((gpa, gpx)):
                turned = jnp.where(head_mask(base - HW, HW), dot(r.hl[...].T, grad[...]), 0.0)
                t2[0:HW, :] = turned
                for p, n in pieces:
                    part = dot(r.cv[:, p : p + n].T, grad[...])
                    t2[0:n, :] += jnp.where(head_mask(base + p, n), part, 0.0)
                t2[HW : 2 * HW, :] = t2[0:HW, :]
                back = pl.multiple_of(lax.rem(HW - turn, HW), HW // 4)
                table = t2[pl.ds(back, HW), :]
                right = jnp.where(head_mask(base + L, HW), dot(r.hr[...].T, grad[...]), 0.0)
                t2[0:HW, :] = right
                t2[HW : 2 * HW, :] = right
                back = pl.multiple_of(lax.rem(HW - turn_right, HW), HW // 4)
                table = (table + t2[pl.ds(back, HW), :]).astype(BF16)
                for q in range(nseq):
                    r.gt[q // nx, q % nx, i] = table[q * d.GR : (q + 1) * d.GR]

            work(3)
            to_left().wait_recv()
            to_right().wait_recv()
            gcd[:, 0:HW] += r.gi_l[...].astype(F32)
            gcd[:, L - HW : L] += r.gi_r[...].astype(F32)
            for b in range(B):
                gcp[b, 0:G, :] = gcd[b * G : (b + 1) * G, :]
                gcp[b, G : G + 8, :] = jnp.zeros((8, L), F32)

            for b in range(B):
                top, keep = gcp[b, 0:8, :], r.mk[b, 0:8, :]
                spill = jnp.zeros((8, L), F32)
                row = lax.broadcasted_iota(jnp.int32, (8, L), 0)
                for k in range(1, d.taps):
                    moved = pltpu.roll(r.vecs[k : k + 1] * (keep[:, k : k + 1] * top), 8 - k, 0)
                    spill = spill + jnp.where(row >= 8 - k, moved, 0.0)
                r.sp_s[b * 8 : (b + 1) * 8, :] = spill

            def spilled():
                return remote(r.sp_s, r.sp_r, r.sp_ss.at[0], r.sp_rs.at[0], (s - 1, m))

            start(spilled, lambda: s > 0)

            @pl.when(s == nseq - 1)
            def _():
                r.sp_r[...] = jnp.zeros((B * 8, L), F32)

            def conv_back(i, spill):
                for b in range(B):
                    grads = gcp[b, pl.ds(pl.multiple_of(i * 16, 16), 24), :]
                    keep = r.mk[b, pl.ds(pl.multiple_of(i * 16, 16), 24), :]
                    window = r.extp[b, pl.ds(pl.multiple_of(i * 16 + 8, 8), 24), :]
                    here = grads[0:16]
                    out = r.vecs[0:1] * here
                    if not spill:
                        r.sacc[4] += fold8(here)
                        r.sacc[0] += fold8(here * window[8:24])
                    for k in range(1, d.taps):
                        masked = keep[:, k : k + 1] * grads
                        out = out + r.vecs[k : k + 1] * masked[k : k + 16]
                        if not spill:
                            r.sacc[k] += fold8(masked[0:16] * window[8 - k : 24 - k])
                    if spill:
                        extra = r.sp_r[b * 8 : (b + 1) * 8, :]
                        out = out + jnp.concatenate([jnp.zeros((8, L), F32), extra], axis=0)
                    r.gpr[rows16(i, b * G), 0:L] = out.astype(BF16)

            loop(G // 16, lambda i: conv_back(i, False))
            for k in range(8):
                r.smv[k : k + 1, :] = jnp.sum(r.sacc[k], axis=0, keepdims=True)

            work(4)

            @pl.when(s < nseq - 1)
            def _():
                spilled().wait_recv()

            conv_back(G // 16 - 1, True)
            q_send(4)
            ld_rec.wait()

            def mix_term(col):
                at = pl.ds(pl.multiple_of(col, CB), CB)
                return dot_nt(r.gpr[:, 0:L], w_v[at, :]) + gmel[lax.div(col, CB)]

            psum_start(2, mix_term)

            def small_x(k):
                to = lax.rem(x + k, nx)
                return remote(
                    r.smv, r.smx.at[x], r.smx_s.at[k], r.smx_r.at[k], (z * nx + to, m)
                )

            def gates_x(k):
                to = lax.rem(x + k, nx)
                return remote(
                    r.gt.at[:, to], r.gtx.at[x], r.gtx_s.at[k], r.gtx_r.at[k], (z * nx + to, m)
                )

            def small_z(k):
                to = lax.rem(z + k, nz)
                return remote(
                    r.smv, r.smz.at[z], r.smz_s.at[k], r.smz_r.at[k], (to * nx + x, m)
                )

            def gates_z(k):
                to = lax.rem(z + k, nz)
                return remote(
                    r.gts.at[to], r.gtz.at[z], r.gtz_s.at[k], r.gtz_r.at[k], (to * nx + x, m)
                )

            def gain_copy(q):
                to = lax.rem(s + q, nseq)
                return remote(r.gsend.at[to], r.gland.at[s], r.ga_s.at[q], r.ga_r.at[q], (to, m))

            for k in range(1, nx):
                small_x(k).start()
                gates_x(k).start()
            ex_relay(1)
            work(5)
            psum_finish(2)

            r.gacc[...] = jnp.zeros((16, D), F32)

            def norm_back_mix(i):
                at = rows16(i)
                scale = r.scm[at, :][:, 0:1]
                inner = jnp.zeros((16, CB), F32)
                for j in range(2 * nb):
                    cols = slice(j * CB, (j + 1) * CB)
                    v = r.x_v[at, cols].astype(F32)
                    inner = inner + r.tot[j, at, :] * r.gains[0:1, cols] * v
                factor = (scale * scale * scale) * (jnp.sum(inner, axis=1, keepdims=True) / D)
                for j in range(2 * nb):
                    cols = slice(j * CB, (j + 1) * CB)
                    n, v = r.tot[j, at, :], r.x_v[at, cols].astype(F32)
                    r.gacc[:, cols] += n * v * scale
                    gr[at, cols] = gr[at, cols] + (scale * (n * r.gains[0:1, cols]) - v * factor)

            loop(T // 16, norm_back_mix)
            out_gin = pltpu.make_async_copy(gr, r.k_gin, r.ow.at[0])
            out_gin.start()
            gain_rows(0)
            for q in range(1, nseq):
                start(functools.partial(gain_copy, q))

            psum_start(3, lambda col: r.fo[lax.div(col, CB)].astype(F32))
            small, gates = r.smv[...], r.gt[:, x].astype(F32)
            for k in range(1, nx):
                src = lax.rem(x + nx - k, nx)
                remote(r.smv, r.smx.at[src], r.smx_s.at[k], r.smx_r.at[k], partner).wait_recv()
                remote(r.gt.at[:, x], r.gtx.at[src], r.gtx_s.at[k], r.gtx_r.at[k], partner).wait()
                small_x(k).wait_send()
            for k in range(1, nx):
                src = lax.rem(x + nx - k, nx)
                small = small + r.smx[src]
                gates = gates + r.gtx[src].astype(F32)
            r.smv[...] = small
            r.gts[...] = gates.astype(BF16)
            for k in range(1, nz):
                start(functools.partial(small_z, k))
                start(functools.partial(gates_z, k))
            work(6)
            psum_finish(3)

            def block_out(i):
                at = rows16(i)
                for j in range(2 * nb):
                    cols = slice(j * CB, (j + 1) * CB)
                    r.resid[at, cols] += r.tot[j, at, :]

            loop(T // 16, block_out)
            out_block = pltpu.make_async_copy(r.resid, r.k_block, r.ow.at[1])
            out_block.start()

            out_gin.wait()
            out_block.wait()

        pl.run_scoped(
            recurrent_backward,
            pltpu.VMEM((D, L), BF16),
            pltpu.VMEM((L, D), BF16),
            pltpu.VMEM((T, D), F32),
            pltpu.VMEM((T, D), BF16),
            pltpu.VMEM((T, L), F32),
            pltpu.VMEM((T, L), F32),
            pltpu.VMEM((B, G + 8, L), F32),
            pltpu.VMEM((2 * nb, T, CB), F32),
            pltpu.VMEM((T, L), BF16),
            pltpu.VMEM((T, L), BF16),
            pltpu.VMEM((T, L), F32),
            pltpu.VMEM((2 * HW, L), F32),
        )


        def rest(stage_o, load_o):
            tail.extend((stage_o, load_o))
            work(7)
            close()

        pl.run_scoped(rest, pltpu.VMEM((nz - 1, DC, LP), BF16), pltpu.VMEM((DC, LP), BF16))

        for q in range(1, nseq):
            src = lax.rem(s + nseq - q, nseq)
            remote(
                r.gsend.at[src], r.gland.at[src], r.ga_s.at[q], r.ga_r.at[q], partner
            ).wait_recv()
        for k in range(1, nz):
            src = lax.rem(z + nz - k, nz)
            remote(r.smv, r.smz.at[src], r.smz_s.at[k], r.smz_r.at[k], partner).wait_recv()
            remote(
                r.gts.at[src], r.gtz.at[src], r.gtz_s.at[k], r.gtz_r.at[k], partner
            ).wait_recv()
        r.gland[s] = r.gsend[s]
        r.smz[z] = r.smv[...]
        r.gtz[z] = r.gts[z]
        small, gates, gain = r.smz[0], r.gtz[0].astype(F32), r.gland[0]
        for q in range(1, nz):
            small = small + r.smz[q]
            gates = gates + r.gtz[q].astype(F32)
        for q in range(1, nseq):
            gain = gain + r.gland[q]
        r.k_small[...] = jnp.zeros((8, LP), F32)
        r.k_small[:, 0:L] = small
        r.k_small[7:8, 0:L] = small[7:8, :] * r.rv[1:2, :]
        r.k_gain[...] = gain
        r.k_gates[...] = gates

        for make, when in pending:
            if when is None:
                make().wait_send()
            else:
                pl.when(when())(lambda make=make: make().wait_send())

    pl.run_scoped(
        after_feed_forward,
        pltpu.VMEM((RING, nz - 1, DC, FB), BF16),
        pltpu.VMEM((DC, FB), BF16),
        pltpu.VMEM((2, DC, d.W), BF16),
        pltpu.VMEM((nz, T, d.W), BF16),
        pltpu.VMEM((5, nx - 1, DC, d.W), BF16),
    )


def finish(d, r):
    L, LP, FB, DC, nseq, nz, nx = d.L, d.LP, d.FB, d.DC, d.nseq, d.nz, d.nx
    s = lax.axis_index("seq")
    z = lax.div(s, nx)
    copies, loads, used = [], [], [0]

    def copy(src, dst):
        used[0] += 1
        return pltpu.make_async_copy(src, dst, r.sem.at[used[0] - 1])

    def load(*pairs):
        group = [copy(*pair) for pair in pairs]
        for one in group:
            one.start()
        loads.append(group)

    far = nz - 1
    for b in range(6):
        load((r.own_f.at[b], r.a_f.at[b]), (r.land_f.at[b, 0], r.b_f.at[b]), (r.land_f.at[b, far], r.c_f.at[b]))
    load((r.own_o, r.a_o), (r.land_o.at[0], r.b_o), (r.land_o.at[far], r.c_o))
    for qb in range(3):
        load((r.own_d.at[qb], r.a_d.at[qb]), (r.xr_d.at[qb], r.b_d.at[qb]))
    for qb in range(2):
        load((r.own_r.at[qb], r.a_r.at[qb]), (r.xr_r.at[qb], r.b_r.at[qb]))
    load((r.k_block, r.w_block))
    load((r.k_gin, r.w_gin))

    def write(buf, ref):
        one = copy(buf, ref)
        one.start()
        copies.append(one)

    def emit(value, buf, ref):
        buf[...] = value
        write(buf, ref)

    def chained(a, left, right):
        v = a.astype(F32) + jnp.where(z > 0, left.astype(F32), 0.0)
        return v + jnp.where(z < nz - 1, right.astype(F32), 0.0)

    def arrived(i):
        for one in loads[i]:
            one.wait()

    for b in range(6):
        arrived(b)
        ref = r.o_wup if b % 2 else r.o_wgate
        v = chained(r.a_f[b], r.b_f[b], r.c_f[b])
        emit(v, r.v_f.at[b], ref.at[:, b // 2 * FB : (b // 2 + 1) * FB])
    arrived(6)
    emit(chained(r.a_o[...], r.b_o[...], r.c_o[...]).T[0:L], r.v_o, r.o_wout)
    for qb in range(5):
        arrived(7 + qb)
        a, b = (r.a_d[qb], r.b_d[qb]) if qb < 3 else (r.a_r[qb - 3], r.b_r[qb - 3])
        v = a.astype(F32)
        for k in range(nx - 1):
            v = v + b[k].astype(F32)
        if qb < 3:
            emit(v.T, r.v_d.at[qb], r.o_wdown.at[qb * FB : (qb + 1) * FB])
        else:
            emit(v[:, 0:L], r.v_r.at[qb - 3], r.o_wgel if qb == 3 else r.o_wrec)

    arrived(12)
    write(r.w_block, r.o_block)
    arrived(13)
    write(r.w_gin, r.o_gin)
    part = L // nseq
    small = pltpu.roll(r.k_small[...], lax.rem(LP - s * part, LP), 1)
    r.o_cw[...] = small[0:4, 0:part]
    r.o_cb[...] = small[4, 0:part]
    r.o_ba[...] = small[5, 0:part]
    r.o_bx[...] = small[6, 0:part]
    r.o_lr[...] = small[7, 0:part]
    r.o_gm[...] = r.k_gain[0, :]
    r.o_gf[...] = r.k_gain[1, :]
    r.o_ga[...] = r.k_gates[0]
    r.o_gx[...] = r.k_gates[1]
    for one in copies:
        one.wait()


IN_ANY = ("x_in", "w_rec", "w_gel", "w_out", "gate_a", "gate_x", "w_gate", "w_up", "w_down", "cot")
IN_VMEM = (
    "ids", "gain_mix", "gain_ffn", "conv_weight", "conv_bias", "bias_a", "bias_x", "log_rate"
)
MID_VMEM = ("k_small", "k_gain", "k_gates")
LIMIT = 62 * 2**20


def space(in_vmem):
    return pl.BlockSpec(memory_space=pltpu.VMEM if in_vmem else pl.ANY)


def on_device(nseq, nm, *args):
    (
        block_input,
        segment_ids,
        gain_mix,
        w_rec,
        w_gel,
        conv_weight,
        conv_bias,
        gate_a,
        gate_x,
        bias_a,
        bias_x,
        log_rate,
        w_out,
        gain_ffn,
        w_gate,
        w_up,
        w_down,
        cotangent,
    ) = args
    B, G, D = block_input.shape
    T, L, F = B * G, w_rec.shape[1], w_gate.shape[1]
    nz = Z_CHIPS
    d = types.SimpleNamespace(
        B=B, G=G, T=T, D=D, L=L, F=F, LP=-(-L // 128) * 128, FB=F // 3, HW=gate_a.shape[0],
        DC=D // nseq, nseq=nseq, nm=nm, nz=nz, nx=nseq // nz, ny=nm // CORES, CB=256,
        nb=D // CORES // 256, taps=conv_weight.shape[0], GR=gate_a.shape[0] // nseq,
    )
    d.W = max(d.FB, d.LP)
    outs, scratch, sems = layout(d)
    feed = dict(
        x_in=block_input.reshape(T, D), w_rec=w_rec, w_gel=w_gel, w_out=w_out, gate_a=gate_a,
        gate_x=gate_x, w_gate=w_gate, w_up=w_up, w_down=w_down, cot=cotangent.reshape(T, D),
        ids=segment_ids, gain_mix=gain_mix, gain_ffn=gain_ffn, conv_weight=conv_weight,
        conv_bias=conv_bias, bias_a=bias_a, bias_x=bias_x, log_rate=log_rate,
    )
    names_in = IN_ANY + IN_VMEM
    names = names_in + tuple(outs) + tuple(scratch) + tuple(sems)

    def kernel(*refs):
        body(d, types.SimpleNamespace(**dict(zip(names, refs))))

    mid = pl.pallas_call(
        kernel,
        out_shape=[jax.ShapeDtypeStruct(*v) for v in outs.values()],
        in_specs=[space(n in IN_VMEM) for n in names_in],
        out_specs=[space(n in MID_VMEM) for n in outs],
        scratch_shapes=[pltpu.VMEM(*v) for v in scratch.values()]
        + [pltpu.SemaphoreType.DMA(v) for v in sems.values()],
        compiler_params=pltpu.CompilerParams(
            collective_id=0, has_side_effects=True, vmem_limit_bytes=LIMIT
        ),
        name="block",
    )(*[feed[n] for n in names_in])
    mid = dict(zip(outs, mid))
    for n in ("hz_d", "hz_r"):
        mid.pop(n)
    DC, FB, LP, GR, part = d.DC, d.FB, d.LP, d.GR, L // nseq
    last = dict(
        o_block=(T, D), o_gin=(T, D), o_gm=(DC,), o_wrec=(DC, L), o_wgel=(DC, L),
        o_cw=(d.taps, part), o_cb=(part,), o_ga=(GR, L), o_gx=(GR, L), o_ba=(part,), o_bx=(part,),
        o_lr=(part,), o_wout=(L, DC), o_gf=(DC,), o_wgate=(DC, F), o_wup=(DC, F), o_wdown=(F, DC),
    )
    large = ("o_block", "o_gin", "o_wrec", "o_wgel", "o_wout", "o_wgate", "o_wup", "o_wdown")
    buffers = dict(
        a_f=((6, DC, FB), BF16), b_f=((6, DC, FB), BF16), c_f=((6, DC, FB), BF16),
        a_o=((DC, LP), BF16), b_o=((DC, LP), BF16), c_o=((DC, LP), BF16),
        a_d=((3, DC, FB), BF16), b_d=((3, d.nx - 1, DC, FB), BF16),
        a_r=((2, DC, LP), BF16), b_r=((2, d.nx - 1, DC, LP), BF16),
        w_block=((T, D), F32), w_gin=((T, D), F32),
        v_f=((6, DC, FB), F32), v_o=((L, DC), F32), v_d=((3, FB, DC), F32), v_r=((2, DC, L), F32),
    )
    names_last = tuple(mid) + tuple(last) + tuple(buffers) + ("sem",)

    def last_kernel(*refs):
        finish(d, types.SimpleNamespace(**dict(zip(names_last, refs))))

    results = pl.pallas_call(
        last_kernel,
        out_shape=[jax.ShapeDtypeStruct(v, F32) for v in last.values()],
        in_specs=[space(n in MID_VMEM) for n in mid],
        out_specs=[space(n not in large) for n in last],
        scratch_shapes=[pltpu.VMEM(*v) for v in buffers.values()] + [pltpu.SemaphoreType.DMA((64,))],
        compiler_params=pltpu.CompilerParams(vmem_limit_bytes=LIMIT),
        name="finish",
    )(*mid.values())
    results = list(results)
    results[0] = results[0].reshape(B, G, D)
    results[1] = results[1].reshape(B, G, D)
    return tuple(results)


def solution(mesh):
    nseq, nm = mesh.shape["seq"], mesh.shape["mp"]
    rows, cols, both = P(None, "seq", None), P(None, "mp"), P(("mp", "seq"))
    part = P("seq", "mp")
    in_specs = (
        rows, P(), P(), cols, cols, cols, P("mp"), cols, cols, P("mp"), P("mp"), P("mp"),
        P("mp", None), P(), cols, cols, P("mp", None), rows,
    )
    out_specs = (
        rows, rows, P("seq"), part, part, P(None, ("mp", "seq")), both, part, part, both, both,
        both, P("mp", "seq"), P("seq"), part, part, P("mp", "seq"),
    )

    def step(*args):
        return on_device(nseq, nm, *args)

    return jax.shard_map(step, mesh=mesh, in_specs=in_specs, out_specs=out_specs, check_vma=False)
```
